32 devices in a mesh: dp: 4 (over y, x), cent: 8 (over z, core).
Axes of the slice: x: 2, y: 2, z: 4, core: 2. Of those that a mesh axis runs over, the one named last changes fastest.
Arguments:
- embeddings: bfloat16 [8192, 1024], P('dp')
- centroids: bfloat16 [4096, 1024], P('cent')
- col_start: float32 [4096], P('cent'), may hold values from -6 to 6
Outputs:
- new_centroids: bfloat16 [4096, 1024], P('cent')
- row_potential: float32 [8192], P('dp')
- col_potential: float32 [4096], P('cent')
The draws below stay inside these ranges and needn't reach their ends.
All inputs are finite; a program needn't handle non-finite values.
Results may differ from the reference program's by a relative error of at most 0.0048.
Values may be sent and summed in bfloat16 or wider, within the bound.
No kernel may reach another device: no remote copies, remote signals or barrier semaphores. Data moves between devices by JAX's collectives and lax.ppermute only.
A program may use at most 64 MiB of HBM per device.

```python
import math
import jax
import jax.numpy as jnp
from jax import lax

D = 1024
ROWS_DEV = 2048
ITERS = 3
N = 8192
K = 4096
N_DP = 4


def centre_base(key):
    return jax.random.normal(key, (K, D), jnp.float32)


def draw_centroids(key, part):
    base = centre_base(key)
    return base.astype(jnp.bfloat16)


def draw_embeddings(key, part):
    base = centre_base(key)
    key = jax.random.fold_in(key, 5)
    key_main, key_first, key_second, key_scale, key_noise, key_apart = jax.random.split(key, 6)
    index = jnp.arange(N)
    first = jax.random.randint(key_first, (N,), 0, K)
    second = (first + 1 + jax.random.randint(key_second, (N,), 0, K - 1)) % K
    kind = index // 64 % 3
    chosen = index % 64 == 0
    strength = jnp.exp(jax.random.uniform(key_scale, (N,), jnp.float32, jnp.log(200.0), jnp.log(600.0)))
    noise = jax.random.normal(key_noise, (N, D), jnp.float32)
    apart = jax.random.normal(key_apart, (N, D), jnp.float32)
    between = 0.5 * (base[first] + base[second]) + 0.3 * noise
    single = base[first] + 0.3 * noise
    shape_rows = jnp.where((kind == 0)[:, None], between, jnp.where((kind == 1)[:, None], single, apart))
    aligned = (strength / jnp.sqrt(1.0 * D))[:, None] * shape_rows
    drawn = jax.random.normal(key_main, (N, D), jnp.float32)
    values = jnp.where(chosen[:, None], aligned, drawn)
    return values.astype(jnp.bfloat16)


def levels(key, extent, cuts, least, top_value):
    def one(axis_at, parts):
        heights = jax.random.uniform(jax.random.fold_in(jax.random.fold_in(key, 6), axis_at), (parts,), jnp.float32, least / len(cuts), top_value / len(cuts))
        return jnp.repeat(jnp.exp(heights), extent[axis_at] // parts).reshape((-1,) + (1,) * (len(extent) - axis_at - 1))

    gain = one(*cuts[0])
    for cut in cuts[1:]:
        gain = gain * one(*cut)
    return gain


def normal_values(stream_key, extent, deviation, bound, pieces=(), dtype=jnp.bfloat16):
    array = jax.random.normal(stream_key, extent, jnp.float32) * deviation
    if len(pieces) > 0:
        array = levels(stream_key, extent, pieces, -0.22, 0.18) * array
    return jnp.clip(array, min=-bound, max=bound).astype(dtype)


def setup_inputs(seed: int = 0) -> dict:
    key_of = jax.random.split(jax.random.key(seed), 4)
    embeddings = draw_embeddings(jax.random.fold_in(key_of[3], 71), 0)
    centroids = draw_centroids(jax.random.fold_in(key_of[3], 71), 0)
    col_start = normal_values(key_of[2], (K,), 1.5, 6.0, ((0, 8),), jnp.float32)
    return {"embeddings": embeddings, "centroids": centroids, "col_start": col_start}


def tile(block, centroids):
    product = lax.dot_general(block, centroids, (((1,), (1,)), ((), ())), preferred_element_type=jnp.float32)
    return product * (1.0 / math.sqrt(D))

def sweep(blocks, centroids, col_now, n_total, k_total):

    def step(carry, block):
        col_peak, col_mass = carry
        scores = tile(block, centroids)
        shifted = scores + col_now[None, :]
        peak = lax.optimization_barrier(jnp.max(shifted, axis=1))
        mass = lax.optimization_barrier(jnp.sum(jnp.exp(shifted - peak[:, None]), axis=1))
        row_new = -jnp.log(n_total) - (peak + jnp.log(mass))
        lifted = scores + row_new[:, None]
        block_peak = lax.optimization_barrier(jnp.max(lifted, axis=0))
        block_mass = lax.optimization_barrier(jnp.sum(jnp.exp(lifted - block_peak[None, :]), axis=0))
        joined = jnp.maximum(col_peak, block_peak)
        total = col_mass * jnp.exp(col_peak - joined) + block_mass * jnp.exp(block_peak - joined)
        return ((joined, total), row_new)
    start = (jnp.full((centroids.shape[0],), -jnp.inf, jnp.float32), jnp.zeros((centroids.shape[0],), jnp.float32))
    (col_peak, col_mass), rows = lax.scan(step, start, blocks)
    col_new = -jnp.log(k_total) - (col_peak + jnp.log(col_mass))
    return (rows, col_new)

def reference(embeddings, centroids, col_start):
    n_total = float(embeddings.shape[0])
    k_total = float(centroids.shape[0])
    blocks = embeddings.reshape(N_DP, ROWS_DEV, D)
    col_now = col_start
    rows = None
    for step_index in range(ITERS):
        rows, col_now = sweep(blocks, centroids, col_now, n_total, k_total)

    def gather_step(acc, pair):
        block, row_block = pair
        scores = tile(block, centroids)
        plan = jnp.exp(scores + row_block[:, None] + col_now[None, :]).astype(jnp.bfloat16)
        acc = acc + lax.dot_general(plan, block, (((0,), (0,)), ((), ())), preferred_element_type=jnp.float32)
        return (acc, 0)
    acc, unused = lax.scan(gather_step, jnp.zeros((centroids.shape[0], D), jnp.float32), (blocks, rows))
    new_centroids = (acc * k_total).astype(jnp.bfloat16)
    return (new_centroids, rows.reshape(-1), col_now)
```

```python
import math

import jax
import jax.numpy as jnp
from jax import lax
from jax.sharding import PartitionSpec as P

ITERS = 3
LOG2E = math.log2(math.e)
LN2 = math.log(2.0)


def flipped(x, axis, mask):
    size = lax.axis_size(axis)
    return lax.ppermute(x, axis, [(k, k ^ mask) for k in range(size)])


def lse2_tree(pieces):
    top = pieces[0]
    for piece in pieces[1:]:
        top = jnp.maximum(top, piece)
    terms = [jnp.exp2(piece - top) for piece in pieces]
    while len(terms) > 1:
        terms = [terms[k] + terms[k + 1] for k in range(0, len(terms), 2)]
    return top + jnp.log2(terms[0])


def lse2_over(x, axis):
    return lse2_tree([x] + [flipped(x, axis, mask) for mask in range(1, lax.axis_size(axis))])


def summed(part, axis, bits, scale):
    bit = bits[0]
    if len(bits) == 1:
        mine = part.astype(jnp.bfloat16)
        other = flipped(mine, axis, 1 << bit)
        return ((mine.astype(jnp.float32) + other.astype(jnp.float32)) * scale).astype(jnp.bfloat16)
    upper = (lax.axis_index(axis) >> bit) & 1 == 1
    half = part.shape[0] // 2
    low, high = part[:half], part[half:]
    sent = jnp.where(upper, low, high).astype(jnp.bfloat16)
    kept = jnp.where(upper, high, low)
    kept = kept + flipped(sent, axis, 1 << bit).astype(jnp.float32)
    done = summed(kept, axis, bits[1:], scale)
    other = flipped(done, axis, 1 << bit)
    return jnp.concatenate([jnp.where(upper, other, done), jnp.where(upper, done, other)], axis=0)


def on_device(embeddings, centroids, col_start):
    rows_here = embeddings.shape[0]
    cent_here = centroids.shape[0]
    n_dp = lax.axis_size("dp")
    n_total = rows_here * n_dp
    k_total = cent_here * lax.axis_size("cent")
    factor = LOG2E / math.sqrt(embeddings.shape[1])
    scores = lax.dot_general(
        centroids, embeddings, (((1,), (1,)), ((), ())), preferred_element_type=jnp.float32
    ) * factor
    col_now = col_start * LOG2E
    row_now = None
    for step_index in range(ITERS):
        shifted = scores + col_now[:, None]
        top = jnp.max(shifted, axis=0)
        part = top + jnp.log2(jnp.sum(jnp.exp2(shifted - top[None, :]), axis=0))
        row_now = -math.log2(n_total) - lse2_over(part, "cent")
        lifted = scores + row_now[None, :]
        top = jnp.max(lifted, axis=1)
        part = top + jnp.log2(jnp.sum(jnp.exp2(lifted - top[:, None]), axis=1))
        col_now = -math.log2(k_total) - lse2_over(part, "dp")
    plan = jnp.exp2(scores + row_now[None, :] + col_now[:, None]).astype(jnp.bfloat16)
    partial_sums = lax.dot_general(
        plan, embeddings, (((1,), (0,)), ((), ())), preferred_element_type=jnp.float32
    )
    bits = list(range(n_dp.bit_length() - 1))
    half = cent_here // 2
    new_centroids = jnp.concatenate(
        [
            summed(partial_sums[:half], "dp", bits, float(k_total)),
            summed(partial_sums[half:], "dp", bits[::-1], float(k_total)),
        ],
        axis=0,
    )
    return (new_centroids, row_now * LN2, col_now * LN2)


def solution(mesh):
    placed = (P("dp", None), P("cent", None), P("cent"))
    return jax.shard_map(
        on_device,
        mesh=mesh,
        in_specs=placed,
        out_specs=(P("cent", None), P("dp"), P("cent")),
        check_vma=False,
    )
```

```python
import math

import jax
import jax.numpy as jnp
from jax import lax
from jax.sharding import PartitionSpec as P

ITERS = 3
LOG2E = math.log2(math.e)
LN2 = math.log(2.0)


def flipped(x, axis, mask):
    size = lax.axis_size(axis)
    return lax.ppermute(x, axis, [(k, k ^ mask) for k in range(size)])


def lse2_over(x, axis):
    size = lax.axis_size(axis)
    copies = jnp.broadcast_to(x[None, :], (size,) + x.shape)
    pieces = lax.all_to_all(copies, axis, 0, 0)
    top = jnp.max(pieces, axis=0)
    return top + jnp.log2(jnp.sum(jnp.exp2(pieces - top[None, :]), axis=0))


def summed(part, axis, bits, scale):
    bit = bits[0]
    if len(bits) == 1:
        mine = part.astype(jnp.bfloat16)
        other = flipped(mine, axis, 1 << bit)
        return ((mine.astype(jnp.float32) + other.astype(jnp.float32)) * scale).astype(jnp.bfloat16)
    upper = (lax.axis_index(axis) >> bit) & 1 == 1
    half = part.shape[0] // 2
    low, high = part[:half], part[half:]
    sent = jnp.where(upper, low, high).astype(jnp.bfloat16)
    kept = jnp.where(upper, high, low)
    kept = kept + flipped(sent, axis, 1 << bit).astype(jnp.float32)
    done = summed(kept, axis, bits[1:], scale)
    other = flipped(done, axis, 1 << bit)
    return jnp.concatenate([jnp.where(upper, other, done), jnp.where(upper, done, other)], axis=0)


def on_device(embeddings, centroids, col_start):
    rows_here = embeddings.shape[0]
    cent_here = centroids.shape[0]
    n_dp = lax.axis_size("dp")
    n_total = rows_here * n_dp
    k_total = cent_here * lax.axis_size("cent")
    factor = LOG2E / math.sqrt(embeddings.shape[1])
    scores = lax.dot_general(
        centroids, embeddings, (((1,), (1,)), ((), ())), preferred_element_type=jnp.float32
    ) * factor
    col_now = col_start * LOG2E
    row_now = None
    for step_index in range(ITERS):
        shifted = scores + col_now[:, None]
        top = jnp.max(shifted, axis=0)
        part = top + jnp.log2(jnp.sum(jnp.exp2(shifted - top[None, :]), axis=0))
        row_now = -math.log2(n_total) - lse2_over(part, "cent")
        lifted = scores + row_now[None, :]
        top = jnp.max(lifted, axis=1)
        part = top + jnp.log2(jnp.sum(jnp.exp2(lifted - top[:, None]), axis=1))
        col_now = -math.log2(k_total) - lse2_over(part, "dp")
    plan = jnp.exp2(scores + row_now[None, :] + col_now[:, None]).astype(jnp.bfloat16)
    partial_sums = lax.dot_general(
        plan, embeddings, (((1,), (0,)), ((), ())), preferred_element_type=jnp.float32
    )
    bits = list(range(n_dp.bit_length() - 1))
    half = cent_here // 2
    new_centroids = jnp.concatenate(
        [
            summed(partial_sums[:half], "dp", bits, float(k_total)),
            summed(partial_sums[half:], "dp", bits[::-1], float(k_total)),
        ],
        axis=0,
    )
    return (new_centroids, row_now * LN2, col_now * LN2)


def solution(mesh):
    placed = (P("dp", None), P("cent", None), P("cent"))
    return jax.shard_map(
        on_device,
        mesh=mesh,
        in_specs=placed,
        out_specs=(P("cent", None), P("dp"), P("cent")),
        check_vma=False,
    )
```

```python
import math

import jax
import jax.numpy as jnp
from jax import lax
from jax.sharding import PartitionSpec as P

ITERS = 3
LOG2E = math.log2(math.e)
LN2 = math.log(2.0)


def bits_of(axis):
    size = lax.axis_size(axis)
    assert size & (size - 1) == 0
    return list(range(size.bit_length() - 1))


def flipped(x, axis, bit):
    size = lax.axis_size(axis)
    return lax.ppermute(x, axis, [(k, k ^ (1 << bit)) for k in range(size)])


def lse2_over(x, axis):
    for bit in bits_of(axis):
        other = flipped(x, axis, bit)
        top = jnp.maximum(x, other)
        x = top + jnp.log2(jnp.exp2(x - top) + jnp.exp2(other - top))
    return x


def summed(sent, kept, axis, bits, scale):
    bit = bits[0]
    upper = (lax.axis_index(axis) >> bit) & 1 == 1
    got = flipped(sent.astype(jnp.bfloat16), axis, bit)
    mine = kept + got.astype(jnp.float32)
    if len(bits) == 2:
        mine = mine.astype(jnp.bfloat16)
        other = flipped(mine, axis, bits[1])
        done = ((mine.astype(jnp.float32) + other.astype(jnp.float32)) * scale).astype(jnp.bfloat16)
    else:
        half = mine.shape[0] // 2
        low, high = mine[:half], mine[half:]
        next_upper = (lax.axis_index(axis) >> bits[1]) & 1 == 1
        done = summed(
            jnp.where(next_upper, low, high), jnp.where(next_upper, high, low), axis, bits[1:], scale
        )
    other = flipped(done, axis, bit)
    return jnp.concatenate([jnp.where(upper, other, done), jnp.where(upper, done, other)], axis=0)


def on_device(embeddings, centroids, col_start):
    rows_here = embeddings.shape[0]
    cent_here = centroids.shape[0]
    n_total = rows_here * lax.axis_size("dp")
    k_total = cent_here * lax.axis_size("cent")
    factor = LOG2E / math.sqrt(embeddings.shape[1])
    scores = lax.dot_general(
        centroids, embeddings, (((1,), (1,)), ((), ())), preferred_element_type=jnp.float32
    ) * factor
    col_now = col_start * LOG2E
    row_now = None
    for step_index in range(ITERS):
        shifted = scores + col_now[:, None]
        top = jnp.max(shifted, axis=0)
        part = top + jnp.log2(jnp.sum(jnp.exp2(shifted - top[None, :]), axis=0))
        row_now = -math.log2(n_total) - lse2_over(part, "cent")
        lifted = scores + row_now[None, :]
        top = jnp.max(lifted, axis=1)
        part = top + jnp.log2(jnp.sum(jnp.exp2(lifted - top[:, None]), axis=1))
        col_now = -math.log2(k_total) - lse2_over(part, "dp")
    plan = jnp.exp2(scores + row_now[None, :] + col_now[:, None]).astype(jnp.bfloat16)
    plan = lax.optimization_barrier(plan)

    def weighted(plan_rows):
        return lax.dot_general(
            plan_rows, embeddings, (((1,), (0,)), ((), ())), preferred_element_type=jnp.float32
        )

    bits = bits_of("dp")
    quarter = cent_here // 4
    whole = []
    for part_index, order in enumerate((bits, bits[::-1])):
        upper = (lax.axis_index("dp") >> order[0]) & 1
        first = 2 * part_index * quarter
        sent = lax.dynamic_slice_in_dim(plan, first + (1 - upper) * quarter, quarter, 0)
        kept = lax.dynamic_slice_in_dim(plan, first + upper * quarter, quarter, 0)
        whole.append(summed(weighted(sent), weighted(kept), "dp", order, float(k_total)))
    new_centroids = jnp.concatenate(whole, axis=0)
    return (new_centroids, row_now * LN2, col_now * LN2)


def solution(mesh):
    placed = (P("dp", None), P("cent", None), P("cent"))
    return jax.shard_map(
        on_device,
        mesh=mesh,
        in_specs=placed,
        out_specs=(P("cent", None), P("dp"), P("cent")),
        check_vma=False,
    )
```

```python
import math

import jax
import jax.numpy as jnp
from jax import lax
from jax.sharding import PartitionSpec as P

ITERS = 3
CHUNKS = 2
LOG2E = math.log2(math.e)
LN2 = math.log(2.0)


def bits_of(axis):
    size = lax.axis_size(axis)
    assert size & (size - 1) == 0
    return list(range(size.bit_length() - 1))


def flipped(x, axis, mask):
    size = lax.axis_size(axis)
    return lax.ppermute(x, axis, [(k, k ^ mask) for k in range(size)])


def lse2_tree(pieces):
    top = pieces[0]
    for piece in pieces[1:]:
        top = jnp.maximum(top, piece)
    terms = [jnp.exp2(piece - top) for piece in pieces]
    while len(terms) > 1:
        terms = [terms[k] + terms[k + 1] for k in range(0, len(terms), 2)]
    return top + jnp.log2(terms[0])


def lse2_over(x, axis, first_group):
    bits = bits_of(axis)
    groups = [bits[:first_group]] + [bits[k:k + 2] for k in range(first_group, len(bits), 2)]
    for group in groups:
        masks = [0]
        for bit in group:
            masks = masks + [mask | 1 << bit for mask in masks]
        pieces = {0: x}
        for mask in sorted(masks[1:], key=lambda mask: -mask.bit_count()):
            pieces[mask] = flipped(x, axis, mask)
        x = lse2_tree([pieces[mask] for mask in masks])
    return x


def summed(sent, kept, axis, bits, scale):
    bit = bits[0]
    upper = (lax.axis_index(axis) >> bit) & 1 == 1
    got = flipped(sent.astype(jnp.bfloat16), axis, 1 << bit)
    mine = kept + got.astype(jnp.float32)
    if len(bits) == 2:
        mine = mine.astype(jnp.bfloat16)
        other = flipped(mine, axis, 1 << bits[1])
        done = ((mine.astype(jnp.float32) + other.astype(jnp.float32)) * scale).astype(jnp.bfloat16)
    else:
        half = mine.shape[0] // 2
        low, high = mine[:half], mine[half:]
        next_upper = (lax.axis_index(axis) >> bits[1]) & 1 == 1
        done = summed(
            jnp.where(next_upper, low, high), jnp.where(next_upper, high, low), axis, bits[1:], scale
        )
    other = flipped(done, axis, 1 << bit)
    return jnp.concatenate([jnp.where(upper, other, done), jnp.where(upper, done, other)], axis=0)


def on_device(embeddings, centroids, col_start):
    rows_here, depth = embeddings.shape
    cent_here = centroids.shape[0]
    n_total = rows_here * lax.axis_size("dp")
    k_total = cent_here * lax.axis_size("cent")
    factor = LOG2E / math.sqrt(depth)
    scores = lax.dot_general(
        centroids, embeddings, (((1,), (1,)), ((), ())), preferred_element_type=jnp.float32
    ) * factor
    col_now = col_start * LOG2E
    row_now = None
    for step_index in range(ITERS):
        shifted = scores + col_now[:, None]
        top = jnp.max(shifted, axis=0)
        part = top + jnp.log2(jnp.sum(jnp.exp2(shifted - top[None, :]), axis=0))
        row_now = -math.log2(n_total) - lse2_over(part, "cent", 1)
        lifted = scores + row_now[None, :]
        top = jnp.max(lifted, axis=1)
        part = top + jnp.log2(jnp.sum(jnp.exp2(lifted - top[:, None]), axis=1))
        col_now = -math.log2(k_total) - lse2_over(part, "dp", 2)
    row_now, col_now = lax.optimization_barrier((row_now, col_now))
    plan = jnp.exp2(scores + row_now[None, :] + col_now[:, None]).astype(jnp.bfloat16)
    plan = lax.optimization_barrier(plan)

    bits = bits_of("dp")
    quarter = cent_here // 4
    width = depth // CHUNKS
    orders = (bits, bits[::-1])

    def weighted(part_index, is_sent, chunk):
        upper = (lax.axis_index("dp") >> orders[part_index][0]) & 1
        at = 2 * part_index * quarter + (1 - upper if is_sent else upper) * quarter
        plan_rows = lax.dynamic_slice_in_dim(plan, at, quarter, 0)
        columns = embeddings[:, chunk * width:(chunk + 1) * width]
        return lax.optimization_barrier(lax.dot_general(
            plan_rows, columns, (((1,), (0,)), ((), ())), preferred_element_type=jnp.float32
        ))

    places = [(chunk, part_index) for chunk in range(CHUNKS) for part_index in range(2)]
    sent = {place: weighted(place[1], True, place[0]) for place in places}
    kept = {place: weighted(place[1], False, place[0]) for place in places}
    whole = {
        place: summed(sent[place], kept[place], "dp", orders[place[1]], float(k_total)) for place in places
    }
    new_centroids = jnp.concatenate(
        [
            jnp.concatenate([whole[chunk, part_index] for chunk in range(CHUNKS)], axis=1)
            for part_index in range(2)
        ],
        axis=0,
    )
    return (new_centroids, row_now * LN2, col_now * LN2)


def solution(mesh):
    placed = (P("dp", None), P("cent", None), P("cent"))
    return jax.shard_map(
        on_device,
        mesh=mesh,
        in_specs=placed,
        out_specs=(P("cent", None), P("dp"), P("cent")),
        check_vma=False,
    )
```

```python
import math

import jax
import jax.numpy as jnp
from jax import lax
from jax.sharding import PartitionSpec as P

ITERS = 3
CHUNKS = 2
LOG2E = math.log2(math.e)
LN2 = math.log(2.0)


def bits_of(axis):
    size = lax.axis_size(axis)
    assert size & (size - 1) == 0
    return list(range(size.bit_length() - 1))


def flipped(x, axis, mask):
    size = lax.axis_size(axis)
    return lax.ppermute(x, axis, [(k, k ^ mask) for k in range(size)])


def lse2_tree(pieces):
    top = pieces[0]
    for piece in pieces[1:]:
        top = jnp.maximum(top, piece)
    terms = [jnp.exp2(piece - top) for piece in pieces]
    while len(terms) > 1:
        terms = [terms[k] + terms[k + 1] for k in range(0, len(terms), 2)]
    return top + jnp.log2(terms[0])


def lse2_over(x, axis, first_group):
    bits = bits_of(axis)
    groups = [bits[:first_group]] + [bits[k:k + 2] for k in range(first_group, len(bits), 2)]
    for group in groups:
        masks = [0]
        for bit in group:
            masks = masks + [mask | 1 << bit for mask in masks]
        pieces = {0: x}
        for mask in sorted(masks[1:], key=lambda mask: -mask.bit_count()):
            pieces[mask] = flipped(x, axis, mask)
        x = lse2_tree([pieces[mask] for mask in masks])
    return x


def summed(sent, kept, axis, bits, scale):
    bit = bits[0]
    upper = (lax.axis_index(axis) >> bit) & 1 == 1
    got = flipped(sent.astype(jnp.bfloat16), axis, 1 << bit)
    mine = kept + got.astype(jnp.float32)
    if len(bits) == 2:
        mine = mine.astype(jnp.bfloat16)
        other = flipped(mine, axis, 1 << bits[1])
        done = ((mine.astype(jnp.float32) + other.astype(jnp.float32)) * scale).astype(jnp.bfloat16)
    else:
        half = mine.shape[0] // 2
        low, high = mine[:half], mine[half:]
        next_upper = (lax.axis_index(axis) >> bits[1]) & 1 == 1
        done = summed(
            jnp.where(next_upper, low, high), jnp.where(next_upper, high, low), axis, bits[1:], scale
        )
    other = flipped(done, axis, 1 << bit)
    return jnp.concatenate([jnp.where(upper, other, done), jnp.where(upper, done, other)], axis=0)


def on_device(embeddings, centroids, col_start):
    rows_here, depth = embeddings.shape
    cent_here = centroids.shape[0]
    n_total = rows_here * lax.axis_size("dp")
    k_total = cent_here * lax.axis_size("cent")
    factor = LOG2E / math.sqrt(depth)
    scores = lax.dot_general(
        centroids, embeddings, (((1,), (1,)), ((), ())), preferred_element_type=jnp.float32
    ) * factor
    col_now = col_start * LOG2E
    row_now = None
    for step_index in range(ITERS):
        shifted = scores + col_now[:, None]
        top = jnp.max(shifted, axis=0)
        part = top + jnp.log2(jnp.sum(jnp.exp2(shifted - top[None, :]), axis=0))
        row_now = -math.log2(n_total) - lse2_over(part, "cent", 1)
        lifted = scores + row_now[None, :]
        top = jnp.max(lifted, axis=1)
        part = top + jnp.log2(jnp.sum(jnp.exp2(lifted - top[:, None]), axis=1))
        col_now = -math.log2(k_total) - lse2_over(part, "dp", 2)
    row_now, col_now = lax.optimization_barrier((row_now, col_now))
    bits = bits_of("dp")
    quarter = cent_here // 4
    width = depth // CHUNKS
    orders = (bits, bits[::-1])

    def plan_of(part_index, is_sent):
        upper = (lax.axis_index("dp") >> orders[part_index][0]) & 1
        at = 2 * part_index * quarter + (1 - upper if is_sent else upper) * quarter
        rows = lax.dynamic_slice_in_dim(scores, at, quarter, 0)
        columns = lax.dynamic_slice_in_dim(col_now, at, quarter, 0)
        return lax.optimization_barrier(
            jnp.exp2(rows + row_now[None, :] + columns[:, None]).astype(jnp.bfloat16)
        )

    plans = {(part_index, is_sent): plan_of(part_index, is_sent) for is_sent in (True, False) for part_index in range(2)}

    def weighted(part_index, is_sent, chunk):
        columns = embeddings[:, chunk * width:(chunk + 1) * width]
        return lax.dot_general(
            plans[part_index, is_sent], columns, (((1,), (0,)), ((), ())), preferred_element_type=jnp.float32
        )

    places = [(chunk, part_index) for chunk in range(CHUNKS) for part_index in range(2)]
    sent = {place: weighted(place[1], True, place[0]) for place in places}
    kept = {place: weighted(place[1], False, place[0]) for place in places}
    whole = {
        place: summed(sent[place], kept[place], "dp", orders[place[1]], float(k_total)) for place in places
    }
    new_centroids = jnp.concatenate(
        [
            jnp.concatenate([whole[chunk, part_index] for chunk in range(CHUNKS)], axis=1)
            for part_index in range(2)
        ],
        axis=0,
    )
    return (new_centroids, row_now * LN2, col_now * LN2)


def solution(mesh):
    placed = (P("dp", None), P("cent", None), P("cent"))
    return jax.shard_map(
        on_device,
        mesh=mesh,
        in_specs=placed,
        out_specs=(P("cent", None), P("dp"), P("cent")),
        check_vma=False,
    )
```

```python
import math

import jax
import jax.numpy as jnp
from jax import lax
from jax.sharding import PartitionSpec as P

ITERS = 3
CHUNKS = 2
LOG2E = math.log2(math.e)
LN2 = math.log(2.0)


def bits_of(axis):
    size = lax.axis_size(axis)
    assert size & (size - 1) == 0
    return list(range(size.bit_length() - 1))


def flipped(x, axis, mask):
    size = lax.axis_size(axis)
    return lax.ppermute(x, axis, [(k, k ^ mask) for k in range(size)])


def lse2_tree(pieces):
    top = pieces[0]
    for piece in pieces[1:]:
        top = jnp.maximum(top, piece)
    terms = [jnp.exp2(piece - top) for piece in pieces]
    while len(terms) > 1:
        terms = [terms[k] + terms[k + 1] for k in range(0, len(terms), 2)]
    return top + jnp.log2(terms[0])


def lse2_over(x, axis, first_group):
    bits = bits_of(axis)
    first = None
    groups = [bits[:first_group]] + [bits[k:k + 2] for k in range(first_group, len(bits), 2)]
    for group in groups:
        masks = [0]
        for bit in group:
            masks = masks + [mask | 1 << bit for mask in masks]
        pieces = {0: x}
        for mask in sorted(masks[1:], key=lambda mask: -mask.bit_count()):
            pieces[mask] = flipped(x, axis, mask)
        first = first or pieces
        x = lse2_tree([pieces[mask] for mask in masks])
    return x, first


def last_sum(plan, mass, part, embeddings):
    n_dp, n_cent = lax.axis_size("dp"), lax.axis_size("cent")
    bits = bits_of("dp")
    orders = (bits, [bits[1], bits[0]] + bits[2:])
    odd = lax.axis_index("cent") & 1
    half = plan.shape[0] // 2
    width = embeddings.shape[1] // CHUNKS

    def paired(x, level):
        pairs = [
            (row * n_cent + col, (row ^ 1 << orders[col & 1][level]) * n_cent + col)
            for row in range(n_dp)
            for col in range(n_cent)
        ]
        return lax.ppermute(x, ("dp", "cent"), pairs)

    def upper(level):
        return lax.axis_index("dp") >> jnp.where(odd == 1, orders[1][level], orders[0][level]) & 1

    sent_at, kept_at = (1 - upper(0)) * half, upper(0) * half

    def rows_of(x, at):
        return lax.dynamic_slice_in_dim(x, at, half, 0)

    def mean(at, chunk):
        sums = lax.dot_general(
            rows_of(plan, at),
            embeddings[:, chunk * width:(chunk + 1) * width],
            (((1,), (0,)), ((), ())),
            preferred_element_type=jnp.float32,
        )
        return sums * (1.0 / rows_of(mass, at))[:, None]

    def gathered(mine, level):
        if level == len(bits) - 1:
            mine = mine.astype(jnp.bfloat16)
            other = paired(mine, level)
            return (mine.astype(jnp.float32) + other.astype(jnp.float32)).astype(jnp.bfloat16)
        up = upper(level) == 1
        low, high = jnp.split(mine, 2, axis=0)
        got = paired(jnp.where(up, low, high).astype(jnp.bfloat16), level)
        done = gathered(jnp.where(up, high, low) + got.astype(jnp.float32), level + 1)
        return spread(done, level)

    def spread(done, level):
        other = paired(done, level)
        up = upper(level) == 1
        return jnp.concatenate([jnp.where(up, other, done), jnp.where(up, done, other)], axis=0)

    got = [paired(mean(sent_at, chunk).astype(jnp.bfloat16), 0) for chunk in range(CHUNKS)]
    whole, partners = lse2_over(part, "dp", 2)
    partner = jnp.where(odd == 1, partners[1 << orders[1][0]], partners[1 << orders[0][0]])
    weight_own = rows_of(jnp.exp2(part - whole), kept_at)[:, None]
    weight_partner = rows_of(jnp.exp2(partner - whole), kept_at)[:, None]
    columns = []
    for chunk in range(CHUNKS):
        mine = mean(kept_at, chunk) * weight_own + got[chunk].astype(jnp.float32) * weight_partner
        columns.append(spread(gathered(mine, 1), 0))
    return whole, jnp.concatenate(columns, axis=1)


def on_device(embeddings, centroids, col_start):
    rows_here, depth = embeddings.shape
    cent_here = centroids.shape[0]
    n_total = rows_here * lax.axis_size("dp")
    k_total = cent_here * lax.axis_size("cent")
    factor = LOG2E / math.sqrt(depth)
    scores = lax.dot_general(
        centroids, embeddings, (((1,), (1,)), ((), ())), preferred_element_type=jnp.float32
    ) * factor
    col_now = col_start * LOG2E
    for step_index in range(ITERS):
        shifted = scores + col_now[:, None]
        top = jnp.max(shifted, axis=0)
        part = top + jnp.log2(jnp.sum(jnp.exp2(shifted - top[None, :]), axis=0))
        row_now = -math.log2(n_total) - lse2_over(part, "cent", 1)[0]
        lifted = scores + row_now[None, :]
        top = jnp.max(lifted, axis=1)
        terms = jnp.exp2(lifted - top[:, None])
        mass = jnp.sum(terms, axis=1)
        part = top + jnp.log2(mass)
        if step_index < ITERS - 1:
            col_now = -math.log2(k_total) - lse2_over(part, "dp", 2)[0]
    whole, new_centroids = last_sum(terms.astype(jnp.bfloat16), mass, part, embeddings)
    col_now = -math.log2(k_total) - whole
    return (new_centroids, lax.optimization_barrier(row_now) * LN2, lax.optimization_barrier(col_now) * LN2)


def solution(mesh):
    placed = (P("dp", None), P("cent", None), P("cent"))
    return jax.shard_map(
        on_device,
        mesh=mesh,
        in_specs=placed,
        out_specs=(P("cent", None), P("dp"), P("cent")),
        check_vma=False,
    )
```

```python
import math

import jax
import jax.numpy as jnp
from jax import lax
from jax.experimental import pallas as pl
from jax.experimental.pallas import tpu as pltpu
from jax.sharding import PartitionSpec as P

ITERS = 3
BLOCK = 16
LANES = 128
VMEM_BYTES = 24 * 2**20
LOG2E = math.log2(math.e)
LN2 = math.log(2.0)


def bits_of(axis):
    size = lax.axis_size(axis)
    assert size & (size - 1) == 0
    return list(range(size.bit_length() - 1))


def flipped(x, axis, mask):
    size = lax.axis_size(axis)
    return lax.ppermute(x, axis, [(k, k ^ mask) for k in range(size)])


def lse2_tree(pieces):
    top = pieces[0]
    for piece in pieces[1:]:
        top = jnp.maximum(top, piece)
    terms = [jnp.exp2(piece - top) for piece in pieces]
    while len(terms) > 1:
        terms = [terms[k] + terms[k + 1] for k in range(0, len(terms), 2)]
    return top + jnp.log2(terms[0])


def lse2_over(x, axis, first_group):
    bits = bits_of(axis)
    first = None
    groups = [bits[:first_group]] + [bits[k:k + 2] for k in range(first_group, len(bits), 2)]
    for group in groups:
        masks = [0]
        for bit in group:
            masks = masks + [mask | 1 << bit for mask in masks]
        pieces = {0: x}
        for mask in sorted(masks[1:], key=lambda mask: -mask.bit_count()):
            pieces[mask] = flipped(x, axis, mask)
        first = first or pieces
        x = lse2_tree([pieces[mask] for mask in masks])
    return x, first


def last_pass_kernel(starts, row, scores, embeddings, sent, kept, part, mass, plan, top_at, mass_at):
    count, rows_here = scores.shape
    quarter = count // 4
    per_quarter = quarter // BLOCK

    def place(index):
        return pl.multiple_of(starts[index // per_quarter] + index % per_quarter * BLOCK, BLOCK)

    def find_top(index, carry):
        at = pl.ds(pl.multiple_of(index * BLOCK, BLOCK), BLOCK)
        top_at[at, :] = jnp.max(scores[at, :] + row[...], axis=1, keepdims=True)
        return carry

    lax.fori_loop(0, count // BLOCK, find_top, 0, unroll=4)

    def take_terms(target, first):
        def body(index, carry):
            at = pl.ds(place(first + index), BLOCK)
            terms = jnp.exp2(scores[at, :] + row[...] - top_at[at, :])
            mass_at[at, :] = jnp.sum(terms, axis=1, keepdims=True)
            target[pl.ds(pl.multiple_of(index * BLOCK, BLOCK), BLOCK), :] = terms.astype(jnp.bfloat16)
            return carry

        lax.fori_loop(0, 2 * per_quarter, body, 0, unroll=4)

    take_terms(plan, 0)
    take_terms(kept, 2 * per_quarter)
    sums = jnp.dot(plan[...], embeddings[...], preferred_element_type=jnp.float32)
    for k in range(2):
        at = pl.ds(pl.multiple_of(starts[k], BLOCK), quarter)
        sent[k] = (sums[k * quarter:(k + 1) * quarter] * (1.0 / mass_at[at, :])).astype(jnp.bfloat16)
    lane = lax.broadcasted_iota(jnp.int32, (LANES, LANES), 1)
    diagonal = lane == lax.broadcasted_iota(jnp.int32, (LANES, LANES), 0)
    for k in range(count // LANES):
        at = pl.ds(k * LANES, LANES)
        total = mass_at[at, :]
        logs = top_at[at, :] + jnp.log2(total)
        part[pl.ds(k, 1), :] = jnp.sum(jnp.where(diagonal, logs, 0.0), axis=0, keepdims=True)
        mass[pl.ds(k, 1), :] = jnp.sum(jnp.where(diagonal, total, 0.0), axis=0, keepdims=True)


def last_pass(starts, row, scores, embeddings):
    count, rows_here = scores.shape
    depth = embeddings.shape[1]
    f32, bf16 = jnp.float32, jnp.bfloat16
    vmem = pl.BlockSpec(memory_space=pltpu.VMEM)
    sent, kept, part, mass = pl.pallas_call(
        last_pass_kernel,
        out_shape=(
            jax.ShapeDtypeStruct((2, count // 4, depth), bf16),
            jax.ShapeDtypeStruct((count // 2, rows_here), bf16),
            jax.ShapeDtypeStruct((count // LANES, LANES), f32),
            jax.ShapeDtypeStruct((count // LANES, LANES), f32),
        ),
        in_specs=[pl.BlockSpec(memory_space=pltpu.SMEM), vmem, vmem, vmem],
        out_specs=(vmem, vmem, vmem, vmem),
        scratch_shapes=[
            pltpu.VMEM((count // 2, rows_here), bf16),
            pltpu.VMEM((count, 1), f32),
            pltpu.VMEM((count, 1), f32),
        ],
        compiler_params=pltpu.CompilerParams(vmem_limit_bytes=VMEM_BYTES),
        cost_estimate=pl.CostEstimate(
            flops=count * rows_here * depth, bytes_accessed=4 * count * rows_here, transcendentals=count * rows_here
        ),
    )(starts, row[None, :], scores, embeddings)
    return sent, kept, part.reshape(count), mass.reshape(count)


def kept_kernel(plan, embeddings, out):
    out[...] = jnp.dot(plan[...], embeddings[...], preferred_element_type=jnp.float32)


def kept_sums(plan, embeddings):
    count, rows_here = plan.shape
    depth = embeddings.shape[1]
    vmem = pl.BlockSpec(memory_space=pltpu.VMEM)
    return pl.pallas_call(
        kept_kernel,
        out_shape=jax.ShapeDtypeStruct((count, depth), jnp.float32),
        in_specs=[vmem, vmem],
        out_specs=vmem,
        compiler_params=pltpu.CompilerParams(vmem_limit_bytes=VMEM_BYTES),
        cost_estimate=pl.CostEstimate(
            flops=2 * count * rows_here * depth, bytes_accessed=2 * rows_here * depth, transcendentals=0
        ),
    )(plan, embeddings)


def last_sum(scores, row_now, embeddings):
    bits = bits_of("dp")
    orders = (bits, [bits[1], bits[0]] + bits[2:])
    quarter = scores.shape[0] // 4

    def upper(bit):
        return lax.axis_index("dp") >> bit & 1

    sent_at = [(2 * k + 1 - upper(order[0])) * quarter for k, order in enumerate(orders)]
    kept_at = [(2 * k + upper(order[0])) * quarter for k, order in enumerate(orders)]
    starts = jnp.stack(sent_at + kept_at).astype(jnp.int32)
    sent, kept, part, mass = last_pass(starts, row_now, scores, embeddings)

    def gathered(mine, order):
        if len(order) == 1:
            mine = mine.astype(jnp.bfloat16)
            other = flipped(mine, "dp", 1 << order[0])
            return (mine.astype(jnp.float32) + other.astype(jnp.float32)).astype(jnp.bfloat16)
        up = upper(order[0]) == 1
        low, high = jnp.split(mine, 2, axis=0)
        got = flipped(jnp.where(up, low, high).astype(jnp.bfloat16), "dp", 1 << order[0])
        return spread(gathered(jnp.where(up, high, low) + got.astype(jnp.float32), order[1:]), order[0])

    def spread(done, bit):
        other = flipped(done, "dp", 1 << bit)
        up = upper(bit) == 1
        return jnp.concatenate([jnp.where(up, other, done), jnp.where(up, done, other)], axis=0)

    got = [flipped(sent[k], "dp", 1 << order[0]) for k, order in enumerate(orders)]
    whole, partners = lse2_over(part, "dp", 2)
    sums = kept_sums(kept, embeddings)
    weight_own = jnp.exp2(part - whole) / mass
    halves = []
    for k, order in enumerate(orders):
        weight_other = jnp.exp2(partners[1 << order[0]] - whole)
        own, other = (lax.dynamic_slice_in_dim(x, kept_at[k], quarter, 0)[:, None] for x in (weight_own, weight_other))
        mine = sums[k * quarter:(k + 1) * quarter] * own + got[k].astype(jnp.float32) * other
        halves.append(spread(gathered(mine, order[1:]), order[0]))
    return whole, jnp.concatenate(halves, axis=0)


def on_device(embeddings, centroids, col_start):
    rows_here, depth = embeddings.shape
    cent_here = centroids.shape[0]
    n_total = rows_here * lax.axis_size("dp")
    k_total = cent_here * lax.axis_size("cent")
    factor = LOG2E / math.sqrt(depth)
    scores = lax.dot_general(
        centroids, embeddings, (((1,), (1,)), ((), ())), preferred_element_type=jnp.float32
    ) * factor
    col_now = col_start * LOG2E
    for step_index in range(ITERS):
        shifted = scores + col_now[:, None]
        top = jnp.max(shifted, axis=0)
        part = top + jnp.log2(jnp.sum(jnp.exp2(shifted - top[None, :]), axis=0))
        row_now = -math.log2(n_total) - lse2_over(part, "cent", 1)[0]
        if step_index < ITERS - 1:
            lifted = scores + row_now[None, :]
            top = jnp.max(lifted, axis=1)
            part = top + jnp.log2(jnp.sum(jnp.exp2(lifted - top[:, None]), axis=1))
            col_now = -math.log2(k_total) - lse2_over(part, "dp", 2)[0]
    whole, new_centroids = last_sum(scores, row_now, embeddings)
    col_now = -math.log2(k_total) - whole
    return (new_centroids, lax.optimization_barrier(row_now) * LN2, lax.optimization_barrier(col_now) * LN2)


def solution(mesh):
    placed = (P("dp", None), P("cent", None), P("cent"))
    return jax.shard_map(
        on_device,
        mesh=mesh,
        in_specs=placed,
        out_specs=(P("cent", None), P("dp"), P("cent")),
        check_vma=False,
    )
```

```python
import math

import jax
import jax.numpy as jnp
from jax import lax
from jax.experimental import pallas as pl
from jax.experimental.pallas import tpu as pltpu
from jax.sharding import PartitionSpec as P

ITERS = 3
CHUNKS = 2
BLOCK = 16
LANES = 128
VMEM_BYTES = 24 * 2**20
LOG2E = math.log2(math.e)
LN2 = math.log(2.0)


def bits_of(axis):
    size = lax.axis_size(axis)
    assert size & (size - 1) == 0
    return list(range(size.bit_length() - 1))


def flipped(x, axis, mask):
    size = lax.axis_size(axis)
    return lax.ppermute(x, axis, [(k, k ^ mask) for k in range(size)])


def lse2_tree(pieces):
    top = pieces[0]
    for piece in pieces[1:]:
        top = jnp.maximum(top, piece)
    terms = [jnp.exp2(piece - top) for piece in pieces]
    while len(terms) > 1:
        terms = [terms[k] + terms[k + 1] for k in range(0, len(terms), 2)]
    return top + jnp.log2(terms[0])


def lse2_over(x, axis, first_group):
    bits = bits_of(axis)
    first = None
    groups = [bits[:first_group]] + [bits[k:k + 2] for k in range(first_group, len(bits), 2)]
    for group in groups:
        masks = [0]
        for bit in group:
            masks = masks + [mask | 1 << bit for mask in masks]
        pieces = {0: x}
        for mask in sorted(masks[1:], key=lambda mask: -mask.bit_count()):
            pieces[mask] = flipped(x, axis, mask)
        first = first or pieces
        x = lse2_tree([pieces[mask] for mask in masks])
    return x, first


def column(values):
    return jnp.sum(jnp.where(diagonal(), values, 0.0), axis=1, keepdims=True)


def line(values):
    return jnp.sum(jnp.where(diagonal(), values, 0.0), axis=0, keepdims=True)


def diagonal():
    lane = lax.broadcasted_iota(jnp.int32, (LANES, LANES), 1)
    return lane == lax.broadcasted_iota(jnp.int32, (LANES, LANES), 0)


def last_pass_kernel(row, scores, plan, part, mass, wide, top_at):
    count, rows_here = scores.shape
    tiles = [pl.ds(k * LANES, LANES) for k in range(rows_here // LANES)]

    def find_top(index, carry):
        at = pl.ds(pl.multiple_of(index * BLOCK, BLOCK), BLOCK)
        top = scores[at, tiles[0]] + row[:, tiles[0]]
        for tile in tiles[1:]:
            top = jnp.maximum(top, scores[at, tile] + row[:, tile])
        wide[at, :] = top
        return carry

    lax.fori_loop(0, count // BLOCK, find_top, 0, unroll=2)
    top = jnp.max(wide[...], axis=1, keepdims=True)
    top_at[...] = top
    wide[...] = jnp.broadcast_to(top, wide.shape)

    def take_terms(index, carry):
        at = pl.ds(pl.multiple_of(index * BLOCK, BLOCK), BLOCK)
        top = wide[at, :]
        total = jnp.zeros_like(top)
        for tile in tiles:
            terms = jnp.exp2(scores[at, tile] + row[:, tile] - top)
            total = total + terms
            plan[at, tile] = terms.astype(jnp.bfloat16)
        wide[at, :] = total
        return carry

    lax.fori_loop(0, count // BLOCK, take_terms, 0, unroll=2)
    total = jnp.sum(wide[...], axis=1, keepdims=True)
    mass[...] = total
    top_at[...] = top_at[...] + jnp.log2(total)
    for k in range(count // LANES):
        part[pl.ds(k, 1), :] = line(top_at[pl.ds(k * LANES, LANES), :])


def last_pass(row, scores):
    count, rows_here = scores.shape
    f32 = jnp.float32
    vmem = pl.BlockSpec(memory_space=pltpu.VMEM)
    plan, part, mass = pl.pallas_call(
        last_pass_kernel,
        out_shape=(
            jax.ShapeDtypeStruct((count, rows_here), jnp.bfloat16),
            jax.ShapeDtypeStruct((count // LANES, LANES), f32),
            jax.ShapeDtypeStruct((count, 1), f32),
        ),
        in_specs=[vmem, vmem],
        out_specs=(vmem, vmem, vmem),
        scratch_shapes=[pltpu.VMEM((count, LANES), f32), pltpu.VMEM((count, 1), f32)],
        compiler_params=pltpu.CompilerParams(vmem_limit_bytes=VMEM_BYTES),
        cost_estimate=pl.CostEstimate(
            flops=8 * count * rows_here, bytes_accessed=6 * count * rows_here, transcendentals=count * rows_here
        ),
    )(row[None, :], scores)
    return plan, part.reshape(count), mass


def means_kernel(starts, plan, embeddings, mass, *rest):
    weights, out, both = rest if len(rest) == 3 else (None, *rest)
    quarter = both.shape[0] // 2
    places = [pl.ds(pl.multiple_of(starts[k], LANES), quarter) for k in range(2)]
    for k, at in enumerate(places):
        both[pl.ds(k * quarter, quarter), :] = plan[at, :]
    sums = jnp.dot(both[...], embeddings[...], preferred_element_type=jnp.float32)
    for k, at in enumerate(places):
        factor = 1.0 / mass[at, :]
        if weights is not None:
            blocks = [
                column(weights[pl.ds(starts[k] // LANES + block, 1), :]) for block in range(quarter // LANES)
            ]
            factor = factor * jnp.concatenate(blocks, axis=0)
        out[k] = (sums[k * quarter:(k + 1) * quarter] * factor).astype(out.dtype)


def means_of(starts, plan, embeddings, mass, weights, dtype):
    count, rows_here = plan.shape
    depth = embeddings.shape[1]
    vmem = pl.BlockSpec(memory_space=pltpu.VMEM)
    operands = [starts, plan, embeddings, mass]
    if weights is not None:
        operands.append(weights.reshape(count // LANES, LANES))
    return pl.pallas_call(
        means_kernel,
        out_shape=jax.ShapeDtypeStruct((2, count // 4, depth), dtype),
        in_specs=[pl.BlockSpec(memory_space=pltpu.SMEM)] + [vmem] * (len(operands) - 1),
        out_specs=vmem,
        scratch_shapes=[pltpu.VMEM((count // 2, rows_here), jnp.bfloat16)],
        compiler_params=pltpu.CompilerParams(vmem_limit_bytes=VMEM_BYTES),
        cost_estimate=pl.CostEstimate(
            flops=count * rows_here * depth, bytes_accessed=2 * rows_here * depth, transcendentals=0
        ),
    )(*operands)


def last_sum(scores, row_now, embeddings, ups, sent_at, kept_at, orders):
    plan, part, mass = last_pass(row_now, scores)
    first, second = orders[0][:2]
    partners = {bit: flipped(part, "dp", 1 << bit) for bit in (first, second)}
    sent = means_of(sent_at, plan, embeddings, mass, None, jnp.bfloat16)
    got = [flipped(sent[k], "dp", 1 << order[0]) for k, order in enumerate(orders)]
    whole = lse2_tree([part, partners[first]])
    for bit in orders[0][1:]:
        whole = lse2_tree([whole, flipped(whole, "dp", 1 << bit)])
    kept = means_of(kept_at, plan, embeddings, mass, jnp.exp2(part - whole), jnp.float32)

    def chosen(bit, yes, no):
        return jnp.where(ups[bit:bit + 1].reshape((1,) * yes.ndim) == 1, yes, no)

    def gathered(mine, order):
        if len(order) == 1:
            mine = mine.astype(jnp.bfloat16)
            other = flipped(mine, "dp", 1 << order[0])
            return (mine.astype(jnp.float32) + other.astype(jnp.float32)).astype(jnp.bfloat16)
        low, high = jnp.split(mine, 2, axis=0)
        got = flipped(chosen(order[0], low, high).astype(jnp.bfloat16), "dp", 1 << order[0])
        return spread(gathered(chosen(order[0], high, low) + got.astype(jnp.float32), order[1:]), order[0])

    def spread(done, bit):
        other = flipped(done, "dp", 1 << bit)
        return jnp.concatenate([chosen(bit, other, done), chosen(bit, done, other)], axis=0)

    quarter, depth = kept.shape[1:]
    width = depth // CHUNKS
    chunks = [[], []]
    for chunk in range(CHUNKS):
        columns = slice(chunk * width, (chunk + 1) * width)
        for k, order in enumerate(orders):
            weights = jnp.exp2(partners[order[0]] - whole)[2 * k * quarter:(2 * k + 2) * quarter]
            weights = chosen(order[0], weights[quarter:], weights[:quarter])[:, None]
            mine = kept[k, :, columns] + got[k][:, columns].astype(jnp.float32) * weights
            chunks[k].append(spread(gathered(mine, order[1:]), order[0]))
    return whole, jnp.concatenate([jnp.concatenate(half, axis=1) for half in chunks], axis=0)


def on_device(embeddings, centroids, col_start):
    rows_here, depth = embeddings.shape
    cent_here = centroids.shape[0]
    n_total = rows_here * lax.axis_size("dp")
    k_total = cent_here * lax.axis_size("cent")
    factor = LOG2E / math.sqrt(depth)

    bits = bits_of("dp")
    orders = (bits, [bits[1], bits[0]] + bits[2:])
    place = jnp.full((len(bits),), lax.axis_index("dp"), jnp.int32)
    ups = place >> jnp.arange(len(bits), dtype=jnp.int32) & 1
    quarter = cent_here // 4
    first_ups = jnp.concatenate([ups[order[0]:order[0] + 1] for order in orders])
    lower = jnp.arange(2, dtype=jnp.int32) * (2 * quarter)
    sent_at, kept_at = lower + (1 - first_ups) * quarter, lower + first_ups * quarter
    ups, sent_at, kept_at, embeddings, centroids = lax.optimization_barrier(
        (ups, sent_at, kept_at, embeddings, centroids)
    )

    scores = lax.dot_general(
        centroids, embeddings, (((1,), (1,)), ((), ())), preferred_element_type=jnp.float32
    ) * factor
    col_now = col_start * LOG2E
    for step_index in range(ITERS):
        shifted = scores + col_now[:, None]
        top = jnp.max(shifted, axis=0)
        part = top + jnp.log2(jnp.sum(jnp.exp2(shifted - top[None, :]), axis=0))
        row_now = -math.log2(n_total) - lse2_over(part, "cent", 1)[0]
        if step_index < ITERS - 1:
            lifted = scores + row_now[None, :]
            top = jnp.max(lifted, axis=1)
            part = top + jnp.log2(jnp.sum(jnp.exp2(lifted - top[:, None]), axis=1))
            col_now = -math.log2(k_total) - lse2_over(part, "dp", 2)[0]
    whole, new_centroids = last_sum(scores, row_now, embeddings, ups, sent_at, kept_at, orders)
    col_now = -math.log2(k_total) - whole
    return (new_centroids, lax.optimization_barrier(row_now) * LN2, lax.optimization_barrier(col_now) * LN2)


def solution(mesh):
    placed = (P("dp", None), P("cent", None), P("cent"))
    return jax.shard_map(
        on_device,
        mesh=mesh,
        in_specs=placed,
        out_specs=(P("cent", None), P("dp"), P("cent")),
        check_vma=False,
    )
```

```python
import math

import jax
import jax.numpy as jnp
from jax import lax
from jax.experimental import pallas as pl
from jax.experimental.pallas import tpu as pltpu
from jax.sharding import PartitionSpec as P

ITERS = 3
CHUNKS = 2
LANES = 128
VMEM_BYTES = 24 * 2**20
LOG2E = math.log2(math.e)
LN2 = math.log(2.0)


def bits_of(axis):
    size = lax.axis_size(axis)
    assert size & (size - 1) == 0
    return list(range(size.bit_length() - 1))


def flipped(x, axis, mask):
    size = lax.axis_size(axis)
    return lax.ppermute(x, axis, [(k, k ^ mask) for k in range(size)])


def lse2(first, second):
    top = jnp.maximum(first, second)
    return top + jnp.log2(jnp.exp2(first - top) + jnp.exp2(second - top))


def lse2_over(x, axis, first_group):
    bits = bits_of(axis)
    groups = [bits[:first_group]] + [bits[k:k + 2] for k in range(first_group, len(bits), 2)]
    for group in groups:
        masks = [1 << bit for bit in group]
        if len(masks) == 2:
            far = flipped(x, axis, masks[0] | masks[1])
            near = [flipped(x, axis, mask) for mask in reversed(masks)]
            x = lse2(lax.optimization_barrier(lse2(x, far)), lse2(*near))
        else:
            for mask in masks:
                x = lse2(x, flipped(x, axis, mask))
    return x


def column(values):
    return jnp.sum(jnp.where(diagonal(), values, 0.0), axis=1, keepdims=True)


def diagonal():
    lane = lax.broadcasted_iota(jnp.int32, (LANES, LANES), 1)
    return lane == lax.broadcasted_iota(jnp.int32, (LANES, LANES), 0)


def means_kernel(starts, plan, embeddings, factors, out, both):
    quarter = both.shape[0] // 2
    places = [pl.ds(pl.multiple_of(starts[k], LANES), quarter) for k in range(2)]
    for k, at in enumerate(places):
        both[pl.ds(k * quarter, quarter), :] = plan[at, :]
    sums = jnp.dot(both[...], embeddings[...], preferred_element_type=jnp.float32)
    for k in range(2):
        for block in range(quarter // LANES):
            rows = slice(k * quarter + block * LANES, k * quarter + (block + 1) * LANES)
            factor = column(factors[pl.ds(starts[k] // LANES + block, 1), :])
            out[k, pl.ds(block * LANES, LANES), :] = (sums[rows] * factor).astype(out.dtype)


def means_of(starts, plan, embeddings, factors, dtype):
    count, rows_here = plan.shape
    depth = embeddings.shape[1]
    vmem = pl.BlockSpec(memory_space=pltpu.VMEM)
    return pl.pallas_call(
        means_kernel,
        out_shape=jax.ShapeDtypeStruct((2, count // 4, depth), dtype),
        in_specs=[pl.BlockSpec(memory_space=pltpu.SMEM), vmem, vmem, vmem],
        out_specs=vmem,
        scratch_shapes=[pltpu.VMEM((count // 2, rows_here), jnp.bfloat16)],
        compiler_params=pltpu.CompilerParams(vmem_limit_bytes=VMEM_BYTES),
        cost_estimate=pl.CostEstimate(
            flops=count * rows_here * depth, bytes_accessed=2 * rows_here * depth, transcendentals=0
        ),
    )(starts, plan, embeddings, factors.reshape(count // LANES, LANES))


def last_sum(plan, part, mass, embeddings, ups, sent_at, kept_at, orders):
    half = part.shape[0] // 2
    first, second = orders[0][:2]
    partners = {bit: flipped(part, "dp", 1 << bit) for bit in (first, second)}
    sent = means_of(sent_at, plan, embeddings, 1.0 / mass, jnp.bfloat16)
    got = [flipped(sent[k], "dp", 1 << order[0]) for k, order in enumerate(orders)]
    pairs = {bit: lse2(partners[bit], part) for bit in (first, second)}
    whole = pairs[first]
    for bit in orders[0][1:]:
        whole = lse2(flipped(whole, "dp", 1 << bit), whole)

    def halves(by_bit):
        return jnp.concatenate([by_bit[first][:half], by_bit[second][half:]])

    pair = halves(pairs)
    kept = means_of(kept_at, plan, embeddings, jnp.exp2(part - pair) / mass, jnp.float32)
    weights = jnp.exp2(halves(partners) - pair)
    weights_pair = jnp.exp2(pair - whole)

    def chosen(bit, yes, no):
        return jnp.where(ups[bit].reshape((1,) * yes.ndim), yes, no)

    def gathered(mine, order):
        if len(order) == 1:
            mine = mine.astype(jnp.bfloat16)
            other = flipped(mine, "dp", 1 << order[0])
            return (mine.astype(jnp.float32) + other.astype(jnp.float32)).astype(jnp.bfloat16)
        low, high = jnp.split(mine, 2, axis=0)
        got = flipped(chosen(order[0], low, high).astype(jnp.bfloat16), "dp", 1 << order[0])
        return spread(gathered(chosen(order[0], high, low) + got.astype(jnp.float32), order[1:]), order[0])

    def spread(done, bit):
        other = flipped(done, "dp", 1 << bit)
        return jnp.concatenate([chosen(bit, other, done), chosen(bit, done, other)], axis=0)

    quarter, depth = kept.shape[1:]
    width = depth // CHUNKS
    chunks = [[], []]
    dones = []
    for chunk in range(CHUNKS):
        columns = slice(chunk * width, (chunk + 1) * width)
        for k, order in enumerate(orders):
            low, high = slice(2 * k * quarter, (2 * k + 1) * quarter), slice((2 * k + 1) * quarter, (2 * k + 2) * quarter)
            other = chosen(order[0], weights[high], weights[low])[:, None]
            after = chosen(order[0], weights_pair[high], weights_pair[low])[:, None]
            mine = (kept[k, :, columns] + got[k][:, columns].astype(jnp.float32) * other) * after
            dones.append(gathered(mine, order[1:]))
            chunks[k].append(spread(dones[-1], order[0]))
    whole = lax.optimization_barrier((whole, dones[0]))[0]
    return whole, jnp.concatenate([jnp.concatenate(half, axis=1) for half in chunks], axis=0)


def on_device(embeddings, centroids, col_start):
    rows_here, depth = embeddings.shape
    cent_here = centroids.shape[0]
    n_total = rows_here * lax.axis_size("dp")
    k_total = cent_here * lax.axis_size("cent")
    factor = LOG2E / math.sqrt(depth)

    bits = bits_of("dp")
    orders = (bits, [bits[1], bits[0]] + bits[2:])
    quarter = cent_here // 4
    place = jnp.full((1,), lax.axis_index("dp"), jnp.int32)
    ups = [place >> bit & 1 for bit in bits]
    first_ups = jnp.concatenate([ups[order[0]] for order in orders])
    lower = jnp.arange(2, dtype=jnp.int32) * (2 * quarter)
    sent_at, kept_at = lower + (1 - first_ups) * quarter, lower + first_ups * quarter
    ups = [up == 1 for up in ups]
    ups, sent_at, kept_at, embeddings, centroids = lax.optimization_barrier(
        (ups, sent_at, kept_at, embeddings, centroids)
    )

    scores = lax.dot_general(
        centroids, embeddings, (((1,), (1,)), ((), ())), preferred_element_type=jnp.float32
    ) * factor
    col_now = col_start * LOG2E
    for step_index in range(ITERS):
        shifted = scores + col_now[:, None]
        top = jnp.max(shifted, axis=0)
        part = top + jnp.log2(jnp.sum(jnp.exp2(shifted - top[None, :]), axis=0))
        row_now = -math.log2(n_total) - lse2_over(part, "cent", 1)
        lifted = scores + row_now[None, :]
        top = jnp.max(lifted, axis=1)
        terms = jnp.exp2(lifted - top[:, None])
        mass = jnp.sum(terms, axis=1)
        part = top + jnp.log2(mass)
        if step_index < ITERS - 1:
            col_now = -math.log2(k_total) - lse2_over(part, "dp", 2)
    whole, new_centroids = last_sum(terms.astype(jnp.bfloat16), part, mass, embeddings, ups, sent_at, kept_at, orders)
    col_now = -math.log2(k_total) - whole
    return (new_centroids, lax.optimization_barrier(row_now) * LN2, col_now * LN2)


def solution(mesh):
    placed = (P("dp", None), P("cent", None), P("cent"))
    return jax.shard_map(
        on_device,
        mesh=mesh,
        in_specs=placed,
        out_specs=(P("cent", None), P("dp"), P("cent")),
        check_vma=False,
    )
```

```python
import functools
import math

import jax
import jax.numpy as jnp
from jax import lax
from jax.experimental import pallas as pl
from jax.experimental.pallas import tpu as pltpu
from jax.sharding import PartitionSpec as P

ITERS = 3
CHUNKS = 2
LANES = 128
VMEM_BYTES = 24 * 2**20
FIRST_VMEM_BYTES = 57 * 2**20
PIECES = 4


def bits_of(axis):
    size = lax.axis_size(axis)
    assert size & (size - 1) == 0
    return list(range(size.bit_length() - 1))


def flipped(x, axis, mask):
    size = lax.axis_size(axis)
    return lax.ppermute(x, axis, [(k, k ^ mask) for k in range(size)])


def lse(first, second):
    top = jnp.maximum(first, second)
    return top + jnp.log(jnp.exp(first - top) + jnp.exp(second - top))


def lse_over(x, axis, first_group, aligned=lambda value, mask: value):
    bits = bits_of(axis)
    groups = [bits[:first_group]] + [bits[k:k + 2] for k in range(first_group, len(bits), 2)]
    for group in groups:
        masks = [1 << bit for bit in group]
        if len(masks) == 2:
            far = masks[0] | masks[1]
            far = aligned(flipped(x, axis, far), far)
            near = [aligned(flipped(x, axis, mask), mask) for mask in reversed(masks)]
            x = lse(lax.optimization_barrier(lse(x, far)), lse(*near))
        else:
            for mask in masks:
                x = lse(x, aligned(flipped(x, axis, mask), mask))
    return x


def column(values):
    lane = lax.broadcasted_iota(jnp.int32, (LANES, LANES), 1)
    diagonal = lane == lax.broadcasted_iota(jnp.int32, (LANES, LANES), 0)
    return jnp.sum(jnp.where(diagonal, values, 0.0), axis=1, keepdims=True)


def first_kernel(factor, starts, centroids, embeddings, col, scores, part, near_centroids, near_embeddings, near_col, arrived):
    quarter = centroids.shape[0] // 4
    span = embeddings.shape[0] // PIECES
    copies = [(col, near_col)]
    for k in range(4):
        at = pl.ds(pl.multiple_of(starts[k], LANES), quarter)
        copies.append((centroids.at[at], near_centroids.at[pl.ds(k * quarter, quarter)]))
    for k in range(PIECES):
        at = pl.ds(k * span, span)
        copies.append((embeddings.at[at], near_embeddings.at[at]))
    copies = [pltpu.make_async_copy(source, target, arrived.at[k]) for k, (source, target) in enumerate(copies)]
    for copy in copies:
        copy.start()
    copies[0].wait()
    columns = [
        column(near_col[pl.ds(starts[k] // LANES + block, 1), :])
        for k in range(4)
        for block in range(quarter // LANES)
    ]
    col_here = jnp.concatenate(columns, axis=0)
    for copy in copies[1:5]:
        copy.wait()
    for k in range(PIECES):
        at = pl.ds(k * span, span)
        copies[5 + k].wait()
        block = lax.dot_general(
            near_centroids[...], near_embeddings[at, :], (((1,), (1,)), ((), ())), preferred_element_type=jnp.float32
        ) * factor
        scores[:, at] = block
        shifted = block + col_here
        top = jnp.max(shifted, axis=0, keepdims=True)
        part[:, at] = top + jnp.log(jnp.sum(jnp.exp(shifted - top), axis=0, keepdims=True))


def first_pass(starts, centroids, embeddings, col_start):
    count, depth = centroids.shape
    rows_here = embeddings.shape[0]
    vmem = pl.BlockSpec(memory_space=pltpu.VMEM)
    anywhere = pl.BlockSpec(memory_space=pl.ANY)
    scores, part = pl.pallas_call(
        functools.partial(first_kernel, 1.0 / math.sqrt(depth)),
        out_shape=(
            jax.ShapeDtypeStruct((count, rows_here), jnp.float32),
            jax.ShapeDtypeStruct((1, rows_here), jnp.float32),
        ),
        in_specs=[pl.BlockSpec(memory_space=pltpu.SMEM), anywhere, anywhere, anywhere],
        out_specs=(vmem, vmem),
        scratch_shapes=[
            pltpu.VMEM((count, depth), jnp.bfloat16),
            pltpu.VMEM((rows_here, depth), jnp.bfloat16),
            pltpu.VMEM((count // LANES, LANES), jnp.float32),
            pltpu.SemaphoreType.DMA((5 + PIECES,)),
        ],
        compiler_params=pltpu.CompilerParams(vmem_limit_bytes=FIRST_VMEM_BYTES),
        cost_estimate=pl.CostEstimate(
            flops=2 * count * rows_here * depth,
            bytes_accessed=2 * (count + rows_here) * depth,
            transcendentals=count * rows_here,
        ),
    )(starts, centroids, embeddings, col_start.reshape(count // LANES, LANES))
    return scores, part.reshape(rows_here)


def means_kernel(is_kept, plan, embeddings, mass, *rest):
    half = plan.shape[0] // 2
    quarter = half // 2
    sums = jnp.dot(plan[pl.ds(is_kept * half, half), :], embeddings[...], preferred_element_type=jnp.float32)
    if is_kept:
        weights, row, out, row_out = rest
        row_out[...] = row[...]
    else:
        out, = rest
    for block in range(half // LANES):
        factor = 1.0 / column(mass[pl.ds(is_kept * (half // LANES) + block, 1), :])
        if is_kept:
            factor = factor * column(weights[pl.ds(block, 1), :])
        place = pl.ds(block * LANES % quarter, LANES)
        values = sums[block * LANES:(block + 1) * LANES] * factor
        out[block * LANES // quarter, place, :] = values.astype(out.dtype)


def means_of(is_kept, plan, embeddings, mass, *rest):
    count, rows_here = plan.shape
    depth = embeddings.shape[1]
    vmem = pl.BlockSpec(memory_space=pltpu.VMEM)
    out = jax.ShapeDtypeStruct((2, count // 4, depth), jnp.float32 if is_kept else jnp.bfloat16)
    row_out = jax.ShapeDtypeStruct((1, rows_here), jnp.float32)
    return pl.pallas_call(
        functools.partial(means_kernel, is_kept),
        out_shape=(out, row_out) if is_kept else out,
        in_specs=[vmem] * (3 + len(rest)),
        out_specs=(vmem, pl.BlockSpec((1, rows_here), lambda: (0, 0))) if is_kept else vmem,
        compiler_params=pltpu.CompilerParams(vmem_limit_bytes=VMEM_BYTES),
        cost_estimate=pl.CostEstimate(
            flops=count * rows_here * depth, bytes_accessed=2 * rows_here * depth, transcendentals=0
        ),
    )(plan, embeddings, mass.reshape(count // LANES, LANES), *rest)


def last_sum(plan, part, mass, row_now, embeddings, ups, orders, aligned):
    quarter = part.shape[0] // 4
    first, second = orders[0][:2]
    partners = {bit: aligned(flipped(part, "dp", 1 << bit), 1 << bit) for bit in (first, second)}
    sent = means_of(0, plan, embeddings, mass)
    got = [flipped(sent[k], "dp", 1 << order[0]) for k, order in enumerate(orders)]
    pairs = {bit: lse(partners[bit], part) for bit in (first, second)}
    whole = pairs[first]
    for bit in orders[0][1:]:
        whole = lse(aligned(flipped(whole, "dp", 1 << bit), 1 << bit), whole)

    def kept_of(lower, upper):
        return jnp.concatenate([lower[2 * quarter:3 * quarter], upper[3 * quarter:]])

    pair = kept_of(pairs[first], pairs[second])
    weights = jnp.exp(kept_of(part, part) - pair).reshape(2 * quarter // LANES, LANES)
    kept, row_out = means_of(1, plan, embeddings, mass, weights, row_now[None, :])
    weights = jnp.exp(kept_of(partners[first], partners[second]) - pair)
    weights_pair = jnp.exp(pair - kept_of(whole, whole))

    def chosen(bit, yes, no):
        return jnp.where(ups[bit].reshape((1,) * yes.ndim), yes, no)

    def gathered(mine, order):
        if len(order) == 1:
            mine = mine.astype(jnp.bfloat16)
            other = flipped(mine, "dp", 1 << order[0])
            return (mine.astype(jnp.float32) + other.astype(jnp.float32)).astype(jnp.bfloat16)
        low, high = jnp.split(mine, 2, axis=0)
        got = flipped(chosen(order[0], low, high).astype(jnp.bfloat16), "dp", 1 << order[0])
        return spread(gathered(chosen(order[0], high, low) + got.astype(jnp.float32), order[1:]), order[0])

    def spread(done, bit):
        return whole_of(done, flipped(done, "dp", 1 << bit), bit)

    def whole_of(kept, sent, bit):
        return jnp.concatenate([chosen(bit, sent, kept), chosen(bit, kept, sent)], axis=0)

    width = kept.shape[2] // CHUNKS
    chunks = [[], []]
    dones = []
    for chunk in range(CHUNKS):
        columns = slice(chunk * width, (chunk + 1) * width)
        for k, order in enumerate(orders):
            rows = slice(k * quarter, (k + 1) * quarter)
            mine = kept[k, :, columns] + got[k][:, columns].astype(jnp.float32) * weights[rows, None]
            dones.append(gathered(mine * weights_pair[rows, None], order[1:]))
            chunks[k].append(spread(dones[-1], order[0]))
    whole = lax.optimization_barrier((whole, dones[0]))[0]
    quarters = jnp.split(whole, 4)
    whole = jnp.concatenate([whole_of(quarters[2 + k], quarters[k], order[0]) for k, order in enumerate(orders)])
    return whole, jnp.concatenate([jnp.concatenate(half, axis=1) for half in chunks], axis=0), row_out


def on_device(embeddings, centroids, col_start):
    rows_here = embeddings.shape[0]
    cent_here = centroids.shape[0]
    n_total = rows_here * lax.axis_size("dp")
    k_total = cent_here * lax.axis_size("cent")

    bits = bits_of("dp")
    orders = (bits, [bits[1], bits[0]] + bits[2:])
    quarter = cent_here // 4
    place = jnp.full((1,), lax.axis_index("dp"), jnp.int32)
    ups = [place >> bit & 1 for bit in bits]
    first_ups = jnp.concatenate([ups[order[0]] for order in orders])
    lower = jnp.arange(2, dtype=jnp.int32) * (2 * quarter)
    starts = jnp.concatenate([lower + (1 - first_ups) * quarter, lower + first_ups * quarter])
    ups = [up == 1 for up in ups]
    ups, starts, embeddings, centroids = lax.optimization_barrier((ups, starts, embeddings, centroids))

    def aligned(value, mask):
        quarters = jnp.split(value, 4)
        for k, order in enumerate(orders):
            if mask >> order[0] & 1:
                quarters[k], quarters[2 + k] = quarters[2 + k], quarters[k]
        return jnp.concatenate(quarters)

    scores, part = first_pass(starts, centroids, embeddings, col_start)
    for step_index in range(ITERS):
        if step_index > 0:
            shifted = scores + col_now[:, None]
            top = jnp.max(shifted, axis=0)
            part = top + jnp.log(jnp.sum(jnp.exp(shifted - top[None, :]), axis=0))
        row_now = -math.log(n_total) - lse_over(part, "cent", 1)
        lifted = scores + row_now[None, :]
        top = jnp.max(lifted, axis=1)
        terms = jnp.exp(lifted - top[:, None])
        mass = jnp.sum(terms, axis=1)
        part = top + jnp.log(mass)
        if step_index < ITERS - 1:
            col_now = -math.log(k_total) - lse_over(part, "dp", 2, aligned)
    whole, new_centroids, row_out = last_sum(
        terms.astype(jnp.bfloat16), part, mass, row_now, embeddings, ups, orders, aligned
    )
    return (new_centroids, row_out.reshape(rows_here), -math.log(k_total) - whole)


def solution(mesh):
    placed = (P("dp", None), P("cent", None), P("cent"))
    return jax.shard_map(
        on_device,
        mesh=mesh,
        in_specs=placed,
        out_specs=(P("cent", None), P("dp"), P("cent")),
        check_vma=False,
    )
```

```python
import functools
import math

import jax
import jax.numpy as jnp
from jax import lax
from jax.experimental import pallas as pl
from jax.experimental.pallas import tpu as pltpu
from jax.sharding import PartitionSpec as P

ITERS = 3
CHUNKS = 2
LANES = 128
VMEM_BYTES = 24 * 2**20


def bits_of(axis):
    size = lax.axis_size(axis)
    assert size & (size - 1) == 0
    return list(range(size.bit_length() - 1))


def flipped(x, axis, mask):
    size = lax.axis_size(axis)
    return lax.ppermute(x, axis, [(k, k ^ mask) for k in range(size)])


def lse(first, second):
    top = jnp.maximum(first, second)
    return top + jnp.log(jnp.exp(first - top) + jnp.exp(second - top))


def lse_over(x, axis, first_group, aligned=lambda value, mask: value):
    bits = bits_of(axis)
    groups = [bits[:first_group]] + [bits[k:k + 2] for k in range(first_group, len(bits), 2)]
    for group in groups:
        masks = [1 << bit for bit in group]
        if len(masks) == 2:
            far = masks[0] | masks[1]
            far = aligned(flipped(x, axis, far), far)
            near = [aligned(flipped(x, axis, mask), mask) for mask in reversed(masks)]
            x = lse(lax.optimization_barrier(lse(x, far)), lse(*near))
        else:
            for mask in masks:
                x = lse(x, aligned(flipped(x, axis, mask), mask))
    return x


def column(values):
    lane = lax.broadcasted_iota(jnp.int32, (LANES, LANES), 1)
    diagonal = lane == lax.broadcasted_iota(jnp.int32, (LANES, LANES), 0)
    return jnp.sum(jnp.where(diagonal, values, 0.0), axis=1, keepdims=True)


def means_kernel(is_kept, plan, embeddings, mass, *rest):
    half = plan.shape[0] // 2
    quarter = half // 2
    sums = jnp.dot(plan[pl.ds(is_kept * half, half), :], embeddings[...], preferred_element_type=jnp.float32)
    if is_kept:
        weights, row, out, row_out = rest
        row_out[...] = row[...]
    else:
        out, = rest
    for block in range(half // LANES):
        factor = 1.0 / column(mass[pl.ds(is_kept * (half // LANES) + block, 1), :])
        if is_kept:
            factor = factor * column(weights[pl.ds(block, 1), :])
        place = pl.ds(block * LANES % quarter, LANES)
        values = sums[block * LANES:(block + 1) * LANES] * factor
        out[block * LANES // quarter, place, :] = values.astype(out.dtype)


def means_of(is_kept, plan, embeddings, mass, *rest):
    count, rows_here = plan.shape
    depth = embeddings.shape[1]
    vmem = pl.BlockSpec(memory_space=pltpu.VMEM)
    out = jax.ShapeDtypeStruct((2, count // 4, depth), jnp.float32 if is_kept else jnp.bfloat16)
    row_out = jax.ShapeDtypeStruct((1, rows_here), jnp.float32)
    return pl.pallas_call(
        functools.partial(means_kernel, is_kept),
        out_shape=(out, row_out) if is_kept else out,
        in_specs=[vmem] * (3 + len(rest)),
        out_specs=(vmem, pl.BlockSpec((1, rows_here), lambda: (0, 0))) if is_kept else vmem,
        compiler_params=pltpu.CompilerParams(vmem_limit_bytes=VMEM_BYTES),
        cost_estimate=pl.CostEstimate(
            flops=count * rows_here * depth, bytes_accessed=2 * rows_here * depth, transcendentals=0
        ),
    )(plan, embeddings, mass.reshape(count // LANES, LANES), *rest)


def last_sum(plan, part, mass, row_now, embeddings, chosen, orders, aligned):
    quarter = part.shape[0] // 4
    first, second = orders[0][:2]
    partners = {bit: aligned(flipped(part, "dp", 1 << bit), 1 << bit) for bit in (first, second)}
    sent = means_of(0, plan, embeddings, mass)
    got = [flipped(sent[k], "dp", 1 << order[0]) for k, order in enumerate(orders)]
    pairs = {bit: lse(partners[bit], part) for bit in (first, second)}
    whole = pairs[first]
    for bit in orders[0][1:]:
        whole = lse(aligned(flipped(whole, "dp", 1 << bit), 1 << bit), whole)

    def kept_of(lower, upper):
        return jnp.concatenate([lower[2 * quarter:3 * quarter], upper[3 * quarter:]])

    pair = kept_of(pairs[first], pairs[second])
    weights = jnp.exp(kept_of(part, part) - pair).reshape(2 * quarter // LANES, LANES)
    kept, row_out = means_of(1, plan, embeddings, mass, weights, row_now[None, :])
    weights = jnp.exp(kept_of(partners[first], partners[second]) - pair)
    weights_pair = jnp.exp(pair - kept_of(whole, whole))

    def gathered(mine, order):
        if len(order) == 1:
            mine = mine.astype(jnp.bfloat16)
            other = flipped(mine, "dp", 1 << order[0])
            return (mine.astype(jnp.float32) + other.astype(jnp.float32)).astype(jnp.bfloat16)
        low, high = jnp.split(mine, 2, axis=0)
        got = flipped(chosen(order[0], low, high).astype(jnp.bfloat16), "dp", 1 << order[0])
        return spread(gathered(chosen(order[0], high, low) + got.astype(jnp.float32), order[1:]), order[0])

    def spread(done, bit):
        return whole_of(done, flipped(done, "dp", 1 << bit), bit)

    def whole_of(kept, sent, bit):
        return jnp.concatenate([chosen(bit, sent, kept), chosen(bit, kept, sent)], axis=0)

    width = kept.shape[2] // CHUNKS
    chunks = []
    dones = []
    for chunk in range(CHUNKS):
        halves = []
        columns = slice(chunk * width, (chunk + 1) * width)
        for k, order in enumerate(orders):
            rows = slice(k * quarter, (k + 1) * quarter)
            mine = kept[k, :, columns] + got[k][:, columns].astype(jnp.float32) * weights[rows, None]
            dones.append(gathered(mine * weights_pair[rows, None], order[1:]))
            halves.append(spread(dones[-1], order[0]))
        chunks.append(jnp.concatenate(halves, axis=0))
    whole = lax.optimization_barrier((whole, dones[0]))[0]
    quarters = jnp.split(whole, 4)
    whole = jnp.concatenate([whole_of(quarters[2 + k], quarters[k], order[0]) for k, order in enumerate(orders)])
    return whole, jnp.concatenate(chunks, axis=1), row_out


def on_device(embeddings, centroids, col_start):
    rows_here = embeddings.shape[0]
    cent_here = centroids.shape[0]
    n_total = rows_here * lax.axis_size("dp")
    k_total = cent_here * lax.axis_size("cent")

    bits = bits_of("dp")
    orders = (bits, [bits[1], bits[0]] + bits[2:])
    place = jnp.full((1,), lax.axis_index("dp"), jnp.int32)
    ups = [place >> bit & 1 for bit in bits]
    ups = [up == 1 for up in ups]
    ups, embeddings, centroids = lax.optimization_barrier((ups, embeddings, centroids))

    def chosen(bit, yes, no):
        return jnp.where(ups[bit].reshape((1,) * yes.ndim), yes, no)

    def sent_and_kept(value):
        quarters = jnp.split(value, 4)
        lows, highs = quarters[0::2], quarters[1::2]
        sent = [chosen(order[0], low, high) for order, low, high in zip(orders, lows, highs)]
        kept = [chosen(order[0], high, low) for order, low, high in zip(orders, lows, highs)]
        return jnp.concatenate(sent + kept)

    def aligned(value, mask):
        quarters = jnp.split(value, 4)
        for k, order in enumerate(orders):
            if mask >> order[0] & 1:
                quarters[k], quarters[2 + k] = quarters[2 + k], quarters[k]
        return jnp.concatenate(quarters)

    scores = lax.dot_general(
        sent_and_kept(centroids), embeddings, (((1,), (1,)), ((), ())), preferred_element_type=jnp.float32
    ) * (1.0 / math.sqrt(embeddings.shape[1]))
    col_now = sent_and_kept(col_start)
    for step_index in range(ITERS):
        shifted = scores + col_now[:, None]
        top = jnp.max(shifted, axis=0)
        part = top + jnp.log(jnp.sum(jnp.exp(shifted - top[None, :]), axis=0))
        row_now = -math.log(n_total) - lse_over(part, "cent", 1)
        lifted = scores + row_now[None, :]
        top = jnp.max(lifted, axis=1)
        terms = jnp.exp(lifted - top[:, None])
        mass = jnp.sum(terms, axis=1)
        part = top + jnp.log(mass)
        if step_index < ITERS - 1:
            col_now = -math.log(k_total) - lse_over(part, "dp", 2, aligned)
    whole, new_centroids, row_out = last_sum(
        terms.astype(jnp.bfloat16), part, mass, row_now, embeddings, chosen, orders, aligned
    )
    return (new_centroids, row_out.reshape(rows_here), -math.log(k_total) - whole)


def solution(mesh):
    placed = (P("dp", None), P("cent", None), P("cent"))
    return jax.shard_map(
        on_device,
        mesh=mesh,
        in_specs=placed,
        out_specs=(P("cent", None), P("dp"), P("cent")),
        check_vma=False,
    )
```

```python
import functools
import math

import jax
import jax.numpy as jnp
from jax import lax
from jax.experimental import pallas as pl
from jax.experimental.pallas import tpu as pltpu
from jax.sharding import PartitionSpec as P

ITERS = 3
CHUNKS = 2
LANES = 128
VMEM_BYTES = 24 * 2**20


def bits_of(axis):
    size = lax.axis_size(axis)
    assert size & (size - 1) == 0
    return list(range(size.bit_length() - 1))


def flipped(x, axis, mask):
    size = lax.axis_size(axis)
    return lax.ppermute(x, axis, [(k, k ^ mask) for k in range(size)])


def lse(first, second):
    top = jnp.maximum(first, second)
    return top + jnp.log(jnp.exp(first - top) + jnp.exp(second - top))


def lse_over(x, axis, first_group, aligned=lambda value, mask: value):
    bits = bits_of(axis)
    groups = [bits[:first_group]] + [bits[k:k + 2] for k in range(first_group, len(bits), 2)]
    for group in groups:
        masks = [1 << bit for bit in group]
        if len(masks) == 2:
            far = masks[0] | masks[1]
            far = aligned(flipped(x, axis, far), far)
            near = [aligned(flipped(x, axis, mask), mask) for mask in reversed(masks)]
            x = lse(lax.optimization_barrier(lse(x, far)), lse(*near))
        else:
            for mask in masks:
                x = lse(x, aligned(flipped(x, axis, mask), mask))
    return x


def column(values):
    lane = lax.broadcasted_iota(jnp.int32, (LANES, LANES), 1)
    diagonal = lane == lax.broadcasted_iota(jnp.int32, (LANES, LANES), 0)
    return jnp.sum(jnp.where(diagonal, values, 0.0), axis=1, keepdims=True)


def quarter_places(orders, quarter):
    ups = [lax.axis_index("dp") >> order[0] & 1 for order in orders]
    sent = [(2 * k + 1 - up) * quarter for k, up in enumerate(ups)]
    return sent + [(2 * k + up) * quarter for k, up in enumerate(ups)]


def place_kernel(chunk, orders, *refs):
    blocks, (out, sent) = refs[:4], refs[-2:]
    quarter, width = blocks[0].shape
    copies = []
    for k, start in enumerate(quarter_places(orders, quarter)):
        rows = pl.ds(pl.multiple_of(start, LANES), quarter)
        copies.append(pltpu.make_async_copy(blocks[k], out.at[rows, pl.ds(chunk * width, width)], sent.at[k]))
        copies[-1].start()
    for copy in copies:
        copy.wait()


def placed(chunk, orders, blocks, shape, so_far):
    vmem = pl.BlockSpec(memory_space=pltpu.VMEM)
    anywhere = pl.BlockSpec(memory_space=pl.ANY)
    return pl.pallas_call(
        functools.partial(place_kernel, chunk, orders),
        out_shape=jax.ShapeDtypeStruct(shape, blocks[0].dtype),
        in_specs=[vmem] * 4 + [anywhere] * len(so_far),
        out_specs=anywhere,
        scratch_shapes=[pltpu.SemaphoreType.DMA((4,))],
        input_output_aliases={4: 0} if so_far else {},
        compiler_params=pltpu.CompilerParams(vmem_limit_bytes=VMEM_BYTES),
    )(*blocks, *so_far)


def means_kernel(is_kept, plan, embeddings, mass, *rest):
    half = plan.shape[0] // 2
    quarter = half // 2
    sums = jnp.dot(plan[pl.ds(is_kept * half, half), :], embeddings[...], preferred_element_type=jnp.float32)
    if is_kept:
        weights, row, out, row_out = rest
        row_out[...] = row[...]
    else:
        out, = rest
    for block in range(half // LANES):
        factor = 1.0 / column(mass[pl.ds(is_kept * (half // LANES) + block, 1), :])
        if is_kept:
            factor = factor * column(weights[pl.ds(block, 1), :])
        place = pl.ds(block * LANES % quarter, LANES)
        values = sums[block * LANES:(block + 1) * LANES] * factor
        out[block * LANES // quarter, place, :] = values.astype(out.dtype)


def means_of(is_kept, plan, embeddings, mass, *rest):
    count, rows_here = plan.shape
    depth = embeddings.shape[1]
    vmem = pl.BlockSpec(memory_space=pltpu.VMEM)
    out = jax.ShapeDtypeStruct((2, count // 4, depth), jnp.float32 if is_kept else jnp.bfloat16)
    row_out = jax.ShapeDtypeStruct((1, rows_here), jnp.float32)
    return pl.pallas_call(
        functools.partial(means_kernel, is_kept),
        out_shape=(out, row_out) if is_kept else out,
        in_specs=[vmem] * (3 + len(rest)),
        out_specs=(vmem, pl.BlockSpec((1, rows_here), lambda: (0, 0))) if is_kept else vmem,
        compiler_params=pltpu.CompilerParams(vmem_limit_bytes=VMEM_BYTES),
        cost_estimate=pl.CostEstimate(
            flops=count * rows_here * depth, bytes_accessed=2 * rows_here * depth, transcendentals=0
        ),
    )(plan, embeddings, mass.reshape(count // LANES, LANES), *rest)


def last_sum(plan, part, mass, row_now, embeddings, chosen, orders, aligned):
    quarter = part.shape[0] // 4
    first, second = orders[0][:2]
    partners = {bit: aligned(flipped(part, "dp", 1 << bit), 1 << bit) for bit in (first, second)}
    sent = means_of(0, plan, embeddings, mass)
    got = [flipped(sent[k], "dp", 1 << order[0]) for k, order in enumerate(orders)]
    pairs = {bit: lse(partners[bit], part) for bit in (first, second)}
    whole = pairs[first]
    for bit in orders[0][1:]:
        whole = lse(aligned(flipped(whole, "dp", 1 << bit), 1 << bit), whole)

    def kept_of(lower, upper):
        return jnp.concatenate([lower[2 * quarter:3 * quarter], upper[3 * quarter:]])

    pair = kept_of(pairs[first], pairs[second])
    weights = jnp.exp(kept_of(part, part) - pair).reshape(2 * quarter // LANES, LANES)
    kept, row_out = means_of(1, plan, embeddings, mass, weights, row_now[None, :])
    weights = jnp.exp(kept_of(partners[first], partners[second]) - pair)
    weights_pair = jnp.exp(pair - kept_of(whole, whole))

    def gathered(mine, order):
        if len(order) == 1:
            mine = mine.astype(jnp.bfloat16)
            other = flipped(mine, "dp", 1 << order[0])
            return (mine.astype(jnp.float32) + other.astype(jnp.float32)).astype(jnp.bfloat16)
        low, high = jnp.split(mine, 2, axis=0)
        got = flipped(chosen(order[0], low, high).astype(jnp.bfloat16), "dp", 1 << order[0])
        done = gathered(chosen(order[0], high, low) + got.astype(jnp.float32), order[1:])
        other = flipped(done, "dp", 1 << order[0])
        return jnp.concatenate([chosen(order[0], other, done), chosen(order[0], done, other)], axis=0)

    width = kept.shape[2] // CHUNKS
    shape = (part.shape[0], kept.shape[2])
    outs = []
    firsts = []
    for chunk in range(CHUNKS):
        columns = slice(chunk * width, (chunk + 1) * width)
        dones = []
        for k, order in enumerate(orders):
            rows = slice(k * quarter, (k + 1) * quarter)
            mine = kept[k, :, columns] + got[k][:, columns].astype(jnp.float32) * weights[rows, None]
            dones.append(gathered(mine * weights_pair[rows, None], order[1:]))
        firsts = firsts or dones
        blocks = [flipped(done, "dp", 1 << order[0]) for done, order in zip(dones, orders)] + dones
        outs = [placed(chunk, orders, blocks, shape, outs)]
    whole = lax.optimization_barrier((whole, firsts[0]))[0]
    quarters = jnp.split(whole, 4)
    halves = []
    for k, order in enumerate(orders):
        sent, kept = quarters[k], quarters[2 + k]
        halves += [chosen(order[0], sent, kept), chosen(order[0], kept, sent)]
    return outs[0], row_out.reshape(row_now.shape), jnp.concatenate(halves)


def on_device(embeddings, centroids, col_start):
    rows_here = embeddings.shape[0]
    cent_here = centroids.shape[0]
    n_total = rows_here * lax.axis_size("dp")
    k_total = cent_here * lax.axis_size("cent")

    bits = bits_of("dp")
    orders = (bits, [bits[1], bits[0]] + bits[2:])
    place = jnp.full((1,), lax.axis_index("dp"), jnp.int32)
    ups = [place >> bit & 1 for bit in bits]
    ups = [up == 1 for up in ups]
    ups, embeddings, centroids = lax.optimization_barrier((ups, embeddings, centroids))

    def chosen(bit, yes, no):
        return jnp.where(ups[bit].reshape((1,) * yes.ndim), yes, no)

    def sent_and_kept(value):
        quarters = jnp.split(value, 4)
        lows, highs = quarters[0::2], quarters[1::2]
        sent = [chosen(order[0], low, high) for order, low, high in zip(orders, lows, highs)]
        kept = [chosen(order[0], high, low) for order, low, high in zip(orders, lows, highs)]
        return jnp.concatenate(sent + kept)

    def aligned(value, mask):
        quarters = jnp.split(value, 4)
        for k, order in enumerate(orders):
            if mask >> order[0] & 1:
                quarters[k], quarters[2 + k] = quarters[2 + k], quarters[k]
        return jnp.concatenate(quarters)

    scores = lax.dot_general(
        sent_and_kept(centroids), embeddings, (((1,), (1,)), ((), ())), preferred_element_type=jnp.float32
    ) * (1.0 / math.sqrt(embeddings.shape[1]))
    col_now = sent_and_kept(col_start)
    for step_index in range(ITERS):
        shifted = scores + col_now[:, None]
        top = jnp.max(shifted, axis=0)
        part = top + jnp.log(jnp.sum(jnp.exp(shifted - top[None, :]), axis=0))
        row_now = -math.log(n_total) - lse_over(part, "cent", 1)
        lifted = scores + row_now[None, :]
        top = jnp.max(lifted, axis=1)
        terms = jnp.exp(lifted - top[:, None])
        mass = jnp.sum(terms, axis=1)
        part = top + jnp.log(mass)
        if step_index < ITERS - 1:
            col_now = -math.log(k_total) - lse_over(part, "dp", 2, aligned)
    plan = terms.astype(jnp.bfloat16)
    new_centroids, row_out, whole = last_sum(plan, part, mass, row_now, embeddings, chosen, orders, aligned)
    return new_centroids, row_out, -math.log(k_total) - whole


def solution(mesh):
    specs = (P("dp", None), P("cent", None), P("cent"))
    return jax.shard_map(
        on_device,
        mesh=mesh,
        in_specs=specs,
        out_specs=(P("cent", None), P("dp"), P("cent")),
        check_vma=False,
    )
```

```python
import functools
import math

import jax
import jax.numpy as jnp
from jax import lax
from jax.experimental import pallas as pl
from jax.experimental.pallas import tpu as pltpu
from jax.sharding import PartitionSpec as P

ITERS = 3
CHUNKS = 2
LANES = 128
VMEM_BYTES = 24 * 2**20


def bits_of(axis):
    size = lax.axis_size(axis)
    assert size & (size - 1) == 0
    return list(range(size.bit_length() - 1))


def flipped(x, axis, mask):
    size = lax.axis_size(axis)
    return lax.ppermute(x, axis, [(k, k ^ mask) for k in range(size)])


def lse(first, second):
    top = jnp.maximum(first, second)
    return top + jnp.log(jnp.exp(first - top) + jnp.exp(second - top))


def lse_over(x, axis, bits, odd_only=False, aligned=lambda value, mask: value):
    def partner(value, mask):
        places = range(1 if odd_only else 0, lax.axis_size(axis), 2 if odd_only else 1)
        return aligned(lax.ppermute(value, axis, [(k, k ^ mask) for k in places]), mask)

    for masks in ([1 << bit for bit in bits[k:k + 2]] for k in range(0, len(bits), 2)):
        if len(masks) == 2:
            far = partner(x, masks[0] | masks[1])
            near = [partner(x, mask) for mask in reversed(masks)]
            x = lse(lax.optimization_barrier(lse(x, far)), lse(*near))
        else:
            x = lse(x, partner(x, masks[0]))
    return x


def lse_over_cent(x, odd):
    size = lax.axis_size("cent")
    x = lse(x, lax.ppermute(x, "cent", [(k, k + 1) for k in range(0, size, 2)]))
    x = lse_over(x, "cent", bits_of("cent")[1:], odd_only=True)
    back = lax.ppermute(x, "cent", [(k + 1, k) for k in range(0, size, 2)])
    return jnp.where(odd, x, back)


def column(values):
    lane = lax.broadcasted_iota(jnp.int32, (LANES, LANES), 1)
    diagonal = lane == lax.broadcasted_iota(jnp.int32, (LANES, LANES), 0)
    return jnp.sum(jnp.where(diagonal, values, 0.0), axis=1, keepdims=True)


def quarter_places(orders, quarter):
    ups = [lax.axis_index("dp") >> order[0] & 1 for order in orders]
    sent = [(2 * k + 1 - up) * quarter for k, up in enumerate(ups)]
    return sent + [(2 * k + up) * quarter for k, up in enumerate(ups)]


def place_kernel(chunk, orders, *refs):
    blocks, (out, sent) = refs[:4], refs[-2:]
    quarter, width = blocks[0].shape
    copies = []
    for k, start in enumerate(quarter_places(orders, quarter)):
        rows = pl.ds(pl.multiple_of(start, LANES), quarter)
        copies.append(pltpu.make_async_copy(blocks[k], out.at[rows, pl.ds(chunk * width, width)], sent.at[k]))
        copies[-1].start()
    for copy in copies:
        copy.wait()


def placed(chunk, orders, blocks, shape, so_far):
    vmem = pl.BlockSpec(memory_space=pltpu.VMEM)
    anywhere = pl.BlockSpec(memory_space=pl.ANY)
    return pl.pallas_call(
        functools.partial(place_kernel, chunk, orders),
        out_shape=jax.ShapeDtypeStruct(shape, blocks[0].dtype),
        in_specs=[vmem] * 4 + [anywhere] * len(so_far),
        out_specs=anywhere,
        scratch_shapes=[pltpu.SemaphoreType.DMA((4,))],
        input_output_aliases={4: 0} if so_far else {},
        compiler_params=pltpu.CompilerParams(vmem_limit_bytes=VMEM_BYTES),
    )(*blocks, *so_far)


def means_kernel(is_kept, plan, embeddings, mass, *rest):
    half = plan.shape[0] // 2
    quarter = half // 2
    sums = jnp.dot(plan[pl.ds(is_kept * half, half), :], embeddings[...], preferred_element_type=jnp.float32)
    if is_kept:
        weights, row, out, row_out = rest
        row_out[...] = row[...]
    else:
        out, = rest
    for block in range(half // LANES):
        factor = 1.0 / column(mass[pl.ds(is_kept * (half // LANES) + block, 1), :])
        if is_kept:
            factor = factor * column(weights[pl.ds(block, 1), :])
        place = pl.ds(block * LANES % quarter, LANES)
        values = sums[block * LANES:(block + 1) * LANES] * factor
        out[block * LANES // quarter, place, :] = values.astype(out.dtype)


def means_of(is_kept, plan, embeddings, mass, *rest):
    count, rows_here = plan.shape
    depth = embeddings.shape[1]
    vmem = pl.BlockSpec(memory_space=pltpu.VMEM)
    out = jax.ShapeDtypeStruct((2, count // 4, depth), jnp.float32 if is_kept else jnp.bfloat16)
    row_out = jax.ShapeDtypeStruct((1, rows_here), jnp.float32)
    return pl.pallas_call(
        functools.partial(means_kernel, is_kept),
        out_shape=(out, row_out) if is_kept else out,
        in_specs=[vmem] * (3 + len(rest)),
        out_specs=(vmem, pl.BlockSpec((1, rows_here), lambda: (0, 0))) if is_kept else vmem,
        compiler_params=pltpu.CompilerParams(vmem_limit_bytes=VMEM_BYTES),
        cost_estimate=pl.CostEstimate(
            flops=count * rows_here * depth, bytes_accessed=2 * rows_here * depth, transcendentals=0
        ),
    )(plan, embeddings, mass.reshape(count // LANES, LANES), *rest)


def last_sum(plan, part, mass, row_now, embeddings, chosen, orders, aligned):
    quarter = part.shape[0] // 4
    first, second = orders[0][:2]
    partners = {bit: aligned(flipped(part, "dp", 1 << bit), 1 << bit) for bit in (first, second)}
    sent = means_of(0, plan, embeddings, mass)
    got = [flipped(sent[k], "dp", 1 << order[0]) for k, order in enumerate(orders)]
    pairs = {bit: lse(partners[bit], part) for bit in (first, second)}
    whole = pairs[first]
    for bit in orders[0][1:]:
        whole = lse(aligned(flipped(whole, "dp", 1 << bit), 1 << bit), whole)

    def kept_of(lower, upper):
        return jnp.concatenate([lower[2 * quarter:3 * quarter], upper[3 * quarter:]])

    pair = kept_of(pairs[first], pairs[second])
    weights = jnp.exp(kept_of(part, part) - pair).reshape(2 * quarter // LANES, LANES)
    kept, row_out = means_of(1, plan, embeddings, mass, weights, row_now[None, :])
    weights = jnp.exp(kept_of(partners[first], partners[second]) - pair)
    weights_pair = jnp.exp(pair - kept_of(whole, whole))

    def gathered(mine, order):
        if len(order) == 1:
            mine = mine.astype(jnp.bfloat16)
            other = flipped(mine, "dp", 1 << order[0])
            return (mine.astype(jnp.float32) + other.astype(jnp.float32)).astype(jnp.bfloat16)
        low, high = jnp.split(mine, 2, axis=0)
        got = flipped(chosen(order[0], low, high).astype(jnp.bfloat16), "dp", 1 << order[0])
        done = gathered(chosen(order[0], high, low) + got.astype(jnp.float32), order[1:])
        other = flipped(done, "dp", 1 << order[0])
        return jnp.concatenate([chosen(order[0], other, done), chosen(order[0], done, other)], axis=0)

    width = kept.shape[2] // CHUNKS
    shape = (part.shape[0], kept.shape[2])
    outs = []
    firsts = []
    for chunk in range(CHUNKS):
        columns = slice(chunk * width, (chunk + 1) * width)
        dones = []
        for k, order in enumerate(orders):
            rows = slice(k * quarter, (k + 1) * quarter)
            mine = kept[k, :, columns] + got[k][:, columns].astype(jnp.float32) * weights[rows, None]
            dones.append(gathered(mine * weights_pair[rows, None], order[1:]))
        firsts = firsts or dones
        blocks = [flipped(done, "dp", 1 << order[0]) for done, order in zip(dones, orders)] + dones
        outs = [placed(chunk, orders, blocks, shape, outs)]
    whole = lax.optimization_barrier((whole, firsts[0]))[0]
    quarters = jnp.split(whole, 4)
    halves = []
    for k, order in enumerate(orders):
        sent, kept = quarters[k], quarters[2 + k]
        halves += [chosen(order[0], sent, kept), chosen(order[0], kept, sent)]
    return outs[0], row_out.reshape(row_now.shape), jnp.concatenate(halves)


def on_device(embeddings, centroids, col_start):
    rows_here = embeddings.shape[0]
    cent_here = centroids.shape[0]
    n_total = rows_here * lax.axis_size("dp")
    k_total = cent_here * lax.axis_size("cent")

    bits = bits_of("dp")
    orders = (bits, [bits[1], bits[0]] + bits[2:])
    place = jnp.full((1,), lax.axis_index("dp"), jnp.int32)
    ups = [place >> bit & 1 for bit in bits]
    ups = [up == 1 for up in ups]
    odd = jnp.full((1,), lax.axis_index("cent"), jnp.int32) & 1 == 1
    ups, odd, embeddings, centroids = lax.optimization_barrier((ups, odd, embeddings, centroids))

    def chosen(bit, yes, no):
        return jnp.where(ups[bit].reshape((1,) * yes.ndim), yes, no)

    def sent_and_kept(value):
        quarters = jnp.split(value, 4)
        lows, highs = quarters[0::2], quarters[1::2]
        sent = [chosen(order[0], low, high) for order, low, high in zip(orders, lows, highs)]
        kept = [chosen(order[0], high, low) for order, low, high in zip(orders, lows, highs)]
        return jnp.concatenate(sent + kept)

    def aligned(value, mask):
        quarters = jnp.split(value, 4)
        for k, order in enumerate(orders):
            if mask >> order[0] & 1:
                quarters[k], quarters[2 + k] = quarters[2 + k], quarters[k]
        return jnp.concatenate(quarters)

    scores = lax.dot_general(
        sent_and_kept(centroids), embeddings, (((1,), (1,)), ((), ())), preferred_element_type=jnp.float32
    ) * (1.0 / math.sqrt(embeddings.shape[1]))
    col_now = sent_and_kept(col_start)
    for step_index in range(ITERS):
        shifted = scores + col_now[:, None]
        top = jnp.max(shifted, axis=0)
        part = top + jnp.log(jnp.sum(jnp.exp(shifted - top[None, :]), axis=0))
        row_now = -math.log(n_total) - lse_over_cent(part, odd)
        lifted = scores + row_now[None, :]
        top = jnp.max(lifted, axis=1)
        terms = jnp.exp(lifted - top[:, None])
        mass = jnp.sum(terms, axis=1)
        part = top + jnp.log(mass)
        if step_index < ITERS - 1:
            col_now = -math.log(k_total) - lse_over(part, "dp", bits, aligned=aligned)
    plan = terms.astype(jnp.bfloat16)
    new_centroids, row_out, whole = last_sum(plan, part, mass, row_now, embeddings, chosen, orders, aligned)
    return new_centroids, row_out, -math.log(k_total) - whole


def solution(mesh):
    specs = (P("dp", None), P("cent", None), P("cent"))
    return jax.shard_map(
        on_device,
        mesh=mesh,
        in_specs=specs,
        out_specs=(P("cent", None), P("dp"), P("cent")),
        check_vma=False,
    )
```

```python
import functools
import math

import jax
import jax.numpy as jnp
from jax import lax
from jax.experimental import pallas as pl
from jax.experimental.pallas import tpu as pltpu
from jax.sharding import PartitionSpec as P

ITERS = 3
CHUNKS = 2
LANES = 128
VMEM_BYTES = 24 * 2**20


def bits_of(axis):
    size = lax.axis_size(axis)
    assert size & (size - 1) == 0
    return list(range(size.bit_length() - 1))


def flipped(x, axis, mask):
    size = lax.axis_size(axis)
    return lax.ppermute(x, axis, [(k, k ^ mask) for k in range(size)])


def lse(first, second):
    top = jnp.maximum(first, second)
    return top + jnp.log(jnp.exp(first - top) + jnp.exp(second - top))


def lse_over(x, axis, bits, odd_only=False, aligned=lambda value, mask: value):
    def partner(value, mask):
        pairs = [(k, k if odd_only and k % 2 == 0 else k ^ mask) for k in range(lax.axis_size(axis))]
        return aligned(lax.ppermute(value, axis, pairs), mask)

    for masks in ([1 << bit for bit in bits[k:k + 2]] for k in range(0, len(bits), 2)):
        if len(masks) == 2:
            far = partner(x, masks[0] | masks[1])
            near = [partner(x, mask) for mask in reversed(masks)]
            x = lse(lax.optimization_barrier(lse(x, far)), lse(*near))
        else:
            x = lse(x, partner(x, masks[0]))
    return x


def lse_over_cent(x, odd):
    x = lse(x, flipped(x, "cent", 1))
    x = lse_over(x, "cent", bits_of("cent")[1:], odd_only=True)
    return jnp.where(odd, x, flipped(x, "cent", 1))


def column(values):
    lane = lax.broadcasted_iota(jnp.int32, (LANES, LANES), 1)
    diagonal = lane == lax.broadcasted_iota(jnp.int32, (LANES, LANES), 0)
    return jnp.sum(jnp.where(diagonal, values, 0.0), axis=1, keepdims=True)


def quarter_places(orders, quarter):
    ups = [lax.axis_index("dp") >> order[0] & 1 for order in orders]
    sent = [(2 * k + 1 - up) * quarter for k, up in enumerate(ups)]
    return sent + [(2 * k + up) * quarter for k, up in enumerate(ups)]


def place_kernel(chunk, orders, *refs):
    blocks, (out, sent) = refs[:4], refs[-2:]
    quarter, width = blocks[0].shape
    copies = []
    for k, start in enumerate(quarter_places(orders, quarter)):
        rows = pl.ds(pl.multiple_of(start, LANES), quarter)
        copies.append(pltpu.make_async_copy(blocks[k], out.at[rows, pl.ds(chunk * width, width)], sent.at[k]))
        copies[-1].start()
    for copy in copies:
        copy.wait()


def placed(chunk, orders, blocks, shape, so_far):
    vmem = pl.BlockSpec(memory_space=pltpu.VMEM)
    anywhere = pl.BlockSpec(memory_space=pl.ANY)
    return pl.pallas_call(
        functools.partial(place_kernel, chunk, orders),
        out_shape=jax.ShapeDtypeStruct(shape, blocks[0].dtype),
        in_specs=[vmem] * 4 + [anywhere] * len(so_far),
        out_specs=anywhere,
        scratch_shapes=[pltpu.SemaphoreType.DMA((4,))],
        input_output_aliases={4: 0} if so_far else {},
        compiler_params=pltpu.CompilerParams(vmem_limit_bytes=VMEM_BYTES),
    )(*blocks, *so_far)


def means_kernel(is_kept, plan, embeddings, mass, *rest):
    half = plan.shape[0] // 2
    quarter = half // 2
    sums = jnp.dot(plan[pl.ds(is_kept * half, half), :], embeddings[...], preferred_element_type=jnp.float32)
    if is_kept:
        weights, row, out, row_out = rest
        row_out[...] = row[...]
    else:
        out, = rest
    for block in range(half // LANES):
        factor = 1.0 / column(mass[pl.ds(is_kept * (half // LANES) + block, 1), :])
        if is_kept:
            factor = factor * column(weights[pl.ds(block, 1), :])
        place = pl.ds(block * LANES % quarter, LANES)
        values = sums[block * LANES:(block + 1) * LANES] * factor
        out[block * LANES // quarter, place, :] = values.astype(out.dtype)


def means_of(is_kept, plan, embeddings, mass, *rest):
    count, rows_here = plan.shape
    depth = embeddings.shape[1]
    vmem = pl.BlockSpec(memory_space=pltpu.VMEM)
    out = jax.ShapeDtypeStruct((2, count // 4, depth), jnp.float32 if is_kept else jnp.bfloat16)
    row_out = jax.ShapeDtypeStruct((1, rows_here), jnp.float32)
    return pl.pallas_call(
        functools.partial(means_kernel, is_kept),
        out_shape=(out, row_out) if is_kept else out,
        in_specs=[vmem] * (3 + len(rest)),
        out_specs=(vmem, pl.BlockSpec((1, rows_here), lambda: (0, 0))) if is_kept else vmem,
        compiler_params=pltpu.CompilerParams(vmem_limit_bytes=VMEM_BYTES),
        cost_estimate=pl.CostEstimate(
            flops=count * rows_here * depth, bytes_accessed=2 * rows_here * depth, transcendentals=0
        ),
    )(plan, embeddings, mass.reshape(count // LANES, LANES), *rest)


def last_sum(plan, part, mass, row_now, embeddings, chosen, orders, aligned):
    quarter = part.shape[0] // 4
    first, second = orders[0][:2]
    partners = {bit: aligned(flipped(part, "dp", 1 << bit), 1 << bit) for bit in (first, second)}
    sent = means_of(0, plan, embeddings, mass)
    got = [flipped(sent[k], "dp", 1 << order[0]) for k, order in enumerate(orders)]
    pairs = {bit: lse(partners[bit], part) for bit in (first, second)}
    whole = pairs[first]
    for bit in orders[0][1:]:
        whole = lse(aligned(flipped(whole, "dp", 1 << bit), 1 << bit), whole)

    def kept_of(lower, upper):
        return jnp.concatenate([lower[2 * quarter:3 * quarter], upper[3 * quarter:]])

    pair = kept_of(pairs[first], pairs[second])
    weights = jnp.exp(kept_of(part, part) - pair).reshape(2 * quarter // LANES, LANES)
    kept, row_out = means_of(1, plan, embeddings, mass, weights, row_now[None, :])
    weights = jnp.exp(kept_of(partners[first], partners[second]) - pair)
    weights_pair = jnp.exp(pair - kept_of(whole, whole))

    def gathered(mine, order):
        if len(order) == 1:
            mine = mine.astype(jnp.bfloat16)
            other = flipped(mine, "dp", 1 << order[0])
            return (mine.astype(jnp.float32) + other.astype(jnp.float32)).astype(jnp.bfloat16)
        low, high = jnp.split(mine, 2, axis=0)
        got = flipped(chosen(order[0], low, high).astype(jnp.bfloat16), "dp", 1 << order[0])
        done = gathered(chosen(order[0], high, low) + got.astype(jnp.float32), order[1:])
        other = flipped(done, "dp", 1 << order[0])
        return jnp.concatenate([chosen(order[0], other, done), chosen(order[0], done, other)], axis=0)

    width = kept.shape[2] // CHUNKS
    shape = (part.shape[0], kept.shape[2])
    outs = []
    firsts = []
    for chunk in range(CHUNKS):
        columns = slice(chunk * width, (chunk + 1) * width)
        dones = []
        for k, order in enumerate(orders):
            rows = slice(k * quarter, (k + 1) * quarter)
            mine = kept[k, :, columns] + got[k][:, columns].astype(jnp.float32) * weights[rows, None]
            dones.append(gathered(mine * weights_pair[rows, None], order[1:]))
        firsts = firsts or dones
        blocks = [flipped(done, "dp", 1 << order[0]) for done, order in zip(dones, orders)] + dones
        outs = [placed(chunk, orders, blocks, shape, outs)]
    whole = lax.optimization_barrier((whole, firsts[0]))[0]
    quarters = jnp.split(whole, 4)
    halves = []
    for k, order in enumerate(orders):
        sent, kept = quarters[k], quarters[2 + k]
        halves += [chosen(order[0], sent, kept), chosen(order[0], kept, sent)]
    return outs[0], row_out.reshape(row_now.shape), jnp.concatenate(halves)


def on_device(embeddings, centroids, col_start):
    rows_here = embeddings.shape[0]
    cent_here = centroids.shape[0]
    n_total = rows_here * lax.axis_size("dp")
    k_total = cent_here * lax.axis_size("cent")

    bits = bits_of("dp")
    orders = (bits, [bits[1], bits[0]] + bits[2:])
    place = jnp.full((1,), lax.axis_index("dp"), jnp.int32)
    ups = [place >> bit & 1 for bit in bits]
    ups = [up == 1 for up in ups]
    odd = jnp.full((1,), lax.axis_index("cent"), jnp.int32) & 1 == 1
    ups, odd, embeddings, centroids = lax.optimization_barrier((ups, odd, embeddings, centroids))

    def chosen(bit, yes, no):
        return jnp.where(ups[bit].reshape((1,) * yes.ndim), yes, no)

    def sent_and_kept(value):
        quarters = jnp.split(value, 4)
        lows, highs = quarters[0::2], quarters[1::2]
        sent = [chosen(order[0], low, high) for order, low, high in zip(orders, lows, highs)]
        kept = [chosen(order[0], high, low) for order, low, high in zip(orders, lows, highs)]
        return jnp.concatenate(sent + kept)

    def aligned(value, mask):
        quarters = jnp.split(value, 4)
        for k, order in enumerate(orders):
            if mask >> order[0] & 1:
                quarters[k], quarters[2 + k] = quarters[2 + k], quarters[k]
        return jnp.concatenate(quarters)

    scores = lax.dot_general(
        sent_and_kept(centroids), embeddings, (((1,), (1,)), ((), ())), preferred_element_type=jnp.float32
    ) * (1.0 / math.sqrt(embeddings.shape[1]))
    col_now = sent_and_kept(col_start)
    for step_index in range(ITERS):
        shifted = scores + col_now[:, None]
        top = jnp.max(shifted, axis=0)
        part = top + jnp.log(jnp.sum(jnp.exp(shifted - top[None, :]), axis=0))
        row_now = -math.log(n_total) - lse_over_cent(part, odd)
        lifted = scores + row_now[None, :]
        top = jnp.max(lifted, axis=1)
        terms = jnp.exp(lifted - top[:, None])
        mass = jnp.sum(terms, axis=1)
        part = top + jnp.log(mass)
        if step_index < ITERS - 1:
            col_now = -math.log(k_total) - lse_over(part, "dp", bits, aligned=aligned)
    plan = terms.astype(jnp.bfloat16)
    new_centroids, row_out, whole = last_sum(plan, part, mass, row_now, embeddings, chosen, orders, aligned)
    return new_centroids, row_out, -math.log(k_total) - whole


def solution(mesh):
    specs = (P("dp", None), P("cent", None), P("cent"))
    return jax.shard_map(
        on_device,
        mesh=mesh,
        in_specs=specs,
        out_specs=(P("cent", None), P("dp"), P("cent")),
        check_vma=False,
    )
```

```python
import functools
import math

import jax
import jax.numpy as jnp
from jax import lax
from jax.experimental import pallas as pl
from jax.experimental.pallas import tpu as pltpu
from jax.sharding import PartitionSpec as P

ITERS = 3
CHUNKS = 2
LANES = 128
VMEM_BYTES = 24 * 2**20


def bits_of(axis):
    size = lax.axis_size(axis)
    assert size & (size - 1) == 0
    return list(range(size.bit_length() - 1))


def flipped(x, axis, mask):
    size = lax.axis_size(axis)
    return lax.ppermute(x, axis, [(k, k ^ mask) for k in range(size)])


def lse(first, second):
    top = jnp.maximum(first, second)
    return top + jnp.log(jnp.exp(first - top) + jnp.exp(second - top))


def lse_over_dp(x, aligned):
    bits = bits_of("dp")

    def partner(value, mask):
        return aligned(flipped(value, "dp", mask), mask)

    for masks in ([1 << bit for bit in bits[k:k + 2]] for k in range(0, len(bits), 2)):
        if len(masks) == 2:
            far = partner(x, masks[0] | masks[1])
            near = [partner(x, mask) for mask in reversed(masks)]
            x = lse(lax.optimization_barrier(lse(x, far)), lse(*near))
        else:
            x = lse(x, partner(x, masks[0]))
    return x


def lse_over_cent(x, odd):
    size = lax.axis_size("cent")
    near, middle, *rest = [1 << bit for bit in bits_of("cent")[1:]]

    def split(value, even_mask, odd_mask):
        return lax.ppermute(value, "cent", [(k, k ^ (odd_mask if k % 2 else even_mask)) for k in range(size)])

    x = lse(x, flipped(x, "cent", 1))
    second = split(x, near, middle)
    first = split(x, near, near | middle)
    x = jnp.where(odd, lse(second, first), lse(x, first))
    for mask in [1] + rest:
        x = lse(x, flipped(x, "cent", mask))
    return x


def column(values):
    lane = lax.broadcasted_iota(jnp.int32, (LANES, LANES), 1)
    diagonal = lane == lax.broadcasted_iota(jnp.int32, (LANES, LANES), 0)
    return jnp.sum(jnp.where(diagonal, values, 0.0), axis=1, keepdims=True)


def quarter_places(orders, quarter):
    ups = [lax.axis_index("dp") >> order[0] & 1 for order in orders]
    sent = [(2 * k + 1 - up) * quarter for k, up in enumerate(ups)]
    return sent + [(2 * k + up) * quarter for k, up in enumerate(ups)]


def place_kernel(chunk, orders, *refs):
    blocks, (out, sent) = refs[:4], refs[-2:]
    quarter, width = blocks[0].shape
    copies = []
    for k, start in enumerate(quarter_places(orders, quarter)):
        rows = pl.ds(pl.multiple_of(start, LANES), quarter)
        copies.append(pltpu.make_async_copy(blocks[k], out.at[rows, pl.ds(chunk * width, width)], sent.at[k]))
        copies[-1].start()
    for copy in copies:
        copy.wait()


def placed(chunk, orders, blocks, shape, so_far):
    vmem = pl.BlockSpec(memory_space=pltpu.VMEM)
    anywhere = pl.BlockSpec(memory_space=pl.ANY)
    return pl.pallas_call(
        functools.partial(place_kernel, chunk, orders),
        out_shape=jax.ShapeDtypeStruct(shape, blocks[0].dtype),
        in_specs=[vmem] * 4 + [anywhere] * len(so_far),
        out_specs=anywhere,
        scratch_shapes=[pltpu.SemaphoreType.DMA((4,))],
        input_output_aliases={4: 0} if so_far else {},
        compiler_params=pltpu.CompilerParams(vmem_limit_bytes=VMEM_BYTES),
    )(*blocks, *so_far)


def means_kernel(is_kept, plan, embeddings, mass, *rest):
    half = plan.shape[0] // 2
    quarter = half // 2
    sums = jnp.dot(plan[pl.ds(is_kept * half, half), :], embeddings[...], preferred_element_type=jnp.float32)
    if is_kept:
        weights, row, out, row_out = rest
        row_out[...] = row[...]
    else:
        out, = rest
    for block in range(half // LANES):
        factor = 1.0 / column(mass[pl.ds(is_kept * (half // LANES) + block, 1), :])
        if is_kept:
            factor = factor * column(weights[pl.ds(block, 1), :])
        place = pl.ds(block * LANES % quarter, LANES)
        values = sums[block * LANES:(block + 1) * LANES] * factor
        out[block * LANES // quarter, place, :] = values.astype(out.dtype)


def means_of(is_kept, plan, embeddings, mass, *rest):
    count, rows_here = plan.shape
    depth = embeddings.shape[1]
    vmem = pl.BlockSpec(memory_space=pltpu.VMEM)
    out = jax.ShapeDtypeStruct((2, count // 4, depth), jnp.float32 if is_kept else jnp.bfloat16)
    row_out = jax.ShapeDtypeStruct((1, rows_here), jnp.float32)
    return pl.pallas_call(
        functools.partial(means_kernel, is_kept),
        out_shape=(out, row_out) if is_kept else out,
        in_specs=[vmem] * (3 + len(rest)),
        out_specs=(vmem, pl.BlockSpec((1, rows_here), lambda: (0, 0))) if is_kept else vmem,
        compiler_params=pltpu.CompilerParams(vmem_limit_bytes=VMEM_BYTES),
        cost_estimate=pl.CostEstimate(
            flops=count * rows_here * depth, bytes_accessed=2 * rows_here * depth, transcendentals=0
        ),
    )(plan, embeddings, mass.reshape(count // LANES, LANES), *rest)


def last_sum(plan, part, mass, row_now, embeddings, chosen, orders, aligned):
    quarter = part.shape[0] // 4
    first, second = orders[0][:2]
    partners = {bit: aligned(flipped(part, "dp", 1 << bit), 1 << bit) for bit in (first, second)}
    sent = means_of(0, plan, embeddings, mass)
    got = [flipped(sent[k], "dp", 1 << order[0]) for k, order in enumerate(orders)]
    pairs = {bit: lse(partners[bit], part) for bit in (first, second)}
    whole = pairs[first]
    for bit in orders[0][1:]:
        whole = lse(aligned(flipped(whole, "dp", 1 << bit), 1 << bit), whole)

    def kept_of(lower, upper):
        return jnp.concatenate([lower[2 * quarter:3 * quarter], upper[3 * quarter:]])

    pair = kept_of(pairs[first], pairs[second])
    weights = jnp.exp(kept_of(part, part) - pair).reshape(2 * quarter // LANES, LANES)
    kept, row_out = means_of(1, plan, embeddings, mass, weights, row_now[None, :])
    weights = jnp.exp(kept_of(partners[first], partners[second]) - pair)
    weights_pair = jnp.exp(pair - kept_of(whole, whole))

    def gathered(mine, order):
        if len(order) == 1:
            mine = mine.astype(jnp.bfloat16)
            other = flipped(mine, "dp", 1 << order[0])
            return (mine.astype(jnp.float32) + other.astype(jnp.float32)).astype(jnp.bfloat16)
        low, high = jnp.split(mine, 2, axis=0)
        got = flipped(chosen(order[0], low, high).astype(jnp.bfloat16), "dp", 1 << order[0])
        done = gathered(chosen(order[0], high, low) + got.astype(jnp.float32), order[1:])
        other = flipped(done, "dp", 1 << order[0])
        return jnp.concatenate([chosen(order[0], other, done), chosen(order[0], done, other)], axis=0)

    width = kept.shape[2] // CHUNKS
    shape = (part.shape[0], kept.shape[2])
    outs = []
    firsts = []
    for chunk in range(CHUNKS):
        columns = slice(chunk * width, (chunk + 1) * width)
        dones = []
        for k, order in enumerate(orders):
            rows = slice(k * quarter, (k + 1) * quarter)
            mine = kept[k, :, columns] + got[k][:, columns].astype(jnp.float32) * weights[rows, None]
            dones.append(gathered(mine * weights_pair[rows, None], order[1:]))
        firsts = firsts or dones
        blocks = [flipped(done, "dp", 1 << order[0]) for done, order in zip(dones, orders)] + dones
        outs = [placed(chunk, orders, blocks, shape, outs)]
    whole = lax.optimization_barrier((whole, firsts[0]))[0]
    quarters = jnp.split(whole, 4)
    halves = []
    for k, order in enumerate(orders):
        sent, kept = quarters[k], quarters[2 + k]
        halves += [chosen(order[0], sent, kept), chosen(order[0], kept, sent)]
    return outs[0], row_out.reshape(row_now.shape), jnp.concatenate(halves)


def on_device(embeddings, centroids, col_start):
    rows_here = embeddings.shape[0]
    cent_here = centroids.shape[0]
    n_total = rows_here * lax.axis_size("dp")
    k_total = cent_here * lax.axis_size("cent")

    bits = bits_of("dp")
    orders = (bits, [bits[1], bits[0]] + bits[2:])
    place = jnp.full((1,), lax.axis_index("dp"), jnp.int32)
    ups = [place >> bit & 1 for bit in bits]
    ups = [up == 1 for up in ups]
    odd = jnp.full((1,), lax.axis_index("cent"), jnp.int32) & 1 == 1
    ups, odd, embeddings, centroids = lax.optimization_barrier((ups, odd, embeddings, centroids))

    def chosen(bit, yes, no):
        return jnp.where(ups[bit].reshape((1,) * yes.ndim), yes, no)

    def sent_and_kept(value):
        quarters = jnp.split(value, 4)
        lows, highs = quarters[0::2], quarters[1::2]
        sent = [chosen(order[0], low, high) for order, low, high in zip(orders, lows, highs)]
        kept = [chosen(order[0], high, low) for order, low, high in zip(orders, lows, highs)]
        return jnp.concatenate(sent + kept)

    def aligned(value, mask):
        quarters = jnp.split(value, 4)
        for k, order in enumerate(orders):
            if mask >> order[0] & 1:
                quarters[k], quarters[2 + k] = quarters[2 + k], quarters[k]
        return jnp.concatenate(quarters)

    scores = lax.dot_general(
        sent_and_kept(centroids), embeddings, (((1,), (1,)), ((), ())), preferred_element_type=jnp.float32
    ) * (1.0 / math.sqrt(embeddings.shape[1]))
    col_now = sent_and_kept(col_start)
    for step_index in range(ITERS):
        shifted = scores + col_now[:, None]
        top = jnp.max(shifted, axis=0)
        part = top + jnp.log(jnp.sum(jnp.exp(shifted - top[None, :]), axis=0))
        row_now = -math.log(n_total) - lse_over_cent(part, odd)
        lifted = scores + row_now[None, :]
        top = jnp.max(lifted, axis=1)
        terms = jnp.exp(lifted - top[:, None])
        mass = jnp.sum(terms, axis=1)
        part = top + jnp.log(mass)
        if step_index < ITERS - 1:
            col_now = -math.log(k_total) - lse_over_dp(part, aligned)
    plan = terms.astype(jnp.bfloat16)
    new_centroids, row_out, whole = last_sum(plan, part, mass, row_now, embeddings, chosen, orders, aligned)
    return new_centroids, row_out, -math.log(k_total) - whole


def solution(mesh):
    specs = (P("dp", None), P("cent", None), P("cent"))
    return jax.shard_map(
        on_device,
        mesh=mesh,
        in_specs=specs,
        out_specs=(P("cent", None), P("dp"), P("cent")),
        check_vma=False,
    )
```

```python
import functools
import math

import jax
import jax.numpy as jnp
from jax import lax
from jax.experimental import pallas as pl
from jax.experimental.pallas import tpu as pltpu
from jax.sharding import PartitionSpec as P

ITERS = 3
CHUNKS = 2
LANES = 128
VMEM_BYTES = 24 * 2**20


def bits_of(axis):
    size = lax.axis_size(axis)
    assert size & (size - 1) == 0
    return list(range(size.bit_length() - 1))


def flipped(x, axis, mask):
    size = lax.axis_size(axis)
    return lax.ppermute(x, axis, [(k, k ^ mask) for k in range(size)])


def lse(first, second):
    top = jnp.maximum(first, second)
    return top + jnp.log(jnp.exp(first - top) + jnp.exp(second - top))


def lse_over_dp(x, aligned):
    bits = bits_of("dp")

    def partner(value, mask):
        return aligned(flipped(value, "dp", mask), mask)

    for masks in ([1 << bit for bit in bits[k:k + 2]] for k in range(0, len(bits), 2)):
        if len(masks) == 2:
            far = partner(x, masks[0] | masks[1])
            near = [partner(x, mask) for mask in reversed(masks)]
            x = lse(lax.optimization_barrier(lse(x, far)), lse(*near))
        else:
            x = lse(x, partner(x, masks[0]))
    return x


def lse_over_cent(x, odd):
    size = lax.axis_size("cent")
    near, middle, *rest = [1 << bit for bit in bits_of("cent")[1:]]

    def split(value, even_mask, odd_mask):
        return lax.ppermute(value, "cent", [(k, k ^ (odd_mask if k % 2 else even_mask)) for k in range(size)])

    x = lse(x, flipped(x, "cent", 1))
    second = split(x, near, middle)
    first = split(x, near, near | middle)
    x = jnp.where(odd, lse(second, first), lse(x, first))
    for mask in [1] + rest:
        x = lse(x, flipped(x, "cent", mask))
    return x


def column(values):
    lane = lax.broadcasted_iota(jnp.int32, (LANES, LANES), 1)
    diagonal = lane == lax.broadcasted_iota(jnp.int32, (LANES, LANES), 0)
    return jnp.sum(jnp.where(diagonal, values, 0.0), axis=1, keepdims=True)


def quarter_places(orders, quarter):
    ups = [lax.axis_index("dp") >> order[0] & 1 for order in orders]
    sent = [(2 * k + 1 - up) * quarter for k, up in enumerate(ups)]
    return sent + [(2 * k + up) * quarter for k, up in enumerate(ups)]


def place_kernel(chunk, orders, *refs):
    blocks, (out, sent) = refs[:4], refs[-2:]
    quarter, width = blocks[0].shape
    copies = []
    for k, start in enumerate(quarter_places(orders, quarter)):
        rows = pl.ds(pl.multiple_of(start, LANES), quarter)
        copies.append(pltpu.make_async_copy(blocks[k], out.at[rows, pl.ds(chunk * width, width)], sent.at[k]))
        copies[-1].start()
    for copy in copies:
        copy.wait()


def placed(chunk, orders, blocks, shape, so_far):
    vmem = pl.BlockSpec(memory_space=pltpu.VMEM)
    anywhere = pl.BlockSpec(memory_space=pl.ANY)
    return pl.pallas_call(
        functools.partial(place_kernel, chunk, orders),
        out_shape=jax.ShapeDtypeStruct(shape, blocks[0].dtype),
        in_specs=[vmem] * 4 + [anywhere] * len(so_far),
        out_specs=anywhere,
        scratch_shapes=[pltpu.SemaphoreType.DMA((4,))],
        input_output_aliases={4: 0} if so_far else {},
        compiler_params=pltpu.CompilerParams(vmem_limit_bytes=VMEM_BYTES),
    )(*blocks, *so_far)


def means_kernel(is_kept, plan, embeddings, mass, *rest):
    half = plan.shape[0] // 2
    quarter = half // 2
    sums = jnp.dot(plan[pl.ds(is_kept * half, half), :], embeddings[...], preferred_element_type=jnp.float32)
    if is_kept:
        weights, row, out, row_out = rest
        row_out[...] = row[...]
    else:
        out = None
    for block in range(half // LANES):
        factor = 1.0 / column(mass[pl.ds(is_kept * (half // LANES) + block, 1), :])
        if is_kept:
            factor = factor * column(weights[pl.ds(block, 1), :])
        rows = pl.ds(block * LANES % quarter, LANES)
        values = sums[block * LANES:(block + 1) * LANES] * factor
        half_index = block * LANES // quarter
        if is_kept:
            out[half_index, rows, :] = values
        else:
            width = rest[0].shape[1]
            for chunk in range(CHUNKS):
                target = rest[2 * chunk + half_index]
                target[rows, :] = values[:, chunk * width:(chunk + 1) * width].astype(target.dtype)


def means_of(is_kept, plan, embeddings, mass, *rest):
    count, rows_here = plan.shape
    depth = embeddings.shape[1]
    vmem = pl.BlockSpec(memory_space=pltpu.VMEM)
    if is_kept:
        out_shape = (
            jax.ShapeDtypeStruct((2, count // 4, depth), jnp.float32),
            jax.ShapeDtypeStruct((1, rows_here), jnp.float32),
        )
        out_specs = (vmem, pl.BlockSpec((1, rows_here), lambda: (0, 0)))
    else:
        out_shape = [jax.ShapeDtypeStruct((count // 4, depth // CHUNKS), jnp.bfloat16)] * (2 * CHUNKS)
        out_specs = [vmem] * (2 * CHUNKS)
    return pl.pallas_call(
        functools.partial(means_kernel, is_kept),
        out_shape=out_shape,
        in_specs=[vmem] * (3 + len(rest)),
        out_specs=out_specs,
        compiler_params=pltpu.CompilerParams(vmem_limit_bytes=VMEM_BYTES),
        cost_estimate=pl.CostEstimate(
            flops=count * rows_here * depth, bytes_accessed=2 * rows_here * depth, transcendentals=0
        ),
    )(plan, embeddings, mass.reshape(count // LANES, LANES), *rest)


def last_sum(plan, part, mass, row_now, embeddings, chosen, orders, aligned):
    quarter = part.shape[0] // 4
    first, second = orders[0][:2]
    partners = {bit: aligned(flipped(part, "dp", 1 << bit), 1 << bit) for bit in (first, second)}
    sent = means_of(0, plan, embeddings, mass)
    got = [flipped(sent[2 * chunk + k], "dp", 1 << order[0]) for chunk in range(CHUNKS) for k, order in enumerate(orders)]

    def kept_of(lower, upper):
        return jnp.concatenate([lower[2 * quarter:3 * quarter], upper[3 * quarter:]])

    pairs = lax.optimization_barrier([lse(partners[first], part), lse(partners[second], part)])
    pair = kept_of(*pairs)
    weights = jnp.exp(kept_of(part, part) - pair).reshape(2 * quarter // LANES, LANES)
    kept, row_out = means_of(1, plan, embeddings, mass, weights, row_now[None, :])
    weights = jnp.exp(kept_of(partners[first], partners[second]) - pair)

    corner = flipped(partners[first], "dp", 1 << second)

    def exchanged(mine, bit, own, other):
        mine = mine.astype(jnp.bfloat16)
        theirs = flipped(mine, "dp", 1 << bit).astype(jnp.float32)
        mine = mine.astype(jnp.float32)
        lower = chosen(bit, theirs, mine) * chosen(bit, other, own)
        upper = chosen(bit, mine, theirs) * chosen(bit, own, other)
        return (lower + upper).astype(jnp.bfloat16)

    def gathered(mine, order, own, other):
        if len(order) == 1:
            return exchanged(mine, order[0], own, other)
        bit = order[0]
        low, high = jnp.split(mine, 2, axis=0)
        got = flipped(chosen(bit, low, high).astype(jnp.bfloat16), "dp", 1 << bit).astype(jnp.float32)
        own, other = (chosen(bit, high, low) for low, high in (jnp.split(x, 2, axis=0) for x in (own, other)))
        ones = jnp.ones((own.shape[0], 1), jnp.float32)
        done = gathered(chosen(bit, high, low) * own + got * other, order[1:], ones, ones)
        theirs = flipped(done, "dp", 1 << bit)
        return jnp.concatenate([chosen(bit, theirs, done), chosen(bit, done, theirs)], axis=0)

    width = kept.shape[2] // CHUNKS
    shape = (part.shape[0], kept.shape[2])
    mines = []
    for chunk in range(CHUNKS):
        columns = slice(chunk * width, (chunk + 1) * width)
        if chunk > 0:
            mines, kept, weights = lax.optimization_barrier((mines, kept, weights))
        for k in range(2):
            rows = slice(k * quarter, (k + 1) * quarter)
            mines.append(kept[k, :, columns] + got[2 * chunk + k].astype(jnp.float32) * weights[rows, None])

    pairs, partners, corner = lax.optimization_barrier((pairs, partners, corner, mines))[:3]
    corner = aligned(corner, 1 << second)
    whole = lse(pairs[0], lse(corner, partners[second]))
    for bit in orders[0][2:]:
        whole = lse(aligned(flipped(whole, "dp", 1 << bit), 1 << bit), whole)
    pair_other = kept_of(lse(partners[second], corner), lse(partners[first], corner))
    weights_own = jnp.exp(kept_of(*pairs) - kept_of(whole, whole))
    weights_other = jnp.exp(pair_other - kept_of(whole, whole))

    outs = []
    firsts = []
    for chunk in range(CHUNKS):
        dones = []
        for k, order in enumerate(orders):
            rows = slice(k * quarter, (k + 1) * quarter)
            dones.append(gathered(mines[2 * chunk + k], order[1:], weights_own[rows, None], weights_other[rows, None]))
        if chunk < CHUNKS - 1:
            dones, weights_own, weights_other = lax.optimization_barrier((dones, weights_own, weights_other))
        firsts = firsts or dones
        blocks = [flipped(done, "dp", 1 << order[0]) for done, order in zip(dones, orders)] + dones
        outs = [placed(chunk, orders, blocks, shape, outs)]
    whole = lax.optimization_barrier((whole, firsts[0]))[0]
    quarters = jnp.split(whole, 4)
    halves = []
    for k, order in enumerate(orders):
        sent, kept = quarters[k], quarters[2 + k]
        halves += [chosen(order[0], sent, kept), chosen(order[0], kept, sent)]
    return outs[0], row_out.reshape(row_now.shape), jnp.concatenate(halves)


def on_device(embeddings, centroids, col_start):
    rows_here = embeddings.shape[0]
    cent_here = centroids.shape[0]
    n_total = rows_here * lax.axis_size("dp")
    k_total = cent_here * lax.axis_size("cent")

    bits = bits_of("dp")
    orders = (bits, [bits[1], bits[0]] + bits[2:])
    place = jnp.full((1,), lax.axis_index("dp"), jnp.int32)
    ups = [place >> bit & 1 for bit in bits]
    ups = [up == 1 for up in ups]
    odd = jnp.full((1,), lax.axis_index("cent"), jnp.int32) & 1 == 1
    ups, odd, embeddings, centroids = lax.optimization_barrier((ups, odd, embeddings, centroids))

    def chosen(bit, yes, no):
        return jnp.where(ups[bit].reshape((1,) * yes.ndim), yes, no)

    def sent_and_kept(value):
        quarters = jnp.split(value, 4)
        lows, highs = quarters[0::2], quarters[1::2]
        sent = [chosen(order[0], low, high) for order, low, high in zip(orders, lows, highs)]
        kept = [chosen(order[0], high, low) for order, low, high in zip(orders, lows, highs)]
        return jnp.concatenate(sent + kept)

    def aligned(value, mask):
        quarters = jnp.split(value, 4)
        for k, order in enumerate(orders):
            if mask >> order[0] & 1:
                quarters[k], quarters[2 + k] = quarters[2 + k], quarters[k]
        return jnp.concatenate(quarters)

    scores = lax.dot_general(
        sent_and_kept(centroids), embeddings, (((1,), (1,)), ((), ())), preferred_element_type=jnp.float32
    ) * (1.0 / math.sqrt(embeddings.shape[1]))
    col_now = sent_and_kept(col_start)
    for step_index in range(ITERS):
        shifted = scores + col_now[:, None]
        top = jnp.max(shifted, axis=0)
        part = top + jnp.log(jnp.sum(jnp.exp(shifted - top[None, :]), axis=0))
        row_now = -math.log(n_total) - lse_over_cent(part, odd)
        lifted = scores + row_now[None, :]
        top = jnp.max(lifted, axis=1)
        terms = jnp.exp(lifted - top[:, None])
        mass = jnp.sum(terms, axis=1)
        part = top + jnp.log(mass)
        if step_index < ITERS - 1:
            col_now = -math.log(k_total) - lse_over_dp(part, aligned)
    plan = terms.astype(jnp.bfloat16)
    new_centroids, row_out, whole = last_sum(plan, part, mass, row_now, embeddings, chosen, orders, aligned)
    return new_centroids, row_out, -math.log(k_total) - whole


def solution(mesh):
    specs = (P("dp", None), P("cent", None), P("cent"))
    return jax.shard_map(
        on_device,
        mesh=mesh,
        in_specs=specs,
        out_specs=(P("cent", None), P("dp"), P("cent")),
        check_vma=False,
    )
```

```python
import functools
import math

import jax
import jax.numpy as jnp
from jax import lax
from jax.experimental import pallas as pl
from jax.experimental.pallas import tpu as pltpu
from jax.sharding import PartitionSpec as P

ITERS = 3
CHUNKS = 2
LANES = 128
VMEM_BYTES = 24 * 2**20


def bits_of(axis):
    size = lax.axis_size(axis)
    assert size & (size - 1) == 0
    return list(range(size.bit_length() - 1))


def flipped(x, axis, mask):
    size = lax.axis_size(axis)
    return lax.ppermute(x, axis, [(k, k ^ mask) for k in range(size)])


def lse(first, second):
    top = jnp.maximum(first, second)
    return top + jnp.log(jnp.exp(first - top) + jnp.exp(second - top))


def lse_over_dp(x, aligned):
    bits = bits_of("dp")

    def partner(value, mask):
        return aligned(flipped(value, "dp", mask), mask)

    for masks in ([1 << bit for bit in bits[k:k + 2]] for k in range(0, len(bits), 2)):
        if len(masks) == 2:
            far = partner(x, masks[0] | masks[1])
            near = [partner(x, mask) for mask in reversed(masks)]
            x = lse(lax.optimization_barrier(lse(x, far)), lse(*near))
        else:
            x = lse(x, partner(x, masks[0]))
    return x


def lse_over_cent(x, odd):
    size = lax.axis_size("cent")
    near, middle, *rest = [1 << bit for bit in bits_of("cent")[1:]]

    def split(value, even_mask, odd_mask):
        return lax.ppermute(value, "cent", [(k, k ^ (odd_mask if k % 2 else even_mask)) for k in range(size)])

    x = lse(x, flipped(x, "cent", 1))
    second = split(x, near, middle)
    first = split(x, near, near | middle)
    x = jnp.where(odd, lse(second, first), lse(x, first))
    for mask in [1] + rest:
        x = lse(x, flipped(x, "cent", mask))
    return x


def column(values):
    lane = lax.broadcasted_iota(jnp.int32, (LANES, LANES), 1)
    diagonal = lane == lax.broadcasted_iota(jnp.int32, (LANES, LANES), 0)
    return jnp.sum(jnp.where(diagonal, values, 0.0), axis=1, keepdims=True)


def quarter_places(orders, quarter):
    ups = [lax.axis_index("dp") >> order[0] & 1 for order in orders]
    sent = [(2 * k + 1 - up) * quarter for k, up in enumerate(ups)]
    return sent + [(2 * k + up) * quarter for k, up in enumerate(ups)]


def place_kernel(chunk, orders, *refs):
    blocks, (out, sent) = refs[:4], refs[-2:]
    quarter, width = blocks[0].shape
    copies = []
    for k, start in enumerate(quarter_places(orders, quarter)):
        rows = pl.ds(pl.multiple_of(start, LANES), quarter)
        copies.append(pltpu.make_async_copy(blocks[k], out.at[rows, pl.ds(chunk * width, width)], sent.at[k]))
        copies[-1].start()
    for copy in copies:
        copy.wait()


def placed(chunk, orders, blocks, shape, so_far):
    vmem = pl.BlockSpec(memory_space=pltpu.VMEM)
    anywhere = pl.BlockSpec(memory_space=pl.ANY)
    return pl.pallas_call(
        functools.partial(place_kernel, chunk, orders),
        out_shape=jax.ShapeDtypeStruct(shape, blocks[0].dtype),
        in_specs=[vmem] * 4 + [anywhere] * len(so_far),
        out_specs=anywhere,
        scratch_shapes=[pltpu.SemaphoreType.DMA((4,))],
        input_output_aliases={4: 0} if so_far else {},
        compiler_params=pltpu.CompilerParams(vmem_limit_bytes=VMEM_BYTES),
    )(*blocks, *so_far)


def means_kernel(is_kept, plan, embeddings, mass, *rest):
    half = plan.shape[0] // 2
    quarter = half // 2
    sums = jnp.dot(plan[pl.ds(is_kept * half, half), :], embeddings[...], preferred_element_type=jnp.float32)
    if is_kept:
        weights, row, out, row_out = rest
        row_out[...] = row[...]
    else:
        out = None
    for block in range(half // LANES):
        factor = 1.0 / column(mass[pl.ds(is_kept * (half // LANES) + block, 1), :])
        if is_kept:
            factor = factor * column(weights[pl.ds(block, 1), :])
        rows = pl.ds(block * LANES % quarter, LANES)
        values = sums[block * LANES:(block + 1) * LANES] * factor
        half_index = block * LANES // quarter
        if is_kept:
            out[half_index, rows, :] = values
        else:
            width = rest[0].shape[1]
            for chunk in range(CHUNKS):
                target = rest[2 * chunk + half_index]
                target[rows, :] = values[:, chunk * width:(chunk + 1) * width].astype(target.dtype)


def means_of(is_kept, plan, embeddings, mass, *rest):
    count, rows_here = plan.shape
    depth = embeddings.shape[1]
    vmem = pl.BlockSpec(memory_space=pltpu.VMEM)
    if is_kept:
        out_shape = (
            jax.ShapeDtypeStruct((2, count // 4, depth), jnp.float32),
            jax.ShapeDtypeStruct((1, rows_here), jnp.float32),
        )
        out_specs = (vmem, pl.BlockSpec((1, rows_here), lambda: (0, 0)))
    else:
        out_shape = [jax.ShapeDtypeStruct((count // 4, depth // CHUNKS), jnp.bfloat16)] * (2 * CHUNKS)
        out_specs = [vmem] * (2 * CHUNKS)
    return pl.pallas_call(
        functools.partial(means_kernel, is_kept),
        out_shape=out_shape,
        in_specs=[vmem] * (3 + len(rest)),
        out_specs=out_specs,
        compiler_params=pltpu.CompilerParams(vmem_limit_bytes=VMEM_BYTES),
        cost_estimate=pl.CostEstimate(
            flops=count * rows_here * depth, bytes_accessed=2 * rows_here * depth, transcendentals=0
        ),
    )(plan, embeddings, mass.reshape(count // LANES, LANES), *rest)


def last_sum(plan, part, mass, row_now, embeddings, chosen, orders, aligned):
    quarter = part.shape[0] // 4
    first, second = orders[0][:2]
    partners = {bit: aligned(flipped(part, "dp", 1 << bit), 1 << bit) for bit in (first, second)}
    sent = means_of(0, plan, embeddings, mass)
    got = [flipped(sent[2 * chunk + k], "dp", 1 << order[0]) for chunk in range(CHUNKS) for k, order in enumerate(orders)]

    def kept_of(lower, upper):
        return jnp.concatenate([lower[2 * quarter:3 * quarter], upper[3 * quarter:]])

    pairs = lax.optimization_barrier([lse(partners[first], part), lse(partners[second], part)])
    pair = kept_of(*pairs)
    weights = jnp.exp(kept_of(part, part) - pair).reshape(2 * quarter // LANES, LANES)
    kept, row_out = means_of(1, plan, embeddings, mass, weights, row_now[None, :])
    weights = jnp.exp(kept_of(partners[first], partners[second]) - pair)

    def exchanged(mine, bit, own, other):
        mine = mine.astype(jnp.bfloat16)
        theirs = flipped(mine, "dp", 1 << bit).astype(jnp.float32)
        mine = mine.astype(jnp.float32)
        lower = chosen(bit, theirs, mine) * chosen(bit, other, own)
        upper = chosen(bit, mine, theirs) * chosen(bit, own, other)
        return (lower + upper).astype(jnp.bfloat16)

    def gathered(mine, order, own, other):
        if len(order) == 1:
            return exchanged(mine, order[0], own, other)
        bit = order[0]
        low, high = jnp.split(mine, 2, axis=0)
        got = flipped(chosen(bit, low, high).astype(jnp.bfloat16), "dp", 1 << bit).astype(jnp.float32)
        own, other = (chosen(bit, high, low) for low, high in (jnp.split(x, 2, axis=0) for x in (own, other)))
        ones = jnp.ones((own.shape[0], 1), jnp.float32)
        done = gathered(chosen(bit, high, low) * own + got * other, order[1:], ones, ones)
        theirs = flipped(done, "dp", 1 << bit)
        return jnp.concatenate([chosen(bit, theirs, done), chosen(bit, done, theirs)], axis=0)

    width = kept.shape[2] // CHUNKS
    shape = (part.shape[0], kept.shape[2])
    mines = []
    for chunk in range(CHUNKS):
        columns = slice(chunk * width, (chunk + 1) * width)
        if chunk > 0:
            mines, kept, weights = lax.optimization_barrier((mines, kept, weights))
        if chunk == 1:
            corner = flipped(lax.optimization_barrier((partners[first], mines))[0], "dp", 1 << second)
        for k in range(2):
            rows = slice(k * quarter, (k + 1) * quarter)
            mines.append(kept[k, :, columns] + got[2 * chunk + k].astype(jnp.float32) * weights[rows, None])

    pairs, partners, corner = lax.optimization_barrier((pairs, partners, corner, mines))[:3]
    corner = aligned(corner, 1 << second)
    whole = lse(pairs[0], lse(corner, partners[second]))
    for bit in orders[0][2:]:
        whole = lse(aligned(flipped(whole, "dp", 1 << bit), 1 << bit), whole)
    pair_other = kept_of(lse(partners[second], corner), lse(partners[first], corner))
    weights_own = jnp.exp(kept_of(*pairs) - kept_of(whole, whole))
    weights_other = jnp.exp(pair_other - kept_of(whole, whole))

    outs = []
    firsts = []
    for chunk in range(CHUNKS):
        dones = []
        for k, order in enumerate(orders):
            rows = slice(k * quarter, (k + 1) * quarter)
            dones.append(gathered(mines[2 * chunk + k], order[1:], weights_own[rows, None], weights_other[rows, None]))
        if chunk < CHUNKS - 1:
            dones, weights_own, weights_other = lax.optimization_barrier((dones, weights_own, weights_other))
        firsts = firsts or dones
        blocks = [flipped(done, "dp", 1 << order[0]) for done, order in zip(dones, orders)] + dones
        outs = [placed(chunk, orders, blocks, shape, outs)]
    whole = lax.optimization_barrier((whole, firsts[0]))[0]
    quarters = jnp.split(whole, 4)
    halves = []
    for k, order in enumerate(orders):
        sent, kept = quarters[k], quarters[2 + k]
        halves += [chosen(order[0], sent, kept), chosen(order[0], kept, sent)]
    return outs[0], row_out.reshape(row_now.shape), jnp.concatenate(halves)


def on_device(embeddings, centroids, col_start):
    rows_here = embeddings.shape[0]
    cent_here = centroids.shape[0]
    n_total = rows_here * lax.axis_size("dp")
    k_total = cent_here * lax.axis_size("cent")

    bits = bits_of("dp")
    orders = (bits, [bits[1], bits[0]] + bits[2:])
    place = jnp.full((1,), lax.axis_index("dp"), jnp.int32)
    ups = [place >> bit & 1 for bit in bits]
    ups = [up == 1 for up in ups]
    odd = jnp.full((1,), lax.axis_index("cent"), jnp.int32) & 1 == 1
    ups, odd, embeddings, centroids = lax.optimization_barrier((ups, odd, embeddings, centroids))

    def chosen(bit, yes, no):
        return jnp.where(ups[bit].reshape((1,) * yes.ndim), yes, no)

    def sent_and_kept(value):
        quarters = jnp.split(value, 4)
        lows, highs = quarters[0::2], quarters[1::2]
        sent = [chosen(order[0], low, high) for order, low, high in zip(orders, lows, highs)]
        kept = [chosen(order[0], high, low) for order, low, high in zip(orders, lows, highs)]
        return sent + kept

    def aligned(value, mask):
        quarters = jnp.split(value, 4)
        for k, order in enumerate(orders):
            if mask >> order[0] & 1:
                quarters[k], quarters[2 + k] = quarters[2 + k], quarters[k]
        return jnp.concatenate(quarters)

    ordered, col_start = lax.optimization_barrier((sent_and_kept(centroids), col_start))
    ordered = jnp.concatenate(ordered)
    scores = lax.dot_general(
        ordered, embeddings, (((1,), (1,)), ((), ())), preferred_element_type=jnp.float32
    ) * (1.0 / math.sqrt(embeddings.shape[1]))
    col_now = jnp.concatenate(sent_and_kept(col_start))
    for step_index in range(ITERS):
        shifted = scores + col_now[:, None]
        top = jnp.max(shifted, axis=0)
        part = top + jnp.log(jnp.sum(jnp.exp(shifted - top[None, :]), axis=0))
        row_now = -math.log(n_total) - lse_over_cent(part, odd)
        lifted = scores + row_now[None, :]
        top = jnp.max(lifted, axis=1)
        terms = jnp.exp(lifted - top[:, None])
        mass = jnp.sum(terms, axis=1)
        part = top + jnp.log(mass)
        if step_index < ITERS - 1:
            col_now = -math.log(k_total) - lse_over_dp(part, aligned)
    plan = terms.astype(jnp.bfloat16)
    new_centroids, row_out, whole = last_sum(plan, part, mass, row_now, embeddings, chosen, orders, aligned)
    return new_centroids, row_out, -math.log(k_total) - whole


def solution(mesh):
    specs = (P("dp", None), P("cent", None), P("cent"))
    return jax.shard_map(
        on_device,
        mesh=mesh,
        in_specs=specs,
        out_specs=(P("cent", None), P("dp"), P("cent")),
        check_vma=False,
    )
```

```python
import functools
import math

import jax
import jax.numpy as jnp
from jax import lax
from jax.experimental import pallas as pl
from jax.experimental.pallas import tpu as pltpu
from jax.sharding import PartitionSpec as P

ITERS = 3
CHUNKS = 2
LANES = 128
VMEM_BYTES = 24 * 2**20


def bits_of(axis):
    size = lax.axis_size(axis)
    assert size & (size - 1) == 0
    return list(range(size.bit_length() - 1))


def flipped(x, axis, mask):
    size = lax.axis_size(axis)
    return lax.ppermute(x, axis, [(k, k ^ mask) for k in range(size)])


def lse(first, second):
    top = jnp.maximum(first, second)
    return top + jnp.log(jnp.exp(first - top) + jnp.exp(second - top))


def lse_over_dp(x, aligned):
    bits = bits_of("dp")

    def partner(value, mask):
        return aligned(flipped(value, "dp", mask), mask)

    for masks in ([1 << bit for bit in bits[k:k + 2]] for k in range(0, len(bits), 2)):
        if len(masks) == 2:
            far = partner(x, masks[0] | masks[1])
            near = [partner(x, mask) for mask in reversed(masks)]
            x = lse(lax.optimization_barrier(lse(x, far)), lse(*near))
        else:
            x = lse(x, partner(x, masks[0]))
    return x


def lse_over_cent(x, odd):
    size = lax.axis_size("cent")
    near, middle, *rest = [1 << bit for bit in bits_of("cent")[1:]]

    def split(value, even_mask, odd_mask):
        return lax.ppermute(value, "cent", [(k, k ^ (odd_mask if k % 2 else even_mask)) for k in range(size)])

    x = lse(x, flipped(x, "cent", 1))
    second = split(x, near, middle)
    first = split(x, near, near | middle)
    x = jnp.where(odd, lse(second, first), lse(x, first))
    for mask in [1] + rest:
        x = lse(x, flipped(x, "cent", mask))
    return x


def column(values):
    lane = lax.broadcasted_iota(jnp.int32, (LANES, LANES), 1)
    diagonal = lane == lax.broadcasted_iota(jnp.int32, (LANES, LANES), 0)
    return jnp.sum(jnp.where(diagonal, values, 0.0), axis=1, keepdims=True)


def quarter_places(orders, quarter):
    ups = [lax.axis_index("dp") >> order[0] & 1 for order in orders]
    sent = [(2 * k + 1 - up) * quarter for k, up in enumerate(ups)]
    return sent + [(2 * k + up) * quarter for k, up in enumerate(ups)]


def place_kernel(chunk, orders, *refs):
    blocks, (out, sent) = refs[:4], refs[-2:]
    quarter, width = blocks[0].shape
    copies = []
    for k, start in enumerate(quarter_places(orders, quarter)):
        rows = pl.ds(pl.multiple_of(start, LANES), quarter)
        copies.append(pltpu.make_async_copy(blocks[k], out.at[rows, pl.ds(chunk * width, width)], sent.at[k]))
        copies[-1].start()
    for copy in copies:
        copy.wait()


def placed(chunk, orders, blocks, shape, so_far):
    vmem = pl.BlockSpec(memory_space=pltpu.VMEM)
    anywhere = pl.BlockSpec(memory_space=pl.ANY)
    return pl.pallas_call(
        functools.partial(place_kernel, chunk, orders),
        out_shape=jax.ShapeDtypeStruct(shape, blocks[0].dtype),
        in_specs=[vmem] * 4 + [anywhere] * len(so_far),
        out_specs=anywhere,
        scratch_shapes=[pltpu.SemaphoreType.DMA((4,))],
        input_output_aliases={4: 0} if so_far else {},
        compiler_params=pltpu.CompilerParams(vmem_limit_bytes=VMEM_BYTES),
    )(*blocks, *so_far)


def scaled(sums, factors, target, half_index=None):
    for block in range(sums.shape[0] // LANES):
        rows = pl.ds(block * LANES, LANES)
        values = (sums[block * LANES:(block + 1) * LANES] * factors[block]).astype(target.dtype)
        if half_index is None:
            target[rows, :] = values
        else:
            target[half_index, rows, :] = values


def means_kernel(is_kept, plan, embeddings, mass, *rest):
    half = plan.shape[0] // 2
    quarter = half // 2
    width = embeddings.shape[1] // CHUNKS
    lines = half // LANES
    per_quarter = lines // 2
    inverse = [1.0 / column(mass[pl.ds(k, 1), :]) for k in range(2 * lines)]
    if is_kept:
        weights, row, kept, row_out, *sent = rest
        row_out[...] = row[...]
    else:
        sent = rest
    for chunk in range(1, CHUNKS) if is_kept else range(1):
        columns = pl.ds(chunk * width, width)
        sums = jnp.dot(plan[pl.ds(0, half), :], embeddings[:, columns], preferred_element_type=jnp.float32)
        for k in range(2):
            target = sent[2 * (chunk - is_kept) + k]
            scaled(sums[k * quarter:(k + 1) * quarter], inverse[k * per_quarter:(k + 1) * per_quarter], target)
    if is_kept:
        sums = jnp.dot(plan[pl.ds(half, half), :], embeddings[...], preferred_element_type=jnp.float32)
        factors = [inverse[lines + k] * column(weights[pl.ds(k, 1), :]) for k in range(lines)]
        for k in range(2):
            scaled(sums[k * quarter:(k + 1) * quarter], factors[k * per_quarter:(k + 1) * per_quarter], kept, k)


def means_of(is_kept, plan, embeddings, mass, *rest):
    count, rows_here = plan.shape
    depth = embeddings.shape[1]
    vmem = pl.BlockSpec(memory_space=pltpu.VMEM)
    sent = [jax.ShapeDtypeStruct((count // 4, depth // CHUNKS), jnp.bfloat16)] * 2
    if is_kept:
        sent = sent * (CHUNKS - 1)
        kept = jax.ShapeDtypeStruct((2, count // 4, depth), jnp.float32)
        row_out = jax.ShapeDtypeStruct((1, rows_here), jnp.float32)
        out_shape = [kept, row_out] + sent
        out_specs = [vmem, pl.BlockSpec((1, rows_here), lambda: (0, 0))] + [vmem] * len(sent)
    else:
        out_shape, out_specs = sent, [vmem] * 2
    return pl.pallas_call(
        functools.partial(means_kernel, is_kept),
        out_shape=out_shape,
        in_specs=[vmem] * (3 + len(rest)),
        out_specs=out_specs,
        compiler_params=pltpu.CompilerParams(vmem_limit_bytes=VMEM_BYTES),
        cost_estimate=pl.CostEstimate(
            flops=count * rows_here * depth, bytes_accessed=2 * rows_here * depth, transcendentals=0
        ),
    )(plan, embeddings, mass.reshape(count // LANES, LANES), *rest)


def last_sum(plan, part, mass, row_now, embeddings, chosen, orders, aligned):
    quarter = part.shape[0] // 4
    first, second = orders[0][:2]
    partners = {bit: aligned(flipped(part, "dp", 1 << bit), 1 << bit) for bit in (first, second)}
    sent = means_of(0, plan, embeddings, mass)
    got = [flipped(sent[k], "dp", 1 << order[0]) for k, order in enumerate(orders)]

    def kept_of(lower, upper):
        return jnp.concatenate([lower[2 * quarter:3 * quarter], upper[3 * quarter:]])

    pairs = lax.optimization_barrier([lse(partners[first], part), lse(partners[second], part)])
    pair = kept_of(*pairs)
    weights = jnp.exp(kept_of(part, part) - pair).reshape(2 * quarter // LANES, LANES)
    kept, row_out, *sent = means_of(1, plan, embeddings, mass, weights, row_now[None, :])
    got += [flipped(sent[k], "dp", 1 << orders[k % 2][0]) for k in range(len(sent))]
    weights = jnp.exp(kept_of(partners[first], partners[second]) - pair)

    corner = flipped(partners[first], "dp", 1 << second)

    def exchanged(mine, bit, own, other):
        mine = mine.astype(jnp.bfloat16)
        theirs = flipped(mine, "dp", 1 << bit).astype(jnp.float32)
        mine = mine.astype(jnp.float32)
        lower = chosen(bit, theirs, mine) * chosen(bit, other, own)
        upper = chosen(bit, mine, theirs) * chosen(bit, own, other)
        return (lower + upper).astype(jnp.bfloat16)

    def gathered(mine, order, own, other):
        if len(order) == 1:
            return exchanged(mine, order[0], own, other)
        bit = order[0]
        low, high = jnp.split(mine, 2, axis=0)
        got = flipped(chosen(bit, low, high).astype(jnp.bfloat16), "dp", 1 << bit).astype(jnp.float32)
        own, other = (chosen(bit, high, low) for low, high in (jnp.split(x, 2, axis=0) for x in (own, other)))
        ones = jnp.ones((own.shape[0], 1), jnp.float32)
        done = gathered(chosen(bit, high, low) * own + got * other, order[1:], ones, ones)
        theirs = flipped(done, "dp", 1 << bit)
        return jnp.concatenate([chosen(bit, theirs, done), chosen(bit, done, theirs)], axis=0)

    width = kept.shape[2] // CHUNKS
    shape = (part.shape[0], kept.shape[2])
    mines = []
    for chunk in range(CHUNKS):
        columns = slice(chunk * width, (chunk + 1) * width)
        if chunk > 0:
            mines, kept, weights = lax.optimization_barrier((mines, kept, weights))
        for k in range(2):
            rows = slice(k * quarter, (k + 1) * quarter)
            mines.append(kept[k, :, columns] + got[2 * chunk + k].astype(jnp.float32) * weights[rows, None])

    pairs, partners, corner = lax.optimization_barrier((pairs, partners, corner, mines))[:3]
    corner = aligned(corner, 1 << second)
    whole = lse(pairs[0], lse(corner, partners[second]))
    for bit in orders[0][2:]:
        whole = lse(aligned(flipped(whole, "dp", 1 << bit), 1 << bit), whole)
    pair_other = kept_of(lse(partners[second], corner), lse(partners[first], corner))
    weights_own = jnp.exp(kept_of(*pairs) - kept_of(whole, whole))
    weights_other = jnp.exp(pair_other - kept_of(whole, whole))

    outs = []
    firsts = []
    for chunk in range(CHUNKS):
        dones = []
        for k, order in enumerate(orders):
            rows = slice(k * quarter, (k + 1) * quarter)
            dones.append(gathered(mines[2 * chunk + k], order[1:], weights_own[rows, None], weights_other[rows, None]))
        if chunk < CHUNKS - 1:
            dones, weights_own, weights_other = lax.optimization_barrier((dones, weights_own, weights_other))
        firsts = firsts or dones
        blocks = [flipped(done, "dp", 1 << order[0]) for done, order in zip(dones, orders)] + dones
        outs = [placed(chunk, orders, blocks, shape, outs)]
    whole = lax.optimization_barrier((whole, firsts[0]))[0]
    quarters = jnp.split(whole, 4)
    halves = []
    for k, order in enumerate(orders):
        sent, kept = quarters[k], quarters[2 + k]
        halves += [chosen(order[0], sent, kept), chosen(order[0], kept, sent)]
    return outs[0], row_out.reshape(row_now.shape), jnp.concatenate(halves)


def on_device(embeddings, centroids, col_start):
    rows_here = embeddings.shape[0]
    cent_here = centroids.shape[0]
    n_total = rows_here * lax.axis_size("dp")
    k_total = cent_here * lax.axis_size("cent")

    bits = bits_of("dp")
    orders = (bits, [bits[1], bits[0]] + bits[2:])
    place = jnp.full((1,), lax.axis_index("dp"), jnp.int32)
    ups = [place >> bit & 1 for bit in bits]
    ups = [up == 1 for up in ups]
    odd = jnp.full((1,), lax.axis_index("cent"), jnp.int32) & 1 == 1
    ups, odd, embeddings, centroids = lax.optimization_barrier((ups, odd, embeddings, centroids))

    def chosen(bit, yes, no):
        return jnp.where(ups[bit].reshape((1,) * yes.ndim), yes, no)

    def sent_and_kept(value):
        quarters = jnp.split(value, 4)
        lows, highs = quarters[0::2], quarters[1::2]
        sent = [chosen(order[0], low, high) for order, low, high in zip(orders, lows, highs)]
        kept = [chosen(order[0], high, low) for order, low, high in zip(orders, lows, highs)]
        return jnp.concatenate(sent + kept)

    def aligned(value, mask):
        quarters = jnp.split(value, 4)
        for k, order in enumerate(orders):
            if mask >> order[0] & 1:
                quarters[k], quarters[2 + k] = quarters[2 + k], quarters[k]
        return jnp.concatenate(quarters)

    scores = lax.dot_general(
        sent_and_kept(centroids), embeddings, (((1,), (1,)), ((), ())), preferred_element_type=jnp.float32
    ) * (1.0 / math.sqrt(embeddings.shape[1]))
    col_now = sent_and_kept(col_start)
    for step_index in range(ITERS):
        shifted = scores + col_now[:, None]
        top = jnp.max(shifted, axis=0)
        part = top + jnp.log(jnp.sum(jnp.exp(shifted - top[None, :]), axis=0))
        row_now = -math.log(n_total) - lse_over_cent(part, odd)
        lifted = scores + row_now[None, :]
        top = jnp.max(lifted, axis=1)
        terms = jnp.exp(lifted - top[:, None])
        mass = jnp.sum(terms, axis=1)
        part = top + jnp.log(mass)
        if step_index < ITERS - 1:
            col_now = -math.log(k_total) - lse_over_dp(part, aligned)
    plan = terms.astype(jnp.bfloat16)
    new_centroids, row_out, whole = last_sum(plan, part, mass, row_now, embeddings, chosen, orders, aligned)
    return new_centroids, row_out, -math.log(k_total) - whole


def solution(mesh):
    specs = (P("dp", None), P("cent", None), P("cent"))
    return jax.shard_map(
        on_device,
        mesh=mesh,
        in_specs=specs,
        out_specs=(P("cent", None), P("dp"), P("cent")),
        check_vma=False,
    )
```

```python
import functools
import math

import jax
import jax.numpy as jnp
from jax import lax
from jax.experimental import pallas as pl
from jax.experimental.pallas import tpu as pltpu
from jax.sharding import PartitionSpec as P

ITERS = 3
CHUNKS = 2
LANES = 128
EXTRA = 16
VMEM_BYTES = 24 * 2**20


def bits_of(axis):
    size = lax.axis_size(axis)
    assert size & (size - 1) == 0
    return list(range(size.bit_length() - 1))


def flipped(x, axis, mask):
    size = lax.axis_size(axis)
    return lax.ppermute(x, axis, [(k, k ^ mask) for k in range(size)])


def lse(first, second):
    top = jnp.maximum(first, second)
    return top + jnp.log(jnp.exp(first - top) + jnp.exp(second - top))


def lse_over_dp(x, aligned):
    bits = bits_of("dp")

    def partner(value, mask):
        return aligned(flipped(value, "dp", mask), mask)

    for masks in ([1 << bit for bit in bits[k:k + 2]] for k in range(0, len(bits), 2)):
        if len(masks) == 2:
            far = partner(x, masks[0] | masks[1])
            near = [partner(x, mask) for mask in reversed(masks)]
            x = lse(lax.optimization_barrier(lse(x, far)), lse(*near))
        else:
            x = lse(x, partner(x, masks[0]))
    return x


def lse_over_cent(x, odd):
    size = lax.axis_size("cent")
    near, middle, *rest = [1 << bit for bit in bits_of("cent")[1:]]

    def split(value, even_mask, odd_mask):
        return lax.ppermute(value, "cent", [(k, k ^ (odd_mask if k % 2 else even_mask)) for k in range(size)])

    x = lse(x, flipped(x, "cent", 1))
    second = split(x, near, middle)
    first = split(x, near, near | middle)
    x = jnp.where(odd, lse(second, first), lse(x, first))
    for mask in [1] + rest:
        x = lse(x, flipped(x, "cent", mask))
    return x


def column(values):
    lane = lax.broadcasted_iota(jnp.int32, (LANES, LANES), 1)
    diagonal = lane == lax.broadcasted_iota(jnp.int32, (LANES, LANES), 0)
    return jnp.sum(jnp.where(diagonal, values, 0.0), axis=1, keepdims=True)


def quarter_places(orders, quarter):
    ups = [lax.axis_index("dp") >> order[0] & 1 for order in orders]
    sent = [(2 * k + 1 - up) * quarter for k, up in enumerate(ups)]
    return sent + [(2 * k + up) * quarter for k, up in enumerate(ups)]


def place_kernel(chunk, orders, *refs):
    blocks, (out, sent) = refs[:4], refs[-2:]
    quarter, width = blocks[0].shape
    copies = []
    for k, start in enumerate(quarter_places(orders, quarter)):
        rows = pl.ds(pl.multiple_of(start, LANES), quarter)
        copies.append(pltpu.make_async_copy(blocks[k], out.at[rows, pl.ds(chunk * width, width)], sent.at[k]))
        copies[-1].start()
    for copy in copies:
        copy.wait()


def placed(chunk, orders, blocks, shape, so_far):
    vmem = pl.BlockSpec(memory_space=pltpu.VMEM)
    anywhere = pl.BlockSpec(memory_space=pl.ANY)
    return pl.pallas_call(
        functools.partial(place_kernel, chunk, orders),
        out_shape=jax.ShapeDtypeStruct(shape, blocks[0].dtype),
        in_specs=[vmem] * 4 + [anywhere] * len(so_far),
        out_specs=anywhere,
        scratch_shapes=[pltpu.SemaphoreType.DMA((4,))],
        input_output_aliases={4: 0} if so_far else {},
        compiler_params=pltpu.CompilerParams(vmem_limit_bytes=VMEM_BYTES),
    )(*blocks, *so_far)


def means_kernel(is_kept, plan, embeddings, mass, *rest):
    half = plan.shape[0] // 2
    quarter = half // 2
    sums = jnp.dot(plan[pl.ds(is_kept * half, half), :], embeddings[...], preferred_element_type=jnp.float32)
    if is_kept:
        weights, row, out, row_out = rest
        row_out[...] = row[...]
    else:
        out = None
    for block in range(half // LANES):
        factor = 1.0 / column(mass[pl.ds(is_kept * (half // LANES) + block, 1), :])
        if is_kept:
            factor = factor * column(weights[pl.ds(block, 1), :])
        rows = pl.ds(block * LANES % quarter, LANES)
        values = sums[block * LANES:(block + 1) * LANES] * factor
        half_index = block * LANES // quarter
        if is_kept:
            out[half_index, rows, :] = values
        else:
            width = rest[0].shape[1]
            for chunk in range(CHUNKS):
                target = rest[2 * chunk + half_index]
                target[rows, :] = values[:, chunk * width:(chunk + 1) * width].astype(target.dtype)


def means_of(is_kept, plan, embeddings, mass, *rest):
    count, rows_here = plan.shape
    depth = embeddings.shape[1]
    vmem = pl.BlockSpec(memory_space=pltpu.VMEM)
    if is_kept:
        out_shape = (
            jax.ShapeDtypeStruct((2, count // 4, depth), jnp.float32),
            jax.ShapeDtypeStruct((1, rows_here), jnp.float32),
        )
        out_specs = (vmem, pl.BlockSpec((1, rows_here), lambda: (0, 0)))
    else:
        out_shape = [jax.ShapeDtypeStruct((count // 4, depth // CHUNKS), jnp.bfloat16)] * (2 * CHUNKS)
        out_specs = [vmem] * (2 * CHUNKS)
    return pl.pallas_call(
        functools.partial(means_kernel, is_kept),
        out_shape=out_shape,
        in_specs=[vmem] * (3 + len(rest)),
        out_specs=out_specs,
        compiler_params=pltpu.CompilerParams(vmem_limit_bytes=VMEM_BYTES),
        cost_estimate=pl.CostEstimate(
            flops=count * rows_here * depth, bytes_accessed=2 * rows_here * depth, transcendentals=0
        ),
    )(plan, embeddings, mass.reshape(count // LANES, LANES), *rest)


def last_sum_by_vectors(plan, part, mass, row_now, embeddings, chosen, orders, aligned):
    quarter = part.shape[0] // 4
    first, second = orders[0][:2]
    partners = {bit: aligned(flipped(part, "dp", 1 << bit), 1 << bit) for bit in (first, second)}
    sent = means_of(0, plan, embeddings, mass)
    got = [flipped(sent[2 * chunk + k], "dp", 1 << order[0]) for chunk in range(CHUNKS) for k, order in enumerate(orders)]

    def kept_of(lower, upper):
        return jnp.concatenate([lower[2 * quarter:3 * quarter], upper[3 * quarter:]])

    pairs = lax.optimization_barrier([lse(partners[first], part), lse(partners[second], part)])
    pair = kept_of(*pairs)
    weights = jnp.exp(kept_of(part, part) - pair).reshape(2 * quarter // LANES, LANES)
    kept, row_out = means_of(1, plan, embeddings, mass, weights, row_now[None, :])
    weights = jnp.exp(kept_of(partners[first], partners[second]) - pair)

    corner = flipped(partners[first], "dp", 1 << second)

    def exchanged(mine, bit, own, other):
        mine = mine.astype(jnp.bfloat16)
        theirs = flipped(mine, "dp", 1 << bit).astype(jnp.float32)
        mine = mine.astype(jnp.float32)
        lower = chosen(bit, theirs, mine) * chosen(bit, other, own)
        upper = chosen(bit, mine, theirs) * chosen(bit, own, other)
        return (lower + upper).astype(jnp.bfloat16)

    def gathered(mine, order, own, other):
        if len(order) == 1:
            return exchanged(mine, order[0], own, other)
        bit = order[0]
        low, high = jnp.split(mine, 2, axis=0)
        got = flipped(chosen(bit, low, high).astype(jnp.bfloat16), "dp", 1 << bit).astype(jnp.float32)
        own, other = (chosen(bit, high, low) for low, high in (jnp.split(x, 2, axis=0) for x in (own, other)))
        ones = jnp.ones((own.shape[0], 1), jnp.float32)
        done = gathered(chosen(bit, high, low) * own + got * other, order[1:], ones, ones)
        theirs = flipped(done, "dp", 1 << bit)
        return jnp.concatenate([chosen(bit, theirs, done), chosen(bit, done, theirs)], axis=0)

    width = kept.shape[2] // CHUNKS
    shape = (part.shape[0], kept.shape[2])
    mines = []
    for chunk in range(CHUNKS):
        columns = slice(chunk * width, (chunk + 1) * width)
        if chunk > 0:
            mines, kept, weights = lax.optimization_barrier((mines, kept, weights))
        for k in range(2):
            rows = slice(k * quarter, (k + 1) * quarter)
            mines.append(kept[k, :, columns] + got[2 * chunk + k].astype(jnp.float32) * weights[rows, None])

    pairs, partners, corner = lax.optimization_barrier((pairs, partners, corner, mines))[:3]
    corner = aligned(corner, 1 << second)
    whole = lse(pairs[0], lse(corner, partners[second]))
    for bit in orders[0][2:]:
        whole = lse(aligned(flipped(whole, "dp", 1 << bit), 1 << bit), whole)
    pair_other = kept_of(lse(partners[second], corner), lse(partners[first], corner))
    weights_own = jnp.exp(kept_of(*pairs) - kept_of(whole, whole))
    weights_other = jnp.exp(pair_other - kept_of(whole, whole))

    outs = []
    firsts = []
    for chunk in range(CHUNKS):
        dones = []
        for k, order in enumerate(orders):
            rows = slice(k * quarter, (k + 1) * quarter)
            dones.append(gathered(mines[2 * chunk + k], order[1:], weights_own[rows, None], weights_other[rows, None]))
        if chunk < CHUNKS - 1:
            dones, weights_own, weights_other = lax.optimization_barrier((dones, weights_own, weights_other))
        firsts = firsts or dones
        blocks = [flipped(done, "dp", 1 << order[0]) for done, order in zip(dones, orders)] + dones
        outs = [placed(chunk, orders, blocks, shape, outs)]
    whole = lax.optimization_barrier((whole, firsts[0]))[0]
    quarters = jnp.split(whole, 4)
    halves = []
    for k, order in enumerate(orders):
        sent, kept = quarters[k], quarters[2 + k]
        halves += [chosen(order[0], sent, kept), chosen(order[0], kept, sent)]
    return outs[0], row_out.reshape(row_now.shape), jnp.concatenate(halves)


def parts_of(lines):
    row = lax.broadcasted_iota(jnp.int32, (EXTRA, LANES), 0)
    rows = jnp.zeros((EXTRA, LANES), jnp.float32)
    for index, line in enumerate(lines):
        for part in range(3):
            rounded = line.astype(jnp.bfloat16).astype(jnp.float32)
            rows = jnp.where(row == 3 * index + part, rounded, rows)
            line = line - rounded
    return rows.astype(jnp.bfloat16)


def lines_of(message, count):
    rows = message[pl.ds(message.shape[0] - EXTRA, EXTRA), pl.ds(0, LANES)].astype(jnp.float32)
    return [(rows[k:k + 1] + rows[k + 1:k + 2]) + rows[k + 2:k + 3] for k in range(0, 3 * count, 3)]


def put(message, values, lines):
    quarter, width = values.shape
    message[pl.ds(0, quarter), :] = values.astype(message.dtype)
    if lines:
        message[pl.ds(quarter, EXTRA), pl.ds(0, LANES)] = parts_of(lines)
        message[pl.ds(quarter, EXTRA), pl.ds(LANES, width - LANES)] = jnp.zeros((EXTRA, width - LANES), message.dtype)


def columns_of(lines):
    return jnp.concatenate([column(line) for line in lines], axis=0)


def read(ref, start, count):
    return [ref[pl.ds(start + k, 1), :] for k in range(count)]


def write(ref, start, lines):
    for k, line in enumerate(lines):
        ref[pl.ds(start + k, 1), :] = line


def joined(first, second):
    whole = [lse(a, b) for a, b in zip(first, second)]
    return whole, [jnp.exp(a - b) for a, b in zip(first, whole)], [jnp.exp(a - b) for a, b in zip(second, whole)]


def sent_kernel(plan, embeddings, mass, part, *sent):
    quarter = plan.shape[0] // 4
    count = quarter // LANES
    width = embeddings.shape[1] // CHUNKS
    sums = jnp.dot(plan[pl.ds(0, 2 * quarter), :], embeddings[...], preferred_element_type=jnp.float32)
    for k in range(2):
        values = sums[k * quarter:(k + 1) * quarter] / columns_of(read(mass, k * count, count))
        for chunk in range(CHUNKS):
            lines = read(part, k * count, count) if chunk == 0 else []
            put(sent[2 * chunk + k], values[:, chunk * width:(chunk + 1) * width], lines)


def kept_kernel(plan, embeddings, mass, row, kept, row_out):
    quarter = plan.shape[0] // 4
    count = quarter // LANES
    row_out[...] = row[...]
    sums = jnp.dot(plan[pl.ds(2 * quarter, 2 * quarter), :], embeddings[...], preferred_element_type=jnp.float32)
    for k in range(2):
        kept[k] = sums[k * quarter:(k + 1) * quarter] / columns_of(read(mass, (2 + k) * count, count))


def pair_kernel(chunk, kept, lower, upper, known, out_lower, out_upper, *weights_out):
    quarter = kept.shape[1]
    count = quarter // LANES
    for k, (got, out) in enumerate(((lower, out_lower), (upper, out_upper))):
        if chunk == 0:
            pair, own, other = joined(read(known, (2 + k) * count, count), lines_of(got, count))
            write(weights_out[0], 2 * k * count, own + other)
        else:
            pair = []
            own, other = read(known, 2 * k * count, count), read(known, (2 * k + 1) * count, count)
        width = got.shape[1]
        values = kept[k, :, pl.ds(chunk * width, width)] * columns_of(own)
        put(out, values + got[pl.ds(0, quarter), :].astype(jnp.float32) * columns_of(other), pair)


def whole_kernel(chunk, bit, quarter, mine, theirs, *rest):
    count = quarter // LANES
    up = lax.axis_index("dp") >> bit & 1 == 1
    if chunk == 0:
        out, weights_out = rest
        own, other = lines_of(mine, count), lines_of(theirs, count)
        lower = [jnp.where(up, b, a) for a, b in zip(own, other)]
        upper = [jnp.where(up, a, b) for a, b in zip(own, other)]
        whole, low, high = joined(lower, upper)
        write(weights_out, 0, low + high)
    else:
        known, out = rest
        whole = []
        low, high = read(known, 0, count), read(known, count, count)
    own, other = (ref[pl.ds(0, quarter), :].astype(jnp.float32) for ref in (mine, theirs))
    values = jnp.where(up, other, own) * columns_of(low) + jnp.where(up, own, other) * columns_of(high)
    put(out, values, whole)


def place_first_kernel(orders, log_k, lower_sent, upper_sent, lower_kept, upper_kept, out, col_out, sent):
    blocks = (lower_sent, upper_sent, lower_kept, upper_kept)
    quarter = blocks[0].shape[0] - EXTRA
    count = quarter // LANES
    copies = []
    for k, start in enumerate(quarter_places(orders, quarter)):
        rows = pl.ds(pl.multiple_of(start, LANES), quarter)
        source = blocks[k].at[pl.ds(0, quarter)]
        copies.append(pltpu.make_async_copy(source, out.at[rows, pl.ds(0, blocks[k].shape[1])], sent.at[k]))
        copies[-1].start()
    for block, start in zip(blocks, quarter_places(orders, count)):
        write(col_out, start, [-log_k - line for line in lines_of(block, count)])
    for copy in copies:
        copy.wait()


def last_sum(plan, part, mass, row_now, embeddings, log_k, orders):
    columns, rows_here = plan.shape
    depth = embeddings.shape[1]
    quarter = columns // 4
    width = depth // CHUNKS
    lines = quarter // LANES
    f32 = jnp.float32
    vmem = pl.BlockSpec(memory_space=pltpu.VMEM)

    def call(kernel, operands, outs, specs=None, flops=0, **options):
        return pl.pallas_call(
            kernel,
            out_shape=outs,
            in_specs=[vmem] * len(operands),
            out_specs=specs or [vmem] * len(outs),
            compiler_params=pltpu.CompilerParams(vmem_limit_bytes=VMEM_BYTES),
            cost_estimate=pl.CostEstimate(flops=flops, bytes_accessed=columns * depth, transcendentals=0),
            **options,
        )(*operands)

    def message(chunk):
        return jax.ShapeDtypeStruct((quarter + (EXTRA if chunk == 0 else 0), width), jnp.bfloat16)

    def table(count):
        return jax.ShapeDtypeStruct((count * lines, LANES), f32)

    mass, part = mass.reshape(table(4).shape), part.reshape(table(4).shape)
    flops = columns * rows_here * depth
    chunks = range(CHUNKS)
    sent = call(sent_kernel, [plan, embeddings, mass, part], [message(chunk) for chunk in chunks for _ in range(2)], flops=flops)
    got = [flipped(sent[2 * chunk + k], "dp", 1 << orders[k][0]) for chunk in chunks for k in range(2)]
    row = row_now[None, :]
    kept, row_out = call(
        kept_kernel,
        [plan, embeddings, mass, row],
        [jax.ShapeDtypeStruct((2, quarter, depth), f32), jax.ShapeDtypeStruct(row.shape, f32)],
        specs=[vmem, pl.BlockSpec(row.shape, lambda: (0, 0))],
        flops=flops,
    )
    pairs = []
    known = part
    for chunk in chunks:
        outs = [message(chunk)] * 2 + ([table(4)] if chunk == 0 else [])
        results = call(functools.partial(pair_kernel, chunk), [kept, got[2 * chunk], got[2 * chunk + 1], known], outs)
        both = results[:2]
        known = results[2] if chunk == 0 else known
        pairs += both
    known = [None, None]
    out = None
    for chunk in chunks:
        dones = []
        for k, order in enumerate(orders):
            mine = pairs[2 * chunk + k]
            theirs = flipped(mine, "dp", 1 << order[1])
            kernel = functools.partial(whole_kernel, chunk, order[1], quarter)
            if chunk == 0:
                done, known[k] = call(kernel, [mine, theirs], [message(chunk), table(2)])
            else:
                done, = call(kernel, [mine, theirs, known[k]], [message(chunk)])
            dones.append(done)
        blocks = [flipped(done, "dp", 1 << order[0]) for done, order in zip(dones, orders)] + dones
        if chunk == 0:
            out, col_out = call(
                functools.partial(place_first_kernel, orders, log_k),
                blocks,
                [jax.ShapeDtypeStruct((columns, depth), jnp.bfloat16), table(4)],
                specs=[pl.BlockSpec(memory_space=pl.ANY), pl.BlockSpec(table(4).shape, lambda: (0, 0))],
                scratch_shapes=[pltpu.SemaphoreType.DMA((4,))],
            )
        else:
            out = placed(chunk, orders, blocks, (columns, depth), [out])
    return out, row_out.reshape(row_now.shape), col_out.reshape(columns)


def on_device(embeddings, centroids, col_start):
    rows_here = embeddings.shape[0]
    cent_here = centroids.shape[0]
    n_total = rows_here * lax.axis_size("dp")
    k_total = cent_here * lax.axis_size("cent")

    bits = bits_of("dp")
    orders = (bits, [bits[1], bits[0]] + bits[2:])
    place = jnp.full((1,), lax.axis_index("dp"), jnp.int32)
    ups = [place >> bit & 1 for bit in bits]
    ups = [up == 1 for up in ups]
    odd = jnp.full((1,), lax.axis_index("cent"), jnp.int32) & 1 == 1
    ups, odd, embeddings, centroids = lax.optimization_barrier((ups, odd, embeddings, centroids))

    def chosen(bit, yes, no):
        return jnp.where(ups[bit].reshape((1,) * yes.ndim), yes, no)

    def sent_and_kept(value):
        quarters = jnp.split(value, 4)
        lows, highs = quarters[0::2], quarters[1::2]
        sent = [chosen(order[0], low, high) for order, low, high in zip(orders, lows, highs)]
        kept = [chosen(order[0], high, low) for order, low, high in zip(orders, lows, highs)]
        return jnp.concatenate(sent + kept)

    def aligned(value, mask):
        quarters = jnp.split(value, 4)
        for k, order in enumerate(orders):
            if mask >> order[0] & 1:
                quarters[k], quarters[2 + k] = quarters[2 + k], quarters[k]
        return jnp.concatenate(quarters)

    scores = lax.dot_general(
        sent_and_kept(centroids), embeddings, (((1,), (1,)), ((), ())), preferred_element_type=jnp.float32
    ) * (1.0 / math.sqrt(embeddings.shape[1]))
    col_now = sent_and_kept(col_start)
    for step_index in range(ITERS):
        shifted = scores + col_now[:, None]
        top = jnp.max(shifted, axis=0)
        part = top + jnp.log(jnp.sum(jnp.exp(shifted - top[None, :]), axis=0))
        row_now = -math.log(n_total) - lse_over_cent(part, odd)
        lifted = scores + row_now[None, :]
        top = jnp.max(lifted, axis=1)
        terms = jnp.exp(lifted - top[:, None])
        mass = jnp.sum(terms, axis=1)
        part = top + jnp.log(mass)
        if step_index < ITERS - 1:
            col_now = -math.log(k_total) - lse_over_dp(part, aligned)
    plan = terms.astype(jnp.bfloat16)
    if len(bits) == 2:
        return last_sum(plan, part, mass, row_now, embeddings, math.log(k_total), orders)
    new_centroids, row_out, whole = last_sum_by_vectors(plan, part, mass, row_now, embeddings, chosen, orders, aligned)
    return new_centroids, row_out, -math.log(k_total) - whole


def solution(mesh):
    specs = (P("dp", None), P("cent", None), P("cent"))
    return jax.shard_map(
        on_device,
        mesh=mesh,
        in_specs=specs,
        out_specs=(P("cent", None), P("dp"), P("cent")),
        check_vma=False,
    )
```

```python
import functools
import math

import jax
import jax.numpy as jnp
from jax import lax
from jax.experimental import pallas as pl
from jax.experimental.pallas import tpu as pltpu
from jax.sharding import PartitionSpec as P

ITERS = 3
CHUNKS = 2
LANES = 128
EXTRA = 16
VMEM_BYTES = 24 * 2**20


def bits_of(axis):
    size = lax.axis_size(axis)
    assert size & (size - 1) == 0
    return list(range(size.bit_length() - 1))


def flipped(x, axis, mask):
    size = lax.axis_size(axis)
    return lax.ppermute(x, axis, [(k, k ^ mask) for k in range(size)])


def lse(first, second):
    top = jnp.maximum(first, second)
    return top + jnp.log(jnp.exp(first - top) + jnp.exp(second - top))


def lse_over_dp(x, aligned):
    bits = bits_of("dp")

    def partner(value, mask):
        return aligned(flipped(value, "dp", mask), mask)

    for masks in ([1 << bit for bit in bits[k:k + 2]] for k in range(0, len(bits), 2)):
        if len(masks) == 2:
            far = partner(x, masks[0] | masks[1])
            near = [partner(x, mask) for mask in reversed(masks)]
            x = lse(lax.optimization_barrier(lse(x, far)), lse(*near))
        else:
            x = lse(x, partner(x, masks[0]))
    return x


def lse_over_cent(x, odd, joined_by):
    size = lax.axis_size("cent")
    near, middle, *rest = [1 << bit for bit in bits_of("cent")[1:]]

    def split(value, even_mask, odd_mask):
        return lax.ppermute(value, "cent", [(k, k ^ (odd_mask if k % 2 else even_mask)) for k in range(size)])

    x = lse(x, flipped(x, "cent", 1))
    second = split(x, near, middle)
    first = split(x, near, near | middle)
    x = joined_by(jnp.where(odd, lse(second, first), lse(x, first)))
    for mask in [1] + rest:
        x = lse(x, flipped(x, "cent", mask))
    return x


def column(values):
    lane = lax.broadcasted_iota(jnp.int32, (LANES, LANES), 1)
    diagonal = lane == lax.broadcasted_iota(jnp.int32, (LANES, LANES), 0)
    return jnp.sum(jnp.where(diagonal, values, 0.0), axis=1, keepdims=True)


def quarter_places(orders, quarter):
    ups = [lax.axis_index("dp") >> order[0] & 1 for order in orders]
    sent = [(2 * k + 1 - up) * quarter for k, up in enumerate(ups)]
    return sent + [(2 * k + up) * quarter for k, up in enumerate(ups)]


def place_kernel(chunk, orders, *refs):
    blocks, (out, sent) = refs[:4], refs[-2:]
    quarter, width = blocks[0].shape
    copies = []
    for k, start in enumerate(quarter_places(orders, quarter)):
        rows = pl.ds(pl.multiple_of(start, LANES), quarter)
        copies.append(pltpu.make_async_copy(blocks[k], out.at[rows, pl.ds(chunk * width, width)], sent.at[k]))
        copies[-1].start()
    for copy in copies:
        copy.wait()


def placed(chunk, orders, blocks, shape, so_far):
    vmem = pl.BlockSpec(memory_space=pltpu.VMEM)
    anywhere = pl.BlockSpec(memory_space=pl.ANY)
    return pl.pallas_call(
        functools.partial(place_kernel, chunk, orders),
        out_shape=jax.ShapeDtypeStruct(shape, blocks[0].dtype),
        in_specs=[vmem] * 4 + [anywhere] * len(so_far),
        out_specs=anywhere,
        scratch_shapes=[pltpu.SemaphoreType.DMA((4,))],
        input_output_aliases={4: 0} if so_far else {},
        compiler_params=pltpu.CompilerParams(vmem_limit_bytes=VMEM_BYTES),
    )(*blocks, *so_far)


def means_kernel(is_kept, plan, embeddings, mass, *rest):
    half = plan.shape[0] // 2
    quarter = half // 2
    sums = jnp.dot(plan[pl.ds(is_kept * half, half), :], embeddings[...], preferred_element_type=jnp.float32)
    if is_kept:
        weights, row, out, row_out = rest
        row_out[...] = row[...]
    else:
        out = None
    for block in range(half // LANES):
        factor = 1.0 / column(mass[pl.ds(is_kept * (half // LANES) + block, 1), :])
        if is_kept:
            factor = factor * column(weights[pl.ds(block, 1), :])
        rows = pl.ds(block * LANES % quarter, LANES)
        values = sums[block * LANES:(block + 1) * LANES] * factor
        half_index = block * LANES // quarter
        if is_kept:
            out[half_index, rows, :] = values
        else:
            width = rest[0].shape[1]
            for chunk in range(CHUNKS):
                target = rest[2 * chunk + half_index]
                target[rows, :] = values[:, chunk * width:(chunk + 1) * width].astype(target.dtype)


def means_of(is_kept, plan, embeddings, mass, *rest):
    count, rows_here = plan.shape
    depth = embeddings.shape[1]
    vmem = pl.BlockSpec(memory_space=pltpu.VMEM)
    if is_kept:
        out_shape = (
            jax.ShapeDtypeStruct((2, count // 4, depth), jnp.float32),
            jax.ShapeDtypeStruct((1, rows_here), jnp.float32),
        )
        out_specs = (vmem, pl.BlockSpec((1, rows_here), lambda: (0, 0)))
    else:
        out_shape = [jax.ShapeDtypeStruct((count // 4, depth // CHUNKS), jnp.bfloat16)] * (2 * CHUNKS)
        out_specs = [vmem] * (2 * CHUNKS)
    return pl.pallas_call(
        functools.partial(means_kernel, is_kept),
        out_shape=out_shape,
        in_specs=[vmem] * (3 + len(rest)),
        out_specs=out_specs,
        compiler_params=pltpu.CompilerParams(vmem_limit_bytes=VMEM_BYTES),
        cost_estimate=pl.CostEstimate(
            flops=count * rows_here * depth, bytes_accessed=2 * rows_here * depth, transcendentals=0
        ),
    )(plan, embeddings, mass.reshape(count // LANES, LANES), *rest)


def last_sum_by_vectors(plan, part, mass, row_now, embeddings, chosen, orders, aligned):
    quarter = part.shape[0] // 4
    first, second = orders[0][:2]
    partners = {bit: aligned(flipped(part, "dp", 1 << bit), 1 << bit) for bit in (first, second)}
    sent = means_of(0, plan, embeddings, mass)
    got = [flipped(sent[2 * chunk + k], "dp", 1 << order[0]) for chunk in range(CHUNKS) for k, order in enumerate(orders)]

    def kept_of(lower, upper):
        return jnp.concatenate([lower[2 * quarter:3 * quarter], upper[3 * quarter:]])

    pairs = lax.optimization_barrier([lse(partners[first], part), lse(partners[second], part)])
    pair = kept_of(*pairs)
    weights = jnp.exp(kept_of(part, part) - pair).reshape(2 * quarter // LANES, LANES)
    kept, row_out = means_of(1, plan, embeddings, mass, weights, row_now[None, :])
    weights = jnp.exp(kept_of(partners[first], partners[second]) - pair)

    corner = flipped(partners[first], "dp", 1 << second)

    def exchanged(mine, bit, own, other):
        mine = mine.astype(jnp.bfloat16)
        theirs = flipped(mine, "dp", 1 << bit).astype(jnp.float32)
        mine = mine.astype(jnp.float32)
        lower = chosen(bit, theirs, mine) * chosen(bit, other, own)
        upper = chosen(bit, mine, theirs) * chosen(bit, own, other)
        return (lower + upper).astype(jnp.bfloat16)

    def gathered(mine, order, own, other):
        if len(order) == 1:
            return exchanged(mine, order[0], own, other)
        bit = order[0]
        low, high = jnp.split(mine, 2, axis=0)
        got = flipped(chosen(bit, low, high).astype(jnp.bfloat16), "dp", 1 << bit).astype(jnp.float32)
        own, other = (chosen(bit, high, low) for low, high in (jnp.split(x, 2, axis=0) for x in (own, other)))
        ones = jnp.ones((own.shape[0], 1), jnp.float32)
        done = gathered(chosen(bit, high, low) * own + got * other, order[1:], ones, ones)
        theirs = flipped(done, "dp", 1 << bit)
        return jnp.concatenate([chosen(bit, theirs, done), chosen(bit, done, theirs)], axis=0)

    width = kept.shape[2] // CHUNKS
    shape = (part.shape[0], kept.shape[2])
    mines = []
    for chunk in range(CHUNKS):
        columns = slice(chunk * width, (chunk + 1) * width)
        if chunk > 0:
            mines, kept, weights = lax.optimization_barrier((mines, kept, weights))
        for k in range(2):
            rows = slice(k * quarter, (k + 1) * quarter)
            mines.append(kept[k, :, columns] + got[2 * chunk + k].astype(jnp.float32) * weights[rows, None])

    pairs, partners, corner = lax.optimization_barrier((pairs, partners, corner, mines))[:3]
    corner = aligned(corner, 1 << second)
    whole = lse(pairs[0], lse(corner, partners[second]))
    for bit in orders[0][2:]:
        whole = lse(aligned(flipped(whole, "dp", 1 << bit), 1 << bit), whole)
    pair_other = kept_of(lse(partners[second], corner), lse(partners[first], corner))
    weights_own = jnp.exp(kept_of(*pairs) - kept_of(whole, whole))
    weights_other = jnp.exp(pair_other - kept_of(whole, whole))

    outs = []
    firsts = []
    for chunk in range(CHUNKS):
        dones = []
        for k, order in enumerate(orders):
            rows = slice(k * quarter, (k + 1) * quarter)
            dones.append(gathered(mines[2 * chunk + k], order[1:], weights_own[rows, None], weights_other[rows, None]))
        if chunk < CHUNKS - 1:
            dones, weights_own, weights_other = lax.optimization_barrier((dones, weights_own, weights_other))
        firsts = firsts or dones
        blocks = [flipped(done, "dp", 1 << order[0]) for done, order in zip(dones, orders)] + dones
        outs = [placed(chunk, orders, blocks, shape, outs)]
    whole = lax.optimization_barrier((whole, firsts[0]))[0]
    quarters = jnp.split(whole, 4)
    halves = []
    for k, order in enumerate(orders):
        sent, kept = quarters[k], quarters[2 + k]
        halves += [chosen(order[0], sent, kept), chosen(order[0], kept, sent)]
    return outs[0], row_out.reshape(row_now.shape), jnp.concatenate(halves)


def parts_of(lines):
    row = lax.broadcasted_iota(jnp.int32, (EXTRA, LANES), 0)
    rows = jnp.zeros((EXTRA, LANES), jnp.float32)
    for index, line in enumerate(lines):
        for part in range(3):
            rounded = line.astype(jnp.bfloat16).astype(jnp.float32)
            rows = jnp.where(row == 3 * index + part, rounded, rows)
            line = line - rounded
    return rows.astype(jnp.bfloat16)


def lines_of(message, count):
    rows = message[pl.ds(message.shape[0] - EXTRA, EXTRA), pl.ds(0, LANES)].astype(jnp.float32)
    return [(rows[k:k + 1] + rows[k + 1:k + 2]) + rows[k + 2:k + 3] for k in range(0, 3 * count, 3)]


def put(message, values, lines):
    quarter, width = values.shape
    message[pl.ds(0, quarter), :] = values.astype(message.dtype)
    if lines:
        message[pl.ds(quarter, EXTRA), pl.ds(0, LANES)] = parts_of(lines)
        message[pl.ds(quarter, EXTRA), pl.ds(LANES, width - LANES)] = jnp.zeros((EXTRA, width - LANES), message.dtype)


def columns_of(lines):
    return jnp.concatenate([column(line) for line in lines], axis=0)


def read(ref, start, count):
    return [ref[pl.ds(start + k, 1), :] for k in range(count)]


def write(ref, start, lines):
    for k, line in enumerate(lines):
        ref[pl.ds(start + k, 1), :] = line


def joined(first, second):
    whole = [lse(a, b) for a, b in zip(first, second)]
    return whole, [jnp.exp(a - b) for a, b in zip(first, whole)], [jnp.exp(a - b) for a, b in zip(second, whole)]


def sent_kernel(plan, embeddings, mass, part, *sent):
    quarter = plan.shape[0] // 4
    count = quarter // LANES
    width = embeddings.shape[1] // CHUNKS
    sums = jnp.dot(plan[pl.ds(0, 2 * quarter), :], embeddings[...], preferred_element_type=jnp.float32)
    for k in range(2):
        values = sums[k * quarter:(k + 1) * quarter] / columns_of(read(mass, k * count, count))
        for chunk in range(CHUNKS):
            lines = read(part, k * count, count) if chunk == 0 else []
            put(sent[2 * chunk + k], values[:, chunk * width:(chunk + 1) * width], lines)


def kept_kernel(plan, embeddings, mass, row, kept, row_out):
    quarter = plan.shape[0] // 4
    count = quarter // LANES
    row_out[...] = row[...]
    sums = jnp.dot(plan[pl.ds(2 * quarter, 2 * quarter), :], embeddings[...], preferred_element_type=jnp.float32)
    for k in range(2):
        kept[k] = sums[k * quarter:(k + 1) * quarter] / columns_of(read(mass, (2 + k) * count, count))


def pair_kernel(chunk, kept, lower, upper, known, out_lower, out_upper, *weights_out):
    quarter = kept.shape[1]
    count = quarter // LANES
    for k, (got, out) in enumerate(((lower, out_lower), (upper, out_upper))):
        if chunk == 0:
            pair, own, other = joined(read(known, (2 + k) * count, count), lines_of(got, count))
            write(weights_out[0], 2 * k * count, own + other)
        else:
            pair = []
            own, other = read(known, 2 * k * count, count), read(known, (2 * k + 1) * count, count)
        width = got.shape[1]
        values = kept[k, :, pl.ds(chunk * width, width)] * columns_of(own)
        put(out, values + got[pl.ds(0, quarter), :].astype(jnp.float32) * columns_of(other), pair)


def whole_kernel(chunk, bit, quarter, mine, theirs, *rest):
    count = quarter // LANES
    up = lax.axis_index("dp") >> bit & 1 == 1
    if chunk == 0:
        out, weights_out = rest
        own, other = lines_of(mine, count), lines_of(theirs, count)
        lower = [jnp.where(up, b, a) for a, b in zip(own, other)]
        upper = [jnp.where(up, a, b) for a, b in zip(own, other)]
        whole, low, high = joined(lower, upper)
        write(weights_out, 0, low + high)
    else:
        known, out = rest
        whole = []
        low, high = read(known, 0, count), read(known, count, count)
    own, other = (ref[pl.ds(0, quarter), :].astype(jnp.float32) for ref in (mine, theirs))
    values = jnp.where(up, other, own) * columns_of(low) + jnp.where(up, own, other) * columns_of(high)
    put(out, values, whole)


def place_first_kernel(orders, log_k, lower_sent, upper_sent, lower_kept, upper_kept, out, col_out, sent):
    blocks = (lower_sent, upper_sent, lower_kept, upper_kept)
    quarter = blocks[0].shape[0] - EXTRA
    count = quarter // LANES
    copies = []
    for k, start in enumerate(quarter_places(orders, quarter)):
        rows = pl.ds(pl.multiple_of(start, LANES), quarter)
        source = blocks[k].at[pl.ds(0, quarter)]
        copies.append(pltpu.make_async_copy(source, out.at[rows, pl.ds(0, blocks[k].shape[1])], sent.at[k]))
        copies[-1].start()
    for block, start in zip(blocks, quarter_places(orders, count)):
        write(col_out, start, [-log_k - line for line in lines_of(block, count)])
    for copy in copies:
        copy.wait()


def last_sum(plan, part, mass, row_now, embeddings, log_k, orders):
    columns, rows_here = plan.shape
    depth = embeddings.shape[1]
    quarter = columns // 4
    width = depth // CHUNKS
    lines = quarter // LANES
    f32 = jnp.float32
    vmem = pl.BlockSpec(memory_space=pltpu.VMEM)

    def call(kernel, operands, outs, specs=None, flops=0, **options):
        return pl.pallas_call(
            kernel,
            out_shape=outs,
            in_specs=[vmem] * len(operands),
            out_specs=specs or [vmem] * len(outs),
            compiler_params=pltpu.CompilerParams(vmem_limit_bytes=VMEM_BYTES),
            cost_estimate=pl.CostEstimate(flops=flops, bytes_accessed=columns * depth, transcendentals=0),
            **options,
        )(*operands)

    def message(chunk):
        return jax.ShapeDtypeStruct((quarter + (EXTRA if chunk == 0 else 0), width), jnp.bfloat16)

    def table(count):
        return jax.ShapeDtypeStruct((count * lines, LANES), f32)

    mass, part = mass.reshape(table(4).shape), part.reshape(table(4).shape)
    flops = columns * rows_here * depth
    chunks = range(CHUNKS)
    sent = call(sent_kernel, [plan, embeddings, mass, part], [message(chunk) for chunk in chunks for _ in range(2)], flops=flops)
    got = [flipped(sent[2 * chunk + k], "dp", 1 << orders[k][0]) for chunk in chunks for k in range(2)]
    row = row_now[None, :]
    kept, row_out = call(
        kept_kernel,
        [plan, embeddings, mass, row],
        [jax.ShapeDtypeStruct((2, quarter, depth), f32), jax.ShapeDtypeStruct(row.shape, f32)],
        specs=[vmem, pl.BlockSpec(row.shape, lambda: (0, 0))],
        flops=flops,
    )
    pairs = []
    known = part
    for chunk in chunks:
        outs = [message(chunk)] * 2 + ([table(4)] if chunk == 0 else [])
        results = call(functools.partial(pair_kernel, chunk), [kept, got[2 * chunk], got[2 * chunk + 1], known], outs)
        both = results[:2]
        known = results[2] if chunk == 0 else known
        pairs += both
    known = [None, None]
    out = None
    for chunk in chunks:
        dones = []
        for k, order in enumerate(orders):
            mine = pairs[2 * chunk + k]
            theirs = flipped(mine, "dp", 1 << order[1])
            kernel = functools.partial(whole_kernel, chunk, order[1], quarter)
            if chunk == 0:
                done, known[k] = call(kernel, [mine, theirs], [message(chunk), table(2)])
            else:
                done, = call(kernel, [mine, theirs, known[k]], [message(chunk)])
            dones.append(done)
        blocks = [flipped(done, "dp", 1 << order[0]) for done, order in zip(dones, orders)] + dones
        if chunk == 0:
            out, col_out = call(
                functools.partial(place_first_kernel, orders, log_k),
                blocks,
                [jax.ShapeDtypeStruct((columns, depth), jnp.bfloat16), table(4)],
                specs=[pl.BlockSpec(memory_space=pl.ANY), pl.BlockSpec(table(4).shape, lambda: (0, 0))],
                scratch_shapes=[pltpu.SemaphoreType.DMA((4,))],
            )
        else:
            out = placed(chunk, orders, blocks, (columns, depth), [out])
    return out, row_out.reshape(row_now.shape), col_out.reshape(columns)


def beside_kernel(x, embeddings, out):
    out[...] = x[...]


def beside(x, embeddings):
    lines = (x.shape[0] // LANES, LANES)
    vmem = pl.BlockSpec(memory_space=pltpu.VMEM)
    return pl.pallas_call(
        beside_kernel,
        out_shape=jax.ShapeDtypeStruct(lines, x.dtype),
        in_specs=[vmem, pl.BlockSpec(memory_space=pl.ANY)],
        out_specs=vmem,
        compiler_params=pltpu.CompilerParams(vmem_limit_bytes=VMEM_BYTES),
    )(x.reshape(lines), embeddings).reshape(x.shape)


def on_device(embeddings, centroids, col_start):
    rows_here = embeddings.shape[0]
    cent_here = centroids.shape[0]
    n_total = rows_here * lax.axis_size("dp")
    k_total = cent_here * lax.axis_size("cent")

    bits = bits_of("dp")
    orders = (bits, [bits[1], bits[0]] + bits[2:])
    place = jnp.full((1,), lax.axis_index("dp"), jnp.int32)
    ups = [place >> bit & 1 for bit in bits]
    ups = [up == 1 for up in ups]
    odd = jnp.full((1,), lax.axis_index("cent"), jnp.int32) & 1 == 1
    ups, odd, embeddings, centroids = lax.optimization_barrier((ups, odd, embeddings, centroids))

    def chosen(bit, yes, no):
        return jnp.where(ups[bit].reshape((1,) * yes.ndim), yes, no)

    def sent_and_kept(value):
        quarters = jnp.split(value, 4)
        lows, highs = quarters[0::2], quarters[1::2]
        sent = [chosen(order[0], low, high) for order, low, high in zip(orders, lows, highs)]
        kept = [chosen(order[0], high, low) for order, low, high in zip(orders, lows, highs)]
        return jnp.concatenate(sent + kept)

    def aligned(value, mask):
        quarters = jnp.split(value, 4)
        for k, order in enumerate(orders):
            if mask >> order[0] & 1:
                quarters[k], quarters[2 + k] = quarters[2 + k], quarters[k]
        return jnp.concatenate(quarters)

    scores = lax.dot_general(
        sent_and_kept(centroids), embeddings, (((1,), (1,)), ((), ())), preferred_element_type=jnp.float32
    ) * (1.0 / math.sqrt(embeddings.shape[1]))
    col_now = sent_and_kept(col_start)
    for step_index in range(ITERS):
        shifted = scores + col_now[:, None]
        top = jnp.max(shifted, axis=0)
        part = top + jnp.log(jnp.sum(jnp.exp(shifted - top[None, :]), axis=0))
        last = step_index == ITERS - 1
        part = lse_over_cent(part, odd, lambda x: beside(x, embeddings) if last else x)
        row_now = -math.log(n_total) - part
        lifted = scores + row_now[None, :]
        top = jnp.max(lifted, axis=1)
        terms = jnp.exp(lifted - top[:, None])
        mass = jnp.sum(terms, axis=1)
        part = top + jnp.log(mass)
        if step_index < ITERS - 1:
            col_now = -math.log(k_total) - lse_over_dp(part, aligned)
    plan = terms.astype(jnp.bfloat16)
    if len(bits) == 2:
        return last_sum(plan, part, mass, row_now, embeddings, math.log(k_total), orders)
    new_centroids, row_out, whole = last_sum_by_vectors(plan, part, mass, row_now, embeddings, chosen, orders, aligned)
    return new_centroids, row_out, -math.log(k_total) - whole


def solution(mesh):
    specs = (P("dp", None), P("cent", None), P("cent"))
    return jax.shard_map(
        on_device,
        mesh=mesh,
        in_specs=specs,
        out_specs=(P("cent", None), P("dp"), P("cent")),
        check_vma=False,
    )
```

```python
import functools
import math

import jax
import jax.numpy as jnp
from jax import lax
from jax.experimental import pallas as pl
from jax.experimental.pallas import tpu as pltpu
from jax.sharding import PartitionSpec as P

ITERS = 3
CHUNKS = 2
LANES = 128
EXTRA = 16
VMEM_BYTES = 24 * 2**20


def bits_of(axis):
    size = lax.axis_size(axis)
    assert size & (size - 1) == 0
    return list(range(size.bit_length() - 1))


def flipped(x, axis, mask):
    size = lax.axis_size(axis)
    return lax.ppermute(x, axis, [(k, k ^ mask) for k in range(size)])


def lse(first, second):
    top = jnp.maximum(first, second)
    return top + jnp.log(jnp.exp(first - top) + jnp.exp(second - top))


def lse_over_dp(x, aligned):
    bits = bits_of("dp")

    def partner(value, mask):
        return aligned(flipped(value, "dp", mask), mask)

    for masks in ([1 << bit for bit in bits[k:k + 2]] for k in range(0, len(bits), 2)):
        if len(masks) == 2:
            far = partner(x, masks[0] | masks[1])
            near = [partner(x, mask) for mask in reversed(masks)]
            x = lse(lax.optimization_barrier(lse(x, far)), lse(*near))
        else:
            x = lse(x, partner(x, masks[0]))
    return x


def lse_over_cent(x, odd, joined_by):
    size = lax.axis_size("cent")
    near, middle, *rest = [1 << bit for bit in bits_of("cent")[1:]]

    def split(value, even_mask, odd_mask):
        return lax.ppermute(value, "cent", [(k, k ^ (odd_mask if k % 2 else even_mask)) for k in range(size)])

    x = lse(x, flipped(x, "cent", 1))
    second = split(x, near, middle)
    first = split(x, near, near | middle)
    x = joined_by(jnp.where(odd, lse(second, first), lse(x, first)))
    for mask in [1] + rest:
        x = lse(x, flipped(x, "cent", mask))
    return x


def column(values):
    lane = lax.broadcasted_iota(jnp.int32, (LANES, LANES), 1)
    diagonal = lane == lax.broadcasted_iota(jnp.int32, (LANES, LANES), 0)
    return jnp.sum(jnp.where(diagonal, values, 0.0), axis=1, keepdims=True)


def quarter_places(orders, quarter):
    ups = [lax.axis_index("dp") >> order[0] & 1 for order in orders]
    sent = [(2 * k + 1 - up) * quarter for k, up in enumerate(ups)]
    return sent + [(2 * k + up) * quarter for k, up in enumerate(ups)]


def place_kernel(chunk, orders, *refs):
    blocks, (out, sent) = refs[:4], refs[-2:]
    quarter, width = blocks[0].shape
    copies = []
    for k, start in enumerate(quarter_places(orders, quarter)):
        rows = pl.ds(pl.multiple_of(start, LANES), quarter)
        copies.append(pltpu.make_async_copy(blocks[k], out.at[rows, pl.ds(chunk * width, width)], sent.at[k]))
        copies[-1].start()
    for copy in copies:
        copy.wait()


def placed(chunk, orders, blocks, shape, so_far):
    vmem = pl.BlockSpec(memory_space=pltpu.VMEM)
    anywhere = pl.BlockSpec(memory_space=pl.ANY)
    return pl.pallas_call(
        functools.partial(place_kernel, chunk, orders),
        out_shape=jax.ShapeDtypeStruct(shape, blocks[0].dtype),
        in_specs=[vmem] * 4 + [anywhere] * len(so_far),
        out_specs=anywhere,
        scratch_shapes=[pltpu.SemaphoreType.DMA((4,))],
        input_output_aliases={4: 0} if so_far else {},
        compiler_params=pltpu.CompilerParams(vmem_limit_bytes=VMEM_BYTES),
    )(*blocks, *so_far)


def means_kernel(is_kept, plan, embeddings, mass, *rest):
    half = plan.shape[0] // 2
    quarter = half // 2
    sums = jnp.dot(plan[pl.ds(is_kept * half, half), :], embeddings[...], preferred_element_type=jnp.float32)
    if is_kept:
        weights, row, out, row_out = rest
        row_out[...] = row[...]
    else:
        out = None
    for block in range(half // LANES):
        factor = 1.0 / column(mass[pl.ds(is_kept * (half // LANES) + block, 1), :])
        if is_kept:
            factor = factor * column(weights[pl.ds(block, 1), :])
        rows = pl.ds(block * LANES % quarter, LANES)
        values = sums[block * LANES:(block + 1) * LANES] * factor
        half_index = block * LANES // quarter
        if is_kept:
            out[half_index, rows, :] = values
        else:
            width = rest[0].shape[1]
            for chunk in range(CHUNKS):
                target = rest[2 * chunk + half_index]
                target[rows, :] = values[:, chunk * width:(chunk + 1) * width].astype(target.dtype)


def means_of(is_kept, plan, embeddings, mass, *rest):
    count, rows_here = plan.shape
    depth = embeddings.shape[1]
    vmem = pl.BlockSpec(memory_space=pltpu.VMEM)
    if is_kept:
        out_shape = (
            jax.ShapeDtypeStruct((2, count // 4, depth), jnp.float32),
            jax.ShapeDtypeStruct((1, rows_here), jnp.float32),
        )
        out_specs = (vmem, pl.BlockSpec((1, rows_here), lambda: (0, 0)))
    else:
        out_shape = [jax.ShapeDtypeStruct((count // 4, depth // CHUNKS), jnp.bfloat16)] * (2 * CHUNKS)
        out_specs = [vmem] * (2 * CHUNKS)
    return pl.pallas_call(
        functools.partial(means_kernel, is_kept),
        out_shape=out_shape,
        in_specs=[vmem] * (3 + len(rest)),
        out_specs=out_specs,
        compiler_params=pltpu.CompilerParams(vmem_limit_bytes=VMEM_BYTES),
        cost_estimate=pl.CostEstimate(
            flops=count * rows_here * depth, bytes_accessed=2 * rows_here * depth, transcendentals=0
        ),
    )(plan, embeddings, mass.reshape(count // LANES, LANES), *rest)


def last_sum_by_vectors(plan, part, mass, row_now, embeddings, chosen, orders, aligned):
    quarter = part.shape[0] // 4
    first, second = orders[0][:2]
    partners = {bit: aligned(flipped(part, "dp", 1 << bit), 1 << bit) for bit in (first, second)}
    sent = means_of(0, plan, embeddings, mass)
    got = [flipped(sent[2 * chunk + k], "dp", 1 << order[0]) for chunk in range(CHUNKS) for k, order in enumerate(orders)]

    def kept_of(lower, upper):
        return jnp.concatenate([lower[2 * quarter:3 * quarter], upper[3 * quarter:]])

    pairs = lax.optimization_barrier([lse(partners[first], part), lse(partners[second], part)])
    pair = kept_of(*pairs)
    weights = jnp.exp(kept_of(part, part) - pair).reshape(2 * quarter // LANES, LANES)
    kept, row_out = means_of(1, plan, embeddings, mass, weights, row_now[None, :])
    weights = jnp.exp(kept_of(partners[first], partners[second]) - pair)

    corner = flipped(partners[first], "dp", 1 << second)

    def exchanged(mine, bit, own, other):
        mine = mine.astype(jnp.bfloat16)
        theirs = flipped(mine, "dp", 1 << bit).astype(jnp.float32)
        mine = mine.astype(jnp.float32)
        lower = chosen(bit, theirs, mine) * chosen(bit, other, own)
        upper = chosen(bit, mine, theirs) * chosen(bit, own, other)
        return (lower + upper).astype(jnp.bfloat16)

    def gathered(mine, order, own, other):
        if len(order) == 1:
            return exchanged(mine, order[0], own, other)
        bit = order[0]
        low, high = jnp.split(mine, 2, axis=0)
        got = flipped(chosen(bit, low, high).astype(jnp.bfloat16), "dp", 1 << bit).astype(jnp.float32)
        own, other = (chosen(bit, high, low) for low, high in (jnp.split(x, 2, axis=0) for x in (own, other)))
        ones = jnp.ones((own.shape[0], 1), jnp.float32)
        done = gathered(chosen(bit, high, low) * own + got * other, order[1:], ones, ones)
        theirs = flipped(done, "dp", 1 << bit)
        return jnp.concatenate([chosen(bit, theirs, done), chosen(bit, done, theirs)], axis=0)

    width = kept.shape[2] // CHUNKS
    shape = (part.shape[0], kept.shape[2])
    mines = []
    for chunk in range(CHUNKS):
        columns = slice(chunk * width, (chunk + 1) * width)
        if chunk > 0:
            mines, kept, weights = lax.optimization_barrier((mines, kept, weights))
        for k in range(2):
            rows = slice(k * quarter, (k + 1) * quarter)
            mines.append(kept[k, :, columns] + got[2 * chunk + k].astype(jnp.float32) * weights[rows, None])

    pairs, partners, corner = lax.optimization_barrier((pairs, partners, corner, mines))[:3]
    corner = aligned(corner, 1 << second)
    whole = lse(pairs[0], lse(corner, partners[second]))
    for bit in orders[0][2:]:
        whole = lse(aligned(flipped(whole, "dp", 1 << bit), 1 << bit), whole)
    pair_other = kept_of(lse(partners[second], corner), lse(partners[first], corner))
    weights_own = jnp.exp(kept_of(*pairs) - kept_of(whole, whole))
    weights_other = jnp.exp(pair_other - kept_of(whole, whole))

    outs = []
    firsts = []
    for chunk in range(CHUNKS):
        dones = []
        for k, order in enumerate(orders):
            rows = slice(k * quarter, (k + 1) * quarter)
            dones.append(gathered(mines[2 * chunk + k], order[1:], weights_own[rows, None], weights_other[rows, None]))
        if chunk < CHUNKS - 1:
            dones, weights_own, weights_other = lax.optimization_barrier((dones, weights_own, weights_other))
        firsts = firsts or dones
        blocks = [flipped(done, "dp", 1 << order[0]) for done, order in zip(dones, orders)] + dones
        outs = [placed(chunk, orders, blocks, shape, outs)]
    whole = lax.optimization_barrier((whole, firsts[0]))[0]
    quarters = jnp.split(whole, 4)
    halves = []
    for k, order in enumerate(orders):
        sent, kept = quarters[k], quarters[2 + k]
        halves += [chosen(order[0], sent, kept), chosen(order[0], kept, sent)]
    return outs[0], row_out.reshape(row_now.shape), jnp.concatenate(halves)


def parts_of(lines):
    row = lax.broadcasted_iota(jnp.int32, (EXTRA, LANES), 0)
    rows = jnp.zeros((EXTRA, LANES), jnp.float32)
    for index, line in enumerate(lines):
        for part in range(3):
            rounded = line.astype(jnp.bfloat16).astype(jnp.float32)
            rows = jnp.where(row == 3 * index + part, rounded, rows)
            line = line - rounded
    return rows.astype(jnp.bfloat16)


def lines_of(message, count):
    rows = message[pl.ds(message.shape[0] - EXTRA, EXTRA), pl.ds(0, LANES)].astype(jnp.float32)
    return [(rows[k:k + 1] + rows[k + 1:k + 2]) + rows[k + 2:k + 3] for k in range(0, 3 * count, 3)]


def put(message, values, lines):
    quarter, width = values.shape
    message[pl.ds(0, quarter), :] = values.astype(message.dtype)
    if lines:
        message[pl.ds(quarter, EXTRA), pl.ds(0, LANES)] = parts_of(lines)
        message[pl.ds(quarter, EXTRA), pl.ds(LANES, width - LANES)] = jnp.zeros((EXTRA, width - LANES), message.dtype)


def columns_of(lines):
    return jnp.concatenate([column(line) for line in lines], axis=0)


def read(ref, start, count):
    return [ref[pl.ds(start + k, 1), :] for k in range(count)]


def write(ref, start, lines):
    for k, line in enumerate(lines):
        ref[pl.ds(start + k, 1), :] = line


def joined(first, second):
    whole = [lse(a, b) for a, b in zip(first, second)]
    return whole, [jnp.exp(a - b) for a, b in zip(first, whole)], [jnp.exp(a - b) for a, b in zip(second, whole)]


def sent_kernel(chunk, plan, embeddings, mass, part, *sent):
    quarter = plan.shape[0] // 4
    count = quarter // LANES
    width = embeddings.shape[1] // CHUNKS
    columns = embeddings[:, pl.ds(chunk * width, width)]
    sums = jnp.dot(plan[pl.ds(0, 2 * quarter), :], columns, preferred_element_type=jnp.float32)
    for k in range(2):
        values = sums[k * quarter:(k + 1) * quarter] / columns_of(read(mass, k * count, count))
        put(sent[k], values, read(part, k * count, count) if chunk == 0 else [])


def kept_kernel(plan, embeddings, mass, row, kept, row_out):
    quarter = plan.shape[0] // 4
    count = quarter // LANES
    row_out[...] = row[...]
    sums = jnp.dot(plan[pl.ds(2 * quarter, 2 * quarter), :], embeddings[...], preferred_element_type=jnp.float32)
    for k in range(2):
        kept[k] = sums[k * quarter:(k + 1) * quarter] / columns_of(read(mass, (2 + k) * count, count))


def pair_kernel(chunk, kept, lower, upper, known, out_lower, out_upper, *weights_out):
    quarter = kept.shape[1]
    count = quarter // LANES
    for k, (got, out) in enumerate(((lower, out_lower), (upper, out_upper))):
        if chunk == 0:
            pair, own, other = joined(read(known, (2 + k) * count, count), lines_of(got, count))
            write(weights_out[0], 2 * k * count, own + other)
        else:
            pair = []
            own, other = read(known, 2 * k * count, count), read(known, (2 * k + 1) * count, count)
        width = got.shape[1]
        values = kept[k, :, pl.ds(chunk * width, width)] * columns_of(own)
        put(out, values + got[pl.ds(0, quarter), :].astype(jnp.float32) * columns_of(other), pair)


def whole_kernel(chunk, bit, quarter, mine, theirs, *rest):
    count = quarter // LANES
    up = lax.axis_index("dp") >> bit & 1 == 1
    if chunk == 0:
        out, weights_out = rest
        own, other = lines_of(mine, count), lines_of(theirs, count)
        lower = [jnp.where(up, b, a) for a, b in zip(own, other)]
        upper = [jnp.where(up, a, b) for a, b in zip(own, other)]
        whole, low, high = joined(lower, upper)
        write(weights_out, 0, low + high)
    else:
        known, out = rest
        whole = []
        low, high = read(known, 0, count), read(known, count, count)
    own, other = (ref[pl.ds(0, quarter), :].astype(jnp.float32) for ref in (mine, theirs))
    values = jnp.where(up, other, own) * columns_of(low) + jnp.where(up, own, other) * columns_of(high)
    put(out, values, whole)


def place_first_kernel(orders, log_k, lower_sent, upper_sent, lower_kept, upper_kept, out, col_out, sent):
    blocks = (lower_sent, upper_sent, lower_kept, upper_kept)
    quarter = blocks[0].shape[0] - EXTRA
    count = quarter // LANES
    copies = []
    for k, start in enumerate(quarter_places(orders, quarter)):
        rows = pl.ds(pl.multiple_of(start, LANES), quarter)
        source = blocks[k].at[pl.ds(0, quarter)]
        copies.append(pltpu.make_async_copy(source, out.at[rows, pl.ds(0, blocks[k].shape[1])], sent.at[k]))
        copies[-1].start()
    for block, start in zip(blocks, quarter_places(orders, count)):
        write(col_out, start, [-log_k - line for line in lines_of(block, count)])
    for copy in copies:
        copy.wait()


def last_sum(plan, part, mass, row_now, embeddings, log_k, orders):
    columns, rows_here = plan.shape
    depth = embeddings.shape[1]
    quarter = columns // 4
    width = depth // CHUNKS
    lines = quarter // LANES
    f32 = jnp.float32
    vmem = pl.BlockSpec(memory_space=pltpu.VMEM)

    def call(kernel, operands, outs, specs=None, flops=0, **options):
        return pl.pallas_call(
            kernel,
            out_shape=outs,
            in_specs=[vmem] * len(operands),
            out_specs=specs or [vmem] * len(outs),
            compiler_params=pltpu.CompilerParams(vmem_limit_bytes=VMEM_BYTES),
            cost_estimate=pl.CostEstimate(flops=flops, bytes_accessed=columns * depth, transcendentals=0),
            **options,
        )(*operands)

    def message(chunk):
        return jax.ShapeDtypeStruct((quarter + (EXTRA if chunk == 0 else 0), width), jnp.bfloat16)

    def table(count):
        return jax.ShapeDtypeStruct((count * lines, LANES), f32)

    mass, part = mass.reshape(table(4).shape), part.reshape(table(4).shape)
    flops = columns * rows_here * depth
    chunks = range(CHUNKS)
    sent = []
    for chunk in chunks:
        kernel = functools.partial(sent_kernel, chunk)
        sent += call(kernel, [plan, embeddings, mass, part], [message(chunk)] * 2, flops=flops // CHUNKS)
    got = [flipped(sent[2 * chunk + k], "dp", 1 << orders[k][0]) for chunk in chunks for k in range(2)]
    row = row_now[None, :]
    kept, row_out = call(
        kept_kernel,
        [plan, embeddings, mass, row],
        [jax.ShapeDtypeStruct((2, quarter, depth), f32), jax.ShapeDtypeStruct(row.shape, f32)],
        specs=[vmem, pl.BlockSpec(row.shape, lambda: (0, 0))],
        flops=flops,
    )
    pairs = []
    known = part
    for chunk in chunks:
        outs = [message(chunk)] * 2 + ([table(4)] if chunk == 0 else [])
        results = call(functools.partial(pair_kernel, chunk), [kept, got[2 * chunk], got[2 * chunk + 1], known], outs)
        both = results[:2]
        known = results[2] if chunk == 0 else known
        pairs += both
    known = [None, None]
    out = None
    for chunk in chunks:
        dones = []
        for k, order in enumerate(orders):
            mine = pairs[2 * chunk + k]
            theirs = flipped(mine, "dp", 1 << order[1])
            kernel = functools.partial(whole_kernel, chunk, order[1], quarter)
            if chunk == 0:
                done, known[k] = call(kernel, [mine, theirs], [message(chunk), table(2)])
            else:
                done, = call(kernel, [mine, theirs, known[k]], [message(chunk)])
            dones.append(done)
        blocks = [flipped(done, "dp", 1 << order[0]) for done, order in zip(dones, orders)] + dones
        if chunk == 0:
            out, col_out = call(
                functools.partial(place_first_kernel, orders, log_k),
                blocks,
                [jax.ShapeDtypeStruct((columns, depth), jnp.bfloat16), table(4)],
                specs=[pl.BlockSpec(memory_space=pl.ANY), pl.BlockSpec(table(4).shape, lambda: (0, 0))],
                scratch_shapes=[pltpu.SemaphoreType.DMA((4,))],
            )
        else:
            out = placed(chunk, orders, blocks, (columns, depth), [out])
    return out, row_out.reshape(row_now.shape), col_out.reshape(columns)


def beside_kernel(x, embeddings, out):
    out[...] = x[...]


def beside(x, embeddings):
    lines = (x.shape[0] // LANES, LANES)
    vmem = pl.BlockSpec(memory_space=pltpu.VMEM)
    return pl.pallas_call(
        beside_kernel,
        out_shape=jax.ShapeDtypeStruct(lines, x.dtype),
        in_specs=[vmem, pl.BlockSpec(memory_space=pl.ANY)],
        out_specs=vmem,
        compiler_params=pltpu.CompilerParams(vmem_limit_bytes=VMEM_BYTES),
    )(x.reshape(lines), embeddings).reshape(x.shape)


def on_device(embeddings, centroids, col_start):
    rows_here = embeddings.shape[0]
    cent_here = centroids.shape[0]
    n_total = rows_here * lax.axis_size("dp")
    k_total = cent_here * lax.axis_size("cent")

    bits = bits_of("dp")
    orders = (bits, [bits[1], bits[0]] + bits[2:])
    place = jnp.full((1,), lax.axis_index("dp"), jnp.int32)
    ups = [place >> bit & 1 for bit in bits]
    ups = [up == 1 for up in ups]
    odd = jnp.full((1,), lax.axis_index("cent"), jnp.int32) & 1 == 1
    ups, odd, embeddings, centroids = lax.optimization_barrier((ups, odd, embeddings, centroids))

    def chosen(bit, yes, no):
        return jnp.where(ups[bit].reshape((1,) * yes.ndim), yes, no)

    def sent_and_kept(value):
        quarters = jnp.split(value, 4)
        lows, highs = quarters[0::2], quarters[1::2]
        sent = [chosen(order[0], low, high) for order, low, high in zip(orders, lows, highs)]
        kept = [chosen(order[0], high, low) for order, low, high in zip(orders, lows, highs)]
        return jnp.concatenate(sent + kept)

    def aligned(value, mask):
        quarters = jnp.split(value, 4)
        for k, order in enumerate(orders):
            if mask >> order[0] & 1:
                quarters[k], quarters[2 + k] = quarters[2 + k], quarters[k]
        return jnp.concatenate(quarters)

    scores = lax.dot_general(
        sent_and_kept(centroids), embeddings, (((1,), (1,)), ((), ())), preferred_element_type=jnp.float32
    ) * (1.0 / math.sqrt(embeddings.shape[1]))
    col_now = sent_and_kept(col_start)
    for step_index in range(ITERS):
        shifted = scores + col_now[:, None]
        top = jnp.max(shifted, axis=0)
        part = top + jnp.log(jnp.sum(jnp.exp(shifted - top[None, :]), axis=0))
        last = step_index == ITERS - 1
        part = lse_over_cent(part, odd, lambda x: beside(x, embeddings) if last else x)
        row_now = -math.log(n_total) - part
        lifted = scores + row_now[None, :]
        top = jnp.max(lifted, axis=1)
        terms = jnp.exp(lifted - top[:, None])
        mass = jnp.sum(terms, axis=1)
        part = top + jnp.log(mass)
        if step_index < ITERS - 1:
            col_now = -math.log(k_total) - lse_over_dp(part, aligned)
    plan = terms.astype(jnp.bfloat16)
    if len(bits) == 2:
        return last_sum(plan, part, mass, row_now, embeddings, math.log(k_total), orders)
    new_centroids, row_out, whole = last_sum_by_vectors(plan, part, mass, row_now, embeddings, chosen, orders, aligned)
    return new_centroids, row_out, -math.log(k_total) - whole


def solution(mesh):
    specs = (P("dp", None), P("cent", None), P("cent"))
    return jax.shard_map(
        on_device,
        mesh=mesh,
        in_specs=specs,
        out_specs=(P("cent", None), P("dp"), P("cent")),
        check_vma=False,
    )
```

```python
import functools
import math

import jax
import jax.numpy as jnp
from jax import lax
from jax.experimental import pallas as pl
from jax.experimental.pallas import tpu as pltpu
from jax.sharding import PartitionSpec as P

ITERS = 3
CHUNKS = 2
LANES = 128
EXTRA = 16
VMEM_BYTES = 24 * 2**20
ORDER_VMEM_BYTES = 52 * 2**20


def bits_of(axis):
    size = lax.axis_size(axis)
    assert size & (size - 1) == 0
    return list(range(size.bit_length() - 1))


def flipped(x, axis, mask):
    size = lax.axis_size(axis)
    return lax.ppermute(x, axis, [(k, k ^ mask) for k in range(size)])


def lse(first, second):
    top = jnp.maximum(first, second)
    return top + jnp.log(jnp.exp(first - top) + jnp.exp(second - top))


def lse_over_dp(x, aligned):
    bits = bits_of("dp")

    def partner(value, mask):
        return aligned(flipped(value, "dp", mask), mask)

    for masks in ([1 << bit for bit in bits[k:k + 2]] for k in range(0, len(bits), 2)):
        if len(masks) == 2:
            far = partner(x, masks[0] | masks[1])
            near = [partner(x, mask) for mask in reversed(masks)]
            x = lse(lax.optimization_barrier(lse(x, far)), lse(*near))
        else:
            x = lse(x, partner(x, masks[0]))
    return x


def lse_over_cent(x, odd, joined_by):
    size = lax.axis_size("cent")
    near, middle, *rest = [1 << bit for bit in bits_of("cent")[1:]]

    def split(value, even_mask, odd_mask):
        return lax.ppermute(value, "cent", [(k, k ^ (odd_mask if k % 2 else even_mask)) for k in range(size)])

    x = lse(x, flipped(x, "cent", 1))
    second = split(x, near, middle)
    first = split(x, near, near | middle)
    x = joined_by(jnp.where(odd, lse(second, first), lse(x, first)))
    for mask in [1] + rest:
        x = lse(x, flipped(x, "cent", mask))
    return x


def column(values):
    lane = lax.broadcasted_iota(jnp.int32, (LANES, LANES), 1)
    diagonal = lane == lax.broadcasted_iota(jnp.int32, (LANES, LANES), 0)
    return jnp.sum(jnp.where(diagonal, values, 0.0), axis=1, keepdims=True)


def quarter_places(orders, quarter):
    ups = [lax.axis_index("dp") >> order[0] & 1 for order in orders]
    sent = [(2 * k + 1 - up) * quarter for k, up in enumerate(ups)]
    return sent + [(2 * k + up) * quarter for k, up in enumerate(ups)]


def place_kernel(chunk, orders, *refs):
    blocks, (out, sent) = refs[:4], refs[-2:]
    quarter, width = blocks[0].shape
    copies = []
    for k, start in enumerate(quarter_places(orders, quarter)):
        rows = pl.ds(pl.multiple_of(start, LANES), quarter)
        copies.append(pltpu.make_async_copy(blocks[k], out.at[rows, pl.ds(chunk * width, width)], sent.at[k]))
        copies[-1].start()
    for copy in copies:
        copy.wait()


def placed(chunk, orders, blocks, shape, so_far):
    vmem = pl.BlockSpec(memory_space=pltpu.VMEM)
    anywhere = pl.BlockSpec(memory_space=pl.ANY)
    return pl.pallas_call(
        functools.partial(place_kernel, chunk, orders),
        out_shape=jax.ShapeDtypeStruct(shape, blocks[0].dtype),
        in_specs=[vmem] * 4 + [anywhere] * len(so_far),
        out_specs=anywhere,
        scratch_shapes=[pltpu.SemaphoreType.DMA((4,))],
        input_output_aliases={4: 0} if so_far else {},
        compiler_params=pltpu.CompilerParams(vmem_limit_bytes=VMEM_BYTES),
    )(*blocks, *so_far)


def means_kernel(is_kept, plan, embeddings, mass, *rest):
    half = plan.shape[0] // 2
    quarter = half // 2
    sums = jnp.dot(plan[pl.ds(is_kept * half, half), :], embeddings[...], preferred_element_type=jnp.float32)
    if is_kept:
        weights, row, out, row_out = rest
        row_out[...] = row[...]
    else:
        out = None
    for block in range(half // LANES):
        factor = 1.0 / column(mass[pl.ds(is_kept * (half // LANES) + block, 1), :])
        if is_kept:
            factor = factor * column(weights[pl.ds(block, 1), :])
        rows = pl.ds(block * LANES % quarter, LANES)
        values = sums[block * LANES:(block + 1) * LANES] * factor
        half_index = block * LANES // quarter
        if is_kept:
            out[half_index, rows, :] = values
        else:
            width = rest[0].shape[1]
            for chunk in range(CHUNKS):
                target = rest[2 * chunk + half_index]
                target[rows, :] = values[:, chunk * width:(chunk + 1) * width].astype(target.dtype)


def means_of(is_kept, plan, embeddings, mass, *rest):
    count, rows_here = plan.shape
    depth = embeddings.shape[1]
    vmem = pl.BlockSpec(memory_space=pltpu.VMEM)
    if is_kept:
        out_shape = (
            jax.ShapeDtypeStruct((2, count // 4, depth), jnp.float32),
            jax.ShapeDtypeStruct((1, rows_here), jnp.float32),
        )
        out_specs = (vmem, pl.BlockSpec((1, rows_here), lambda: (0, 0)))
    else:
        out_shape = [jax.ShapeDtypeStruct((count // 4, depth // CHUNKS), jnp.bfloat16)] * (2 * CHUNKS)
        out_specs = [vmem] * (2 * CHUNKS)
    return pl.pallas_call(
        functools.partial(means_kernel, is_kept),
        out_shape=out_shape,
        in_specs=[vmem] * (3 + len(rest)),
        out_specs=out_specs,
        compiler_params=pltpu.CompilerParams(vmem_limit_bytes=VMEM_BYTES),
        cost_estimate=pl.CostEstimate(
            flops=count * rows_here * depth, bytes_accessed=2 * rows_here * depth, transcendentals=0
        ),
    )(plan, embeddings, mass.reshape(count // LANES, LANES), *rest)


def last_sum_by_vectors(plan, part, mass, row_now, embeddings, chosen, orders, aligned):
    quarter = part.shape[0] // 4
    first, second = orders[0][:2]
    partners = {bit: aligned(flipped(part, "dp", 1 << bit), 1 << bit) for bit in (first, second)}
    sent = means_of(0, plan, embeddings, mass)
    got = [flipped(sent[2 * chunk + k], "dp", 1 << order[0]) for chunk in range(CHUNKS) for k, order in enumerate(orders)]

    def kept_of(lower, upper):
        return jnp.concatenate([lower[2 * quarter:3 * quarter], upper[3 * quarter:]])

    pairs = lax.optimization_barrier([lse(partners[first], part), lse(partners[second], part)])
    pair = kept_of(*pairs)
    weights = jnp.exp(kept_of(part, part) - pair).reshape(2 * quarter // LANES, LANES)
    kept, row_out = means_of(1, plan, embeddings, mass, weights, row_now[None, :])
    weights = jnp.exp(kept_of(partners[first], partners[second]) - pair)

    corner = flipped(partners[first], "dp", 1 << second)

    def exchanged(mine, bit, own, other):
        mine = mine.astype(jnp.bfloat16)
        theirs = flipped(mine, "dp", 1 << bit).astype(jnp.float32)
        mine = mine.astype(jnp.float32)
        lower = chosen(bit, theirs, mine) * chosen(bit, other, own)
        upper = chosen(bit, mine, theirs) * chosen(bit, own, other)
        return (lower + upper).astype(jnp.bfloat16)

    def gathered(mine, order, own, other):
        if len(order) == 1:
            return exchanged(mine, order[0], own, other)
        bit = order[0]
        low, high = jnp.split(mine, 2, axis=0)
        got = flipped(chosen(bit, low, high).astype(jnp.bfloat16), "dp", 1 << bit).astype(jnp.float32)
        own, other = (chosen(bit, high, low) for low, high in (jnp.split(x, 2, axis=0) for x in (own, other)))
        ones = jnp.ones((own.shape[0], 1), jnp.float32)
        done = gathered(chosen(bit, high, low) * own + got * other, order[1:], ones, ones)
        theirs = flipped(done, "dp", 1 << bit)
        return jnp.concatenate([chosen(bit, theirs, done), chosen(bit, done, theirs)], axis=0)

    width = kept.shape[2] // CHUNKS
    shape = (part.shape[0], kept.shape[2])
    mines = []
    for chunk in range(CHUNKS):
        columns = slice(chunk * width, (chunk + 1) * width)
        if chunk > 0:
            mines, kept, weights = lax.optimization_barrier((mines, kept, weights))
        for k in range(2):
            rows = slice(k * quarter, (k + 1) * quarter)
            mines.append(kept[k, :, columns] + got[2 * chunk + k].astype(jnp.float32) * weights[rows, None])

    pairs, partners, corner = lax.optimization_barrier((pairs, partners, corner, mines))[:3]
    corner = aligned(corner, 1 << second)
    whole = lse(pairs[0], lse(corner, partners[second]))
    for bit in orders[0][2:]:
        whole = lse(aligned(flipped(whole, "dp", 1 << bit), 1 << bit), whole)
    pair_other = kept_of(lse(partners[second], corner), lse(partners[first], corner))
    weights_own = jnp.exp(kept_of(*pairs) - kept_of(whole, whole))
    weights_other = jnp.exp(pair_other - kept_of(whole, whole))

    outs = []
    firsts = []
    for chunk in range(CHUNKS):
        dones = []
        for k, order in enumerate(orders):
            rows = slice(k * quarter, (k + 1) * quarter)
            dones.append(gathered(mines[2 * chunk + k], order[1:], weights_own[rows, None], weights_other[rows, None]))
        if chunk < CHUNKS - 1:
            dones, weights_own, weights_other = lax.optimization_barrier((dones, weights_own, weights_other))
        firsts = firsts or dones
        blocks = [flipped(done, "dp", 1 << order[0]) for done, order in zip(dones, orders)] + dones
        outs = [placed(chunk, orders, blocks, shape, outs)]
    whole = lax.optimization_barrier((whole, firsts[0]))[0]
    quarters = jnp.split(whole, 4)
    halves = []
    for k, order in enumerate(orders):
        sent, kept = quarters[k], quarters[2 + k]
        halves += [chosen(order[0], sent, kept), chosen(order[0], kept, sent)]
    return outs[0], row_out.reshape(row_now.shape), jnp.concatenate(halves)


def parts_of(lines):
    row = lax.broadcasted_iota(jnp.int32, (EXTRA, LANES), 0)
    rows = jnp.zeros((EXTRA, LANES), jnp.float32)
    for index, line in enumerate(lines):
        for part in range(3):
            rounded = line.astype(jnp.bfloat16).astype(jnp.float32)
            rows = jnp.where(row == 3 * index + part, rounded, rows)
            line = line - rounded
    return rows.astype(jnp.bfloat16)


def lines_of(message, count):
    rows = message[pl.ds(message.shape[0] - EXTRA, EXTRA), pl.ds(0, LANES)].astype(jnp.float32)
    return [(rows[k:k + 1] + rows[k + 1:k + 2]) + rows[k + 2:k + 3] for k in range(0, 3 * count, 3)]


def put(message, values, lines):
    quarter, width = values.shape
    message[pl.ds(0, quarter), :] = values.astype(message.dtype)
    if lines:
        message[pl.ds(quarter, EXTRA), pl.ds(0, LANES)] = parts_of(lines)
        message[pl.ds(quarter, EXTRA), pl.ds(LANES, width - LANES)] = jnp.zeros((EXTRA, width - LANES), message.dtype)


def columns_of(lines):
    return jnp.concatenate([column(line) for line in lines], axis=0)


def read(ref, start, count):
    return [ref[pl.ds(start + k, 1), :] for k in range(count)]


def write(ref, start, lines):
    for k, line in enumerate(lines):
        ref[pl.ds(start + k, 1), :] = line


def joined(first, second):
    whole = [lse(a, b) for a, b in zip(first, second)]
    return whole, [jnp.exp(a - b) for a, b in zip(first, whole)], [jnp.exp(a - b) for a, b in zip(second, whole)]


def sent_kernel(chunk, plan, embeddings, mass, part, *sent):
    quarter = plan.shape[0] // 4
    count = quarter // LANES
    width = embeddings.shape[1] // CHUNKS
    columns = embeddings[:, pl.ds(chunk * width, width)]
    sums = jnp.dot(plan[pl.ds(0, 2 * quarter), :], columns, preferred_element_type=jnp.float32)
    for k in range(2):
        values = sums[k * quarter:(k + 1) * quarter] / columns_of(read(mass, k * count, count))
        put(sent[k], values, read(part, k * count, count) if chunk == 0 else [])


def kept_kernel(plan, embeddings, mass, row, kept, row_out):
    quarter = plan.shape[0] // 4
    count = quarter // LANES
    row_out[...] = row[...]
    sums = jnp.dot(plan[pl.ds(2 * quarter, 2 * quarter), :], embeddings[...], preferred_element_type=jnp.float32)
    for k in range(2):
        kept[k] = sums[k * quarter:(k + 1) * quarter] / columns_of(read(mass, (2 + k) * count, count))


def pair_kernel(chunk, kept, lower, upper, known, out_lower, out_upper, *weights_out):
    quarter = kept.shape[1]
    count = quarter // LANES
    for k, (got, out) in enumerate(((lower, out_lower), (upper, out_upper))):
        if chunk == 0:
            pair, own, other = joined(read(known, (2 + k) * count, count), lines_of(got, count))
            write(weights_out[0], 2 * k * count, own + other)
        else:
            pair = []
            own, other = read(known, 2 * k * count, count), read(known, (2 * k + 1) * count, count)
        width = got.shape[1]
        values = kept[k, :, pl.ds(chunk * width, width)] * columns_of(own)
        put(out, values + got[pl.ds(0, quarter), :].astype(jnp.float32) * columns_of(other), pair)


def whole_kernel(chunk, bit, quarter, mine, theirs, *rest):
    count = quarter // LANES
    up = lax.axis_index("dp") >> bit & 1 == 1
    if chunk == 0:
        out, weights_out = rest
        own, other = lines_of(mine, count), lines_of(theirs, count)
        lower = [jnp.where(up, b, a) for a, b in zip(own, other)]
        upper = [jnp.where(up, a, b) for a, b in zip(own, other)]
        whole, low, high = joined(lower, upper)
        write(weights_out, 0, low + high)
    else:
        known, out = rest
        whole = []
        low, high = read(known, 0, count), read(known, count, count)
    own, other = (ref[pl.ds(0, quarter), :].astype(jnp.float32) for ref in (mine, theirs))
    values = jnp.where(up, other, own) * columns_of(low) + jnp.where(up, own, other) * columns_of(high)
    put(out, values, whole)


def place_first_kernel(orders, log_k, lower_sent, upper_sent, lower_kept, upper_kept, out, col_out, sent):
    blocks = (lower_sent, upper_sent, lower_kept, upper_kept)
    quarter = blocks[0].shape[0] - EXTRA
    count = quarter // LANES
    copies = []
    for k, start in enumerate(quarter_places(orders, quarter)):
        rows = pl.ds(pl.multiple_of(start, LANES), quarter)
        source = blocks[k].at[pl.ds(0, quarter)]
        copies.append(pltpu.make_async_copy(source, out.at[rows, pl.ds(0, blocks[k].shape[1])], sent.at[k]))
        copies[-1].start()
    for block, start in zip(blocks, quarter_places(orders, count)):
        write(col_out, start, [-log_k - line for line in lines_of(block, count)])
    for copy in copies:
        copy.wait()


def last_sum(plan, part, mass, row_now, embeddings, log_k, orders):
    columns, rows_here = plan.shape
    depth = embeddings.shape[1]
    quarter = columns // 4
    width = depth // CHUNKS
    lines = quarter // LANES
    f32 = jnp.float32
    vmem = pl.BlockSpec(memory_space=pltpu.VMEM)

    def call(kernel, operands, outs, specs=None, flops=0, **options):
        return pl.pallas_call(
            kernel,
            out_shape=outs,
            in_specs=[vmem] * len(operands),
            out_specs=specs or [vmem] * len(outs),
            compiler_params=pltpu.CompilerParams(vmem_limit_bytes=VMEM_BYTES),
            cost_estimate=pl.CostEstimate(flops=flops, bytes_accessed=columns * depth, transcendentals=0),
            **options,
        )(*operands)

    def message(chunk):
        return jax.ShapeDtypeStruct((quarter + (EXTRA if chunk == 0 else 0), width), jnp.bfloat16)

    def table(count):
        return jax.ShapeDtypeStruct((count * lines, LANES), f32)

    mass, part = mass.reshape(table(4).shape), part.reshape(table(4).shape)
    flops = columns * rows_here * depth
    chunks = range(CHUNKS)
    sent = []
    for chunk in chunks:
        kernel = functools.partial(sent_kernel, chunk)
        sent += call(kernel, [plan, embeddings, mass, part], [message(chunk)] * 2, flops=flops // CHUNKS)
    got = [flipped(sent[2 * chunk + k], "dp", 1 << orders[k][0]) for chunk in chunks for k in range(2)]
    row = row_now[None, :]
    kept, row_out = call(
        kept_kernel,
        [plan, embeddings, mass, row],
        [jax.ShapeDtypeStruct((2, quarter, depth), f32), jax.ShapeDtypeStruct(row.shape, f32)],
        specs=[vmem, pl.BlockSpec(row.shape, lambda: (0, 0))],
        flops=flops,
    )
    pairs = []
    known = part
    for chunk in chunks:
        outs = [message(chunk)] * 2 + ([table(4)] if chunk == 0 else [])
        results = call(functools.partial(pair_kernel, chunk), [kept, got[2 * chunk], got[2 * chunk + 1], known], outs)
        both = results[:2]
        known = results[2] if chunk == 0 else known
        pairs += both
    known = [None, None]
    out = None
    for chunk in chunks:
        dones = []
        for k, order in enumerate(orders):
            mine = pairs[2 * chunk + k]
            theirs = flipped(mine, "dp", 1 << order[1])
            kernel = functools.partial(whole_kernel, chunk, order[1], quarter)
            if chunk == 0:
                done, known[k] = call(kernel, [mine, theirs], [message(chunk), table(2)])
            else:
                done, = call(kernel, [mine, theirs, known[k]], [message(chunk)])
            dones.append(done)
        blocks = [flipped(done, "dp", 1 << order[0]) for done, order in zip(dones, orders)] + dones
        if chunk == 0:
            out, col_out = call(
                functools.partial(place_first_kernel, orders, log_k),
                blocks,
                [jax.ShapeDtypeStruct((columns, depth), jnp.bfloat16), table(4)],
                specs=[pl.BlockSpec(memory_space=pl.ANY), pl.BlockSpec(table(4).shape, lambda: (0, 0))],
                scratch_shapes=[pltpu.SemaphoreType.DMA((4,))],
            )
        else:
            out = placed(chunk, orders, blocks, (columns, depth), [out])
    return out, row_out.reshape(row_now.shape), col_out.reshape(columns)


def order_kernel(orders, centroids, col, centroids_out, col_out, arrived):
    copies = []
    for source, target in ((centroids, centroids_out), (col, col_out)):
        quarter = source.shape[0] // 4
        for k, start in enumerate(quarter_places(orders, quarter)):
            start = start if source is col else pl.multiple_of(start, LANES)
            rows = pl.ds(k * quarter, quarter)
            copies.append(pltpu.make_async_copy(
                source.at[pl.ds(start, quarter)], target.at[rows], arrived.at[len(copies)]
            ))
            copies[-1].start()
    for copy in copies:
        copy.wait()


def in_order(centroids, col_start, orders):
    count = centroids.shape[0]
    vmem = pl.BlockSpec(memory_space=pltpu.VMEM)
    anywhere = pl.BlockSpec(memory_space=pl.ANY)
    lines = jax.ShapeDtypeStruct((count // LANES, LANES), jnp.float32)
    ordered, col = pl.pallas_call(
        functools.partial(order_kernel, orders),
        out_shape=(jax.ShapeDtypeStruct(centroids.shape, centroids.dtype), lines),
        in_specs=[anywhere, anywhere],
        out_specs=(vmem, vmem),
        scratch_shapes=[pltpu.SemaphoreType.DMA((8,))],
        compiler_params=pltpu.CompilerParams(vmem_limit_bytes=ORDER_VMEM_BYTES),
    )(centroids, col_start.reshape(lines.shape))
    return ordered, col.reshape(count)


def beside_kernel(x, embeddings, out):
    out[...] = x[...]


def beside(x, embeddings):
    lines = (x.shape[0] // LANES, LANES)
    vmem = pl.BlockSpec(memory_space=pltpu.VMEM)
    return pl.pallas_call(
        beside_kernel,
        out_shape=jax.ShapeDtypeStruct(lines, x.dtype),
        in_specs=[vmem, pl.BlockSpec(memory_space=pl.ANY)],
        out_specs=vmem,
        compiler_params=pltpu.CompilerParams(vmem_limit_bytes=VMEM_BYTES),
    )(x.reshape(lines), embeddings).reshape(x.shape)


def on_device(embeddings, centroids, col_start):
    rows_here = embeddings.shape[0]
    cent_here = centroids.shape[0]
    n_total = rows_here * lax.axis_size("dp")
    k_total = cent_here * lax.axis_size("cent")

    bits = bits_of("dp")
    orders = (bits, [bits[1], bits[0]] + bits[2:])
    place = jnp.full((1,), lax.axis_index("dp"), jnp.int32)
    ups = [place >> bit & 1 for bit in bits]
    ups = [up == 1 for up in ups]
    odd = jnp.full((1,), lax.axis_index("cent"), jnp.int32) & 1 == 1
    ups, odd, embeddings, centroids = lax.optimization_barrier((ups, odd, embeddings, centroids))

    def chosen(bit, yes, no):
        return jnp.where(ups[bit].reshape((1,) * yes.ndim), yes, no)

    def aligned(value, mask):
        quarters = jnp.split(value, 4)
        for k, order in enumerate(orders):
            if mask >> order[0] & 1:
                quarters[k], quarters[2 + k] = quarters[2 + k], quarters[k]
        return jnp.concatenate(quarters)

    ordered, col_now = in_order(centroids, col_start, orders)
    scores = lax.dot_general(
        ordered, embeddings, (((1,), (1,)), ((), ())), preferred_element_type=jnp.float32
    ) * (1.0 / math.sqrt(embeddings.shape[1]))
    for step_index in range(ITERS):
        shifted = scores + col_now[:, None]
        top = jnp.max(shifted, axis=0)
        part = top + jnp.log(jnp.sum(jnp.exp(shifted - top[None, :]), axis=0))
        last = step_index == ITERS - 1
        part = lse_over_cent(part, odd, lambda x: beside(x, embeddings) if last else x)
        row_now = -math.log(n_total) - part
        lifted = scores + row_now[None, :]
        top = jnp.max(lifted, axis=1)
        terms = jnp.exp(lifted - top[:, None])
        mass = jnp.sum(terms, axis=1)
        part = top + jnp.log(mass)
        if step_index < ITERS - 1:
            col_now = -math.log(k_total) - lse_over_dp(part, aligned)
    plan = terms.astype(jnp.bfloat16)
    if len(bits) == 2:
        return last_sum(plan, part, mass, row_now, embeddings, math.log(k_total), orders)
    new_centroids, row_out, whole = last_sum_by_vectors(plan, part, mass, row_now, embeddings, chosen, orders, aligned)
    return new_centroids, row_out, -math.log(k_total) - whole


def solution(mesh):
    specs = (P("dp", None), P("cent", None), P("cent"))
    return jax.shard_map(
        on_device,
        mesh=mesh,
        in_specs=specs,
        out_specs=(P("cent", None), P("dp"), P("cent")),
        check_vma=False,
    )
```

```python
import functools
import math

import jax
import jax.numpy as jnp
from jax import lax
from jax.experimental import pallas as pl
from jax.experimental.pallas import tpu as pltpu
from jax.sharding import PartitionSpec as P

ITERS = 3
CHUNKS = 2
LANES = 128
EXTRA = 16
VMEM_BYTES = 24 * 2**20


def bits_of(axis):
    size = lax.axis_size(axis)
    assert size & (size - 1) == 0
    return list(range(size.bit_length() - 1))


def flipped(x, axis, mask):
    size = lax.axis_size(axis)
    return lax.ppermute(x, axis, [(k, k ^ mask) for k in range(size)])


def lse(first, second):
    top = jnp.maximum(first, second)
    return top + jnp.log(jnp.exp(first - top) + jnp.exp(second - top))


def lse_over_dp(x, aligned):
    bits = bits_of("dp")

    def partner(value, mask):
        return aligned(flipped(value, "dp", mask), mask)

    for masks in ([1 << bit for bit in bits[k:k + 2]] for k in range(0, len(bits), 2)):
        if len(masks) == 2:
            far = partner(x, masks[0] | masks[1])
            near = [partner(x, mask) for mask in reversed(masks)]
            x = lse(lax.optimization_barrier(lse(x, far)), lse(*near))
        else:
            x = lse(x, partner(x, masks[0]))
    return x


def lse_over_cent(x, odd, joined_by):
    size = lax.axis_size("cent")
    near, middle, *rest = [1 << bit for bit in bits_of("cent")[1:]]

    def split(value, even_mask, odd_mask):
        return lax.ppermute(value, "cent", [(k, k ^ (odd_mask if k % 2 else even_mask)) for k in range(size)])

    x = lse(x, flipped(x, "cent", 1))
    second = split(x, near, middle)
    first = split(x, near, near | middle)
    x = joined_by(jnp.where(odd, lse(second, first), lse(x, first)))
    for mask in [1] + rest:
        x = lse(x, flipped(x, "cent", mask))
    return x


def column(values):
    lane = lax.broadcasted_iota(jnp.int32, (LANES, LANES), 1)
    diagonal = lane == lax.broadcasted_iota(jnp.int32, (LANES, LANES), 0)
    return jnp.sum(jnp.where(diagonal, values, 0.0), axis=1, keepdims=True)


def quarter_places(orders, quarter):
    ups = [lax.axis_index("dp") >> order[0] & 1 for order in orders]
    sent = [(2 * k + 1 - up) * quarter for k, up in enumerate(ups)]
    return sent + [(2 * k + up) * quarter for k, up in enumerate(ups)]


def place_kernel(chunk, orders, *refs):
    blocks, (out, sent) = refs[:4], refs[-2:]
    quarter, width = blocks[0].shape
    copies = []
    for k, start in enumerate(quarter_places(orders, quarter)):
        rows = pl.ds(pl.multiple_of(start, LANES), quarter)
        copies.append(pltpu.make_async_copy(blocks[k], out.at[rows, pl.ds(chunk * width, width)], sent.at[k]))
        copies[-1].start()
    for copy in copies:
        copy.wait()


def placed(chunk, orders, blocks, shape, so_far):
    vmem = pl.BlockSpec(memory_space=pltpu.VMEM)
    anywhere = pl.BlockSpec(memory_space=pl.ANY)
    return pl.pallas_call(
        functools.partial(place_kernel, chunk, orders),
        out_shape=jax.ShapeDtypeStruct(shape, blocks[0].dtype),
        in_specs=[vmem] * 4 + [anywhere] * len(so_far),
        out_specs=anywhere,
        scratch_shapes=[pltpu.SemaphoreType.DMA((4,))],
        input_output_aliases={4: 0} if so_far else {},
        compiler_params=pltpu.CompilerParams(vmem_limit_bytes=VMEM_BYTES),
    )(*blocks, *so_far)


def means_kernel(is_kept, plan, embeddings, mass, *rest):
    half = plan.shape[0] // 2
    quarter = half // 2
    sums = jnp.dot(plan[pl.ds(is_kept * half, half), :], embeddings[...], preferred_element_type=jnp.float32)
    if is_kept:
        weights, row, out, row_out = rest
        row_out[...] = row[...]
    else:
        out = None
    for block in range(half // LANES):
        factor = 1.0 / column(mass[pl.ds(is_kept * (half // LANES) + block, 1), :])
        if is_kept:
            factor = factor * column(weights[pl.ds(block, 1), :])
        rows = pl.ds(block * LANES % quarter, LANES)
        values = sums[block * LANES:(block + 1) * LANES] * factor
        half_index = block * LANES // quarter
        if is_kept:
            out[half_index, rows, :] = values
        else:
            width = rest[0].shape[1]
            for chunk in range(CHUNKS):
                target = rest[2 * chunk + half_index]
                target[rows, :] = values[:, chunk * width:(chunk + 1) * width].astype(target.dtype)


def means_of(is_kept, plan, embeddings, mass, *rest):
    count, rows_here = plan.shape
    depth = embeddings.shape[1]
    vmem = pl.BlockSpec(memory_space=pltpu.VMEM)
    if is_kept:
        out_shape = (
            jax.ShapeDtypeStruct((2, count // 4, depth), jnp.float32),
            jax.ShapeDtypeStruct((1, rows_here), jnp.float32),
        )
        out_specs = (vmem, pl.BlockSpec((1, rows_here), lambda: (0, 0)))
    else:
        out_shape = [jax.ShapeDtypeStruct((count // 4, depth // CHUNKS), jnp.bfloat16)] * (2 * CHUNKS)
        out_specs = [vmem] * (2 * CHUNKS)
    return pl.pallas_call(
        functools.partial(means_kernel, is_kept),
        out_shape=out_shape,
        in_specs=[vmem] * (3 + len(rest)),
        out_specs=out_specs,
        compiler_params=pltpu.CompilerParams(vmem_limit_bytes=VMEM_BYTES),
        cost_estimate=pl.CostEstimate(
            flops=count * rows_here * depth, bytes_accessed=2 * rows_here * depth, transcendentals=0
        ),
    )(plan, embeddings, mass.reshape(count // LANES, LANES), *rest)


def last_sum_by_vectors(plan, part, mass, row_now, embeddings, chosen, orders, aligned):
    quarter = part.shape[0] // 4
    first, second = orders[0][:2]
    partners = {bit: aligned(flipped(part, "dp", 1 << bit), 1 << bit) for bit in (first, second)}
    sent = means_of(0, plan, embeddings, mass)
    got = [flipped(sent[2 * chunk + k], "dp", 1 << order[0]) for chunk in range(CHUNKS) for k, order in enumerate(orders)]

    def kept_of(lower, upper):
        return jnp.concatenate([lower[2 * quarter:3 * quarter], upper[3 * quarter:]])

    pairs = lax.optimization_barrier([lse(partners[first], part), lse(partners[second], part)])
    pair = kept_of(*pairs)
    weights = jnp.exp(kept_of(part, part) - pair).reshape(2 * quarter // LANES, LANES)
    kept, row_out = means_of(1, plan, embeddings, mass, weights, row_now[None, :])
    weights = jnp.exp(kept_of(partners[first], partners[second]) - pair)

    corner = flipped(partners[first], "dp", 1 << second)

    def exchanged(mine, bit, own, other):
        mine = mine.astype(jnp.bfloat16)
        theirs = flipped(mine, "dp", 1 << bit).astype(jnp.float32)
        mine = mine.astype(jnp.float32)
        lower = chosen(bit, theirs, mine) * chosen(bit, other, own)
        upper = chosen(bit, mine, theirs) * chosen(bit, own, other)
        return (lower + upper).astype(jnp.bfloat16)

    def gathered(mine, order, own, other):
        if len(order) == 1:
            return exchanged(mine, order[0], own, other)
        bit = order[0]
        low, high = jnp.split(mine, 2, axis=0)
        got = flipped(chosen(bit, low, high).astype(jnp.bfloat16), "dp", 1 << bit).astype(jnp.float32)
        own, other = (chosen(bit, high, low) for low, high in (jnp.split(x, 2, axis=0) for x in (own, other)))
        ones = jnp.ones((own.shape[0], 1), jnp.float32)
        done = gathered(chosen(bit, high, low) * own + got * other, order[1:], ones, ones)
        theirs = flipped(done, "dp", 1 << bit)
        return jnp.concatenate([chosen(bit, theirs, done), chosen(bit, done, theirs)], axis=0)

    width = kept.shape[2] // CHUNKS
    shape = (part.shape[0], kept.shape[2])
    mines = []
    for chunk in range(CHUNKS):
        columns = slice(chunk * width, (chunk + 1) * width)
        if chunk > 0:
            mines, kept, weights = lax.optimization_barrier((mines, kept, weights))
        for k in range(2):
            rows = slice(k * quarter, (k + 1) * quarter)
            mines.append(kept[k, :, columns] + got[2 * chunk + k].astype(jnp.float32) * weights[rows, None])

    pairs, partners, corner = lax.optimization_barrier((pairs, partners, corner, mines))[:3]
    corner = aligned(corner, 1 << second)
    whole = lse(pairs[0], lse(corner, partners[second]))
    for bit in orders[0][2:]:
        whole = lse(aligned(flipped(whole, "dp", 1 << bit), 1 << bit), whole)
    pair_other = kept_of(lse(partners[second], corner), lse(partners[first], corner))
    weights_own = jnp.exp(kept_of(*pairs) - kept_of(whole, whole))
    weights_other = jnp.exp(pair_other - kept_of(whole, whole))

    outs = []
    firsts = []
    for chunk in range(CHUNKS):
        dones = []
        for k, order in enumerate(orders):
            rows = slice(k * quarter, (k + 1) * quarter)
            dones.append(gathered(mines[2 * chunk + k], order[1:], weights_own[rows, None], weights_other[rows, None]))
        if chunk < CHUNKS - 1:
            dones, weights_own, weights_other = lax.optimization_barrier((dones, weights_own, weights_other))
        firsts = firsts or dones
        blocks = [flipped(done, "dp", 1 << order[0]) for done, order in zip(dones, orders)] + dones
        outs = [placed(chunk, orders, blocks, shape, outs)]
    whole = lax.optimization_barrier((whole, firsts[0]))[0]
    quarters = jnp.split(whole, 4)
    halves = []
    for k, order in enumerate(orders):
        sent, kept = quarters[k], quarters[2 + k]
        halves += [chosen(order[0], sent, kept), chosen(order[0], kept, sent)]
    return outs[0], row_out.reshape(row_now.shape), jnp.concatenate(halves)


def parts_of(lines):
    row = lax.broadcasted_iota(jnp.int32, (EXTRA, LANES), 0)
    rows = jnp.zeros((EXTRA, LANES), jnp.float32)
    for index, line in enumerate(lines):
        for part in range(3):
            rounded = line.astype(jnp.bfloat16).astype(jnp.float32)
            rows = jnp.where(row == 3 * index + part, rounded, rows)
            line = line - rounded
    return rows.astype(jnp.bfloat16)


def lines_of(message, count):
    rows = message[pl.ds(message.shape[0] - EXTRA, EXTRA), pl.ds(0, LANES)].astype(jnp.float32)
    return [(rows[k:k + 1] + rows[k + 1:k + 2]) + rows[k + 2:k + 3] for k in range(0, 3 * count, 3)]


def put(message, values, lines):
    quarter, width = values.shape
    message[pl.ds(0, quarter), :] = values.astype(message.dtype)
    if lines:
        message[pl.ds(quarter, EXTRA), pl.ds(0, LANES)] = parts_of(lines)
        message[pl.ds(quarter, EXTRA), pl.ds(LANES, width - LANES)] = jnp.zeros((EXTRA, width - LANES), message.dtype)


def columns_of(lines):
    return jnp.concatenate([column(line) for line in lines], axis=0)


def read(ref, start, count):
    return [ref[pl.ds(start + k, 1), :] for k in range(count)]


def write(ref, start, lines):
    for k, line in enumerate(lines):
        ref[pl.ds(start + k, 1), :] = line


def joined(first, second):
    whole = [lse(a, b) for a, b in zip(first, second)]
    return whole, [jnp.exp(a - b) for a, b in zip(first, whole)], [jnp.exp(a - b) for a, b in zip(second, whole)]


def sent_kernel(chunk, plan, embeddings, mass, part, *sent):
    quarter = plan.shape[0] // 2
    count = quarter // LANES
    width = embeddings.shape[1] // CHUNKS
    columns = embeddings[:, pl.ds(chunk * width, width)]
    sums = jnp.dot(plan[...], columns, preferred_element_type=jnp.float32)
    for k in range(2):
        values = sums[k * quarter:(k + 1) * quarter] / columns_of(read(mass, k * count, count))
        put(sent[k], values, read(part, k * count, count) if chunk == 0 else [])


def kept_kernel(plan, embeddings, mass, row, kept, row_out):
    quarter = plan.shape[0] // 2
    count = quarter // LANES
    row_out[...] = row[...]
    sums = jnp.dot(plan[...], embeddings[...], preferred_element_type=jnp.float32)
    for k in range(2):
        kept[k] = sums[k * quarter:(k + 1) * quarter] / columns_of(read(mass, k * count, count))


def pair_kernel(chunk, kept, lower, upper, known, out_lower, out_upper, *weights_out):
    quarter = kept.shape[1]
    count = quarter // LANES
    for k, (got, out) in enumerate(((lower, out_lower), (upper, out_upper))):
        if chunk == 0:
            pair, own, other = joined(read(known, k * count, count), lines_of(got, count))
            write(weights_out[0], 2 * k * count, own + other)
        else:
            pair = []
            own, other = read(known, 2 * k * count, count), read(known, (2 * k + 1) * count, count)
        width = got.shape[1]
        values = kept[k, :, pl.ds(chunk * width, width)] * columns_of(own)
        put(out, values + got[pl.ds(0, quarter), :].astype(jnp.float32) * columns_of(other), pair)


def whole_kernel(chunk, bit, quarter, mine, theirs, *rest):
    count = quarter // LANES
    up = lax.axis_index("dp") >> bit & 1 == 1
    if chunk == 0:
        out, weights_out = rest
        own, other = lines_of(mine, count), lines_of(theirs, count)
        lower = [jnp.where(up, b, a) for a, b in zip(own, other)]
        upper = [jnp.where(up, a, b) for a, b in zip(own, other)]
        whole, low, high = joined(lower, upper)
        write(weights_out, 0, low + high)
    else:
        known, out = rest
        whole = []
        low, high = read(known, 0, count), read(known, count, count)
    own, other = (ref[pl.ds(0, quarter), :].astype(jnp.float32) for ref in (mine, theirs))
    values = jnp.where(up, other, own) * columns_of(low) + jnp.where(up, own, other) * columns_of(high)
    put(out, values, whole)


def place_first_kernel(orders, log_k, lower_sent, upper_sent, lower_kept, upper_kept, out, col_out, sent):
    blocks = (lower_sent, upper_sent, lower_kept, upper_kept)
    quarter = blocks[0].shape[0] - EXTRA
    count = quarter // LANES
    copies = []
    for k, start in enumerate(quarter_places(orders, quarter)):
        rows = pl.ds(pl.multiple_of(start, LANES), quarter)
        source = blocks[k].at[pl.ds(0, quarter)]
        copies.append(pltpu.make_async_copy(source, out.at[rows, pl.ds(0, blocks[k].shape[1])], sent.at[k]))
        copies[-1].start()
    for block, start in zip(blocks, quarter_places(orders, count)):
        write(col_out, start, [-log_k - line for line in lines_of(block, count)])
    for copy in copies:
        copy.wait()


def last_terms(scores, row):
    lifted = scores + row[None, :]
    top = jnp.max(lifted, axis=1)
    terms = jnp.exp(lifted - top[:, None])
    mass = jnp.sum(terms, axis=1)
    return terms.astype(jnp.bfloat16), mass, top + jnp.log(mass)


def last_sum(scores, row_now, embeddings, log_k, orders):
    columns, rows_here = scores.shape
    depth = embeddings.shape[1]
    quarter = columns // 4
    width = depth // CHUNKS
    lines = quarter // LANES
    f32 = jnp.float32
    vmem = pl.BlockSpec(memory_space=pltpu.VMEM)

    def call(kernel, operands, outs, specs=None, flops=0, **options):
        return pl.pallas_call(
            kernel,
            out_shape=outs,
            in_specs=[vmem] * len(operands),
            out_specs=specs or [vmem] * len(outs),
            compiler_params=pltpu.CompilerParams(vmem_limit_bytes=VMEM_BYTES),
            cost_estimate=pl.CostEstimate(flops=flops, bytes_accessed=columns * depth, transcendentals=0),
            **options,
        )(*operands)

    def message(chunk):
        return jax.ShapeDtypeStruct((quarter + (EXTRA if chunk == 0 else 0), width), jnp.bfloat16)

    def table(count):
        return jax.ShapeDtypeStruct((count * lines, LANES), f32)

    flops = columns * rows_here * depth
    chunks = range(CHUNKS)
    plan, mass, part = last_terms(scores[:2 * quarter], row_now)
    operands = [plan, embeddings, mass.reshape(table(2).shape), part.reshape(table(2).shape)]
    sent = []
    for chunk in chunks:
        sent += call(functools.partial(sent_kernel, chunk), operands, [message(chunk)] * 2, flops=flops // CHUNKS)
    got = [flipped(sent[2 * chunk + k], "dp", 1 << orders[k][0]) for chunk in chunks for k in range(2)]
    row_now = lax.optimization_barrier((row_now, sent[:2]))[0]
    plan, mass, part = last_terms(scores[2 * quarter:], row_now)
    row = row_now[None, :]
    kept, row_out = call(
        kept_kernel,
        [plan, embeddings, mass.reshape(table(2).shape), row],
        [jax.ShapeDtypeStruct((2, quarter, depth), f32), jax.ShapeDtypeStruct(row.shape, f32)],
        specs=[vmem, pl.BlockSpec(row.shape, lambda: (0, 0))],
        flops=flops,
    )
    pairs = []
    known = part.reshape(table(2).shape)
    for chunk in chunks:
        outs = [message(chunk)] * 2 + ([table(4)] if chunk == 0 else [])
        results = call(functools.partial(pair_kernel, chunk), [kept, got[2 * chunk], got[2 * chunk + 1], known], outs)
        both = results[:2]
        known = results[2] if chunk == 0 else known
        pairs += both
    known = [None, None]
    out = None
    for chunk in chunks:
        dones = []
        for k, order in enumerate(orders):
            mine = pairs[2 * chunk + k]
            theirs = flipped(mine, "dp", 1 << order[1])
            kernel = functools.partial(whole_kernel, chunk, order[1], quarter)
            if chunk == 0:
                done, known[k] = call(kernel, [mine, theirs], [message(chunk), table(2)])
            else:
                done, = call(kernel, [mine, theirs, known[k]], [message(chunk)])
            dones.append(done)
        blocks = [flipped(done, "dp", 1 << order[0]) for done, order in zip(dones, orders)] + dones
        if chunk == 0:
            out, col_out = call(
                functools.partial(place_first_kernel, orders, log_k),
                blocks,
                [jax.ShapeDtypeStruct((columns, depth), jnp.bfloat16), table(4)],
                specs=[pl.BlockSpec(memory_space=pl.ANY), pl.BlockSpec(table(4).shape, lambda: (0, 0))],
                scratch_shapes=[pltpu.SemaphoreType.DMA((4,))],
            )
        else:
            out = placed(chunk, orders, blocks, (columns, depth), [out])
    return out, row_out.reshape(row_now.shape), col_out.reshape(columns)


def beside_kernel(x, embeddings, out):
    out[...] = x[...]


def beside(x, embeddings):
    lines = (x.shape[0] // LANES, LANES)
    vmem = pl.BlockSpec(memory_space=pltpu.VMEM)
    return pl.pallas_call(
        beside_kernel,
        out_shape=jax.ShapeDtypeStruct(lines, x.dtype),
        in_specs=[vmem, pl.BlockSpec(memory_space=pl.ANY)],
        out_specs=vmem,
        compiler_params=pltpu.CompilerParams(vmem_limit_bytes=VMEM_BYTES),
    )(x.reshape(lines), embeddings).reshape(x.shape)


def on_device(embeddings, centroids, col_start):
    rows_here = embeddings.shape[0]
    cent_here = centroids.shape[0]
    n_total = rows_here * lax.axis_size("dp")
    k_total = cent_here * lax.axis_size("cent")

    bits = bits_of("dp")
    orders = (bits, [bits[1], bits[0]] + bits[2:])
    place = jnp.full((1,), lax.axis_index("dp"), jnp.int32)
    ups = [place >> bit & 1 for bit in bits]
    ups = [up == 1 for up in ups]
    odd = jnp.full((1,), lax.axis_index("cent"), jnp.int32) & 1 == 1
    ups, odd, embeddings, centroids = lax.optimization_barrier((ups, odd, embeddings, centroids))

    def chosen(bit, yes, no):
        return jnp.where(ups[bit].reshape((1,) * yes.ndim), yes, no)

    def sent_and_kept(value):
        quarters = jnp.split(value, 4)
        lows, highs = quarters[0::2], quarters[1::2]
        sent = [chosen(order[0], low, high) for order, low, high in zip(orders, lows, highs)]
        kept = [chosen(order[0], high, low) for order, low, high in zip(orders, lows, highs)]
        return jnp.concatenate(sent + kept)

    def aligned(value, mask):
        quarters = jnp.split(value, 4)
        for k, order in enumerate(orders):
            if mask >> order[0] & 1:
                quarters[k], quarters[2 + k] = quarters[2 + k], quarters[k]
        return jnp.concatenate(quarters)

    scores = lax.dot_general(
        sent_and_kept(centroids), embeddings, (((1,), (1,)), ((), ())), preferred_element_type=jnp.float32
    ) * (1.0 / math.sqrt(embeddings.shape[1]))
    col_now = sent_and_kept(col_start)
    for step_index in range(ITERS):
        shifted = scores + col_now[:, None]
        top = jnp.max(shifted, axis=0)
        part = top + jnp.log(jnp.sum(jnp.exp(shifted - top[None, :]), axis=0))
        last = step_index == ITERS - 1
        part = lse_over_cent(part, odd, lambda x: beside(x, embeddings) if last else x)
        row_now = -math.log(n_total) - part
        if last and len(bits) == 2:
            return last_sum(scores, row_now, embeddings, math.log(k_total), orders)
        plan, mass, part = last_terms(scores, row_now)
        if not last:
            col_now = -math.log(k_total) - lse_over_dp(part, aligned)
    new_centroids, row_out, whole = last_sum_by_vectors(plan, part, mass, row_now, embeddings, chosen, orders, aligned)
    return new_centroids, row_out, -math.log(k_total) - whole


def solution(mesh):
    specs = (P("dp", None), P("cent", None), P("cent"))
    return jax.shard_map(
        on_device,
        mesh=mesh,
        in_specs=specs,
        out_specs=(P("cent", None), P("dp"), P("cent")),
        check_vma=False,
    )
```

```python
import functools
import math

import jax
import jax.numpy as jnp
from jax import lax
from jax.experimental import pallas as pl
from jax.experimental.pallas import tpu as pltpu
from jax.sharding import PartitionSpec as P

ITERS = 3
CHUNKS = 2
LANES = 128
EXTRA = 16
VMEM_BYTES = 24 * 2**20


def bits_of(axis):
    size = lax.axis_size(axis)
    assert size & (size - 1) == 0
    return list(range(size.bit_length() - 1))


def flipped(x, axis, mask):
    size = lax.axis_size(axis)
    return lax.ppermute(x, axis, [(k, k ^ mask) for k in range(size)])


def lse(first, second):
    top = jnp.maximum(first, second)
    return top + jnp.log(jnp.exp(first - top) + jnp.exp(second - top))


def lse_over_dp(x, aligned):
    bits = bits_of("dp")

    def partner(value, mask):
        return aligned(flipped(value, "dp", mask), mask)

    for masks in ([1 << bit for bit in bits[k:k + 2]] for k in range(0, len(bits), 2)):
        if len(masks) == 2:
            far = partner(x, masks[0] | masks[1])
            near = [partner(x, mask) for mask in reversed(masks)]
            x = lse(lax.optimization_barrier(lse(x, far)), lse(*near))
        else:
            x = lse(x, partner(x, masks[0]))
    return x


def lse_over_cent(x, odd, joined_by):
    size = lax.axis_size("cent")
    near, middle, *rest = [1 << bit for bit in bits_of("cent")[1:]]

    def split(value, even_mask, odd_mask):
        return lax.ppermute(value, "cent", [(k, k ^ (odd_mask if k % 2 else even_mask)) for k in range(size)])

    x = lse(x, flipped(x, "cent", 1))
    second = split(x, near, middle)
    first = split(x, near, near | middle)
    x = joined_by(jnp.where(odd, lse(second, first), lse(x, first)))
    for mask in [1] + rest:
        x = lse(x, flipped(x, "cent", mask))
    return x


def column(values):
    lane = lax.broadcasted_iota(jnp.int32, (LANES, LANES), 1)
    diagonal = lane == lax.broadcasted_iota(jnp.int32, (LANES, LANES), 0)
    return jnp.sum(jnp.where(diagonal, values, 0.0), axis=1, keepdims=True)


def quarter_places(orders, quarter):
    ups = [lax.axis_index("dp") >> order[0] & 1 for order in orders]
    sent = [(2 * k + 1 - up) * quarter for k, up in enumerate(ups)]
    return sent + [(2 * k + up) * quarter for k, up in enumerate(ups)]


def place_kernel(chunk, orders, *refs):
    blocks, (out, sent) = refs[:4], refs[-2:]
    quarter, width = blocks[0].shape
    copies = []
    for k, start in enumerate(quarter_places(orders, quarter)):
        rows = pl.ds(pl.multiple_of(start, LANES), quarter)
        copies.append(pltpu.make_async_copy(blocks[k], out.at[rows, pl.ds(chunk * width, width)], sent.at[k]))
        copies[-1].start()
    for copy in copies:
        copy.wait()


def placed(chunk, orders, blocks, shape, so_far):
    vmem = pl.BlockSpec(memory_space=pltpu.VMEM)
    anywhere = pl.BlockSpec(memory_space=pl.ANY)
    return pl.pallas_call(
        functools.partial(place_kernel, chunk, orders),
        out_shape=jax.ShapeDtypeStruct(shape, blocks[0].dtype),
        in_specs=[vmem] * 4 + [anywhere] * len(so_far),
        out_specs=anywhere,
        scratch_shapes=[pltpu.SemaphoreType.DMA((4,))],
        input_output_aliases={4: 0} if so_far else {},
        compiler_params=pltpu.CompilerParams(vmem_limit_bytes=VMEM_BYTES),
    )(*blocks, *so_far)


def means_kernel(is_kept, plan, embeddings, mass, *rest):
    half = plan.shape[0] // 2
    quarter = half // 2
    sums = jnp.dot(plan[pl.ds(is_kept * half, half), :], embeddings[...], preferred_element_type=jnp.float32)
    if is_kept:
        weights, row, out, row_out = rest
        row_out[...] = row[...]
    else:
        out = None
    for block in range(half // LANES):
        factor = 1.0 / column(mass[pl.ds(is_kept * (half // LANES) + block, 1), :])
        if is_kept:
            factor = factor * column(weights[pl.ds(block, 1), :])
        rows = pl.ds(block * LANES % quarter, LANES)
        values = sums[block * LANES:(block + 1) * LANES] * factor
        half_index = block * LANES // quarter
        if is_kept:
            out[half_index, rows, :] = values
        else:
            width = rest[0].shape[1]
            for chunk in range(CHUNKS):
                target = rest[2 * chunk + half_index]
                target[rows, :] = values[:, chunk * width:(chunk + 1) * width].astype(target.dtype)


def means_of(is_kept, plan, embeddings, mass, *rest):
    count, rows_here = plan.shape
    depth = embeddings.shape[1]
    vmem = pl.BlockSpec(memory_space=pltpu.VMEM)
    if is_kept:
        out_shape = (
            jax.ShapeDtypeStruct((2, count // 4, depth), jnp.float32),
            jax.ShapeDtypeStruct((1, rows_here), jnp.float32),
        )
        out_specs = (vmem, pl.BlockSpec((1, rows_here), lambda: (0, 0)))
    else:
        out_shape = [jax.ShapeDtypeStruct((count // 4, depth // CHUNKS), jnp.bfloat16)] * (2 * CHUNKS)
        out_specs = [vmem] * (2 * CHUNKS)
    return pl.pallas_call(
        functools.partial(means_kernel, is_kept),
        out_shape=out_shape,
        in_specs=[vmem] * (3 + len(rest)),
        out_specs=out_specs,
        compiler_params=pltpu.CompilerParams(vmem_limit_bytes=VMEM_BYTES),
        cost_estimate=pl.CostEstimate(
            flops=count * rows_here * depth, bytes_accessed=2 * rows_here * depth, transcendentals=0
        ),
    )(plan, embeddings, mass.reshape(count // LANES, LANES), *rest)


def last_sum_by_vectors(plan, part, mass, row_now, embeddings, chosen, orders, aligned):
    quarter = part.shape[0] // 4
    first, second = orders[0][:2]
    partners = {bit: aligned(flipped(part, "dp", 1 << bit), 1 << bit) for bit in (first, second)}
    sent = means_of(0, plan, embeddings, mass)
    got = [flipped(sent[2 * chunk + k], "dp", 1 << order[0]) for chunk in range(CHUNKS) for k, order in enumerate(orders)]

    def kept_of(lower, upper):
        return jnp.concatenate([lower[2 * quarter:3 * quarter], upper[3 * quarter:]])

    pairs = lax.optimization_barrier([lse(partners[first], part), lse(partners[second], part)])
    pair = kept_of(*pairs)
    weights = jnp.exp(kept_of(part, part) - pair).reshape(2 * quarter // LANES, LANES)
    kept, row_out = means_of(1, plan, embeddings, mass, weights, row_now[None, :])
    weights = jnp.exp(kept_of(partners[first], partners[second]) - pair)

    corner = flipped(partners[first], "dp", 1 << second)

    def exchanged(mine, bit, own, other):
        mine = mine.astype(jnp.bfloat16)
        theirs = flipped(mine, "dp", 1 << bit).astype(jnp.float32)
        mine = mine.astype(jnp.float32)
        lower = chosen(bit, theirs, mine) * chosen(bit, other, own)
        upper = chosen(bit, mine, theirs) * chosen(bit, own, other)
        return (lower + upper).astype(jnp.bfloat16)

    def gathered(mine, order, own, other):
        if len(order) == 1:
            return exchanged(mine, order[0], own, other)
        bit = order[0]
        low, high = jnp.split(mine, 2, axis=0)
        got = flipped(chosen(bit, low, high).astype(jnp.bfloat16), "dp", 1 << bit).astype(jnp.float32)
        own, other = (chosen(bit, high, low) for low, high in (jnp.split(x, 2, axis=0) for x in (own, other)))
        ones = jnp.ones((own.shape[0], 1), jnp.float32)
        done = gathered(chosen(bit, high, low) * own + got * other, order[1:], ones, ones)
        theirs = flipped(done, "dp", 1 << bit)
        return jnp.concatenate([chosen(bit, theirs, done), chosen(bit, done, theirs)], axis=0)

    width = kept.shape[2] // CHUNKS
    shape = (part.shape[0], kept.shape[2])
    mines = []
    for chunk in range(CHUNKS):
        columns = slice(chunk * width, (chunk + 1) * width)
        if chunk > 0:
            mines, kept, weights = lax.optimization_barrier((mines, kept, weights))
        for k in range(2):
            rows = slice(k * quarter, (k + 1) * quarter)
            mines.append(kept[k, :, columns] + got[2 * chunk + k].astype(jnp.float32) * weights[rows, None])

    pairs, partners, corner = lax.optimization_barrier((pairs, partners, corner, mines))[:3]
    corner = aligned(corner, 1 << second)
    whole = lse(pairs[0], lse(corner, partners[second]))
    for bit in orders[0][2:]:
        whole = lse(aligned(flipped(whole, "dp", 1 << bit), 1 << bit), whole)
    pair_other = kept_of(lse(partners[second], corner), lse(partners[first], corner))
    weights_own = jnp.exp(kept_of(*pairs) - kept_of(whole, whole))
    weights_other = jnp.exp(pair_other - kept_of(whole, whole))

    outs = []
    firsts = []
    for chunk in range(CHUNKS):
        dones = []
        for k, order in enumerate(orders):
            rows = slice(k * quarter, (k + 1) * quarter)
            dones.append(gathered(mines[2 * chunk + k], order[1:], weights_own[rows, None], weights_other[rows, None]))
        if chunk < CHUNKS - 1:
            dones, weights_own, weights_other = lax.optimization_barrier((dones, weights_own, weights_other))
        firsts = firsts or dones
        blocks = [flipped(done, "dp", 1 << order[0]) for done, order in zip(dones, orders)] + dones
        outs = [placed(chunk, orders, blocks, shape, outs)]
    whole = lax.optimization_barrier((whole, firsts[0]))[0]
    quarters = jnp.split(whole, 4)
    halves = []
    for k, order in enumerate(orders):
        sent, kept = quarters[k], quarters[2 + k]
        halves += [chosen(order[0], sent, kept), chosen(order[0], kept, sent)]
    return outs[0], row_out.reshape(row_now.shape), jnp.concatenate(halves)


def parts_of(lines):
    row = lax.broadcasted_iota(jnp.int32, (EXTRA, LANES), 0)
    rows = jnp.zeros((EXTRA, LANES), jnp.float32)
    for index, line in enumerate(lines):
        for part in range(3):
            rounded = line.astype(jnp.bfloat16).astype(jnp.float32)
            rows = jnp.where(row == 3 * index + part, rounded, rows)
            line = line - rounded
    return rows.astype(jnp.bfloat16)


def lines_of(message, count):
    rows = message[pl.ds(message.shape[0] - EXTRA, EXTRA), pl.ds(0, LANES)].astype(jnp.float32)
    return [(rows[k:k + 1] + rows[k + 1:k + 2]) + rows[k + 2:k + 3] for k in range(0, 3 * count, 3)]


def put(message, values, lines):
    quarter, width = values.shape
    message[pl.ds(0, quarter), :] = values.astype(message.dtype)
    if lines:
        message[pl.ds(quarter, EXTRA), pl.ds(0, LANES)] = parts_of(lines)
        message[pl.ds(quarter, EXTRA), pl.ds(LANES, width - LANES)] = jnp.zeros((EXTRA, width - LANES), message.dtype)


def columns_of(lines):
    return jnp.concatenate([column(line) for line in lines], axis=0)


def read(ref, start, count):
    return [ref[pl.ds(start + k, 1), :] for k in range(count)]


def write(ref, start, lines):
    for k, line in enumerate(lines):
        ref[pl.ds(start + k, 1), :] = line


def joined(first, second):
    whole = [lse(a, b) for a, b in zip(first, second)]
    return whole, [jnp.exp(a - b) for a, b in zip(first, whole)], [jnp.exp(a - b) for a, b in zip(second, whole)]


def sent_kernel(chunk, plan, embeddings, mass, part, *sent):
    quarter = plan.shape[0] // 2
    count = quarter // LANES
    width = embeddings.shape[1] // CHUNKS
    columns = embeddings[:, pl.ds(chunk * width, width)]
    sums = jnp.dot(plan[...], columns, preferred_element_type=jnp.float32)
    for k in range(2):
        values = sums[k * quarter:(k + 1) * quarter] / columns_of(read(mass, k * count, count))
        put(sent[k], values, read(part, k * count, count) if chunk == 0 else [])


def kept_kernel(plan, embeddings, mass, kept):
    quarter = plan.shape[0] // 2
    count = quarter // LANES
    sums = jnp.dot(plan[...], embeddings[...], preferred_element_type=jnp.float32)
    for k in range(2):
        kept[k] = sums[k * quarter:(k + 1) * quarter] / columns_of(read(mass, k * count, count))


def pair_kernel(chunk, kept, lower, upper, known, out_lower, out_upper, *weights_out):
    quarter = kept.shape[1]
    count = quarter // LANES
    for k, (got, out) in enumerate(((lower, out_lower), (upper, out_upper))):
        if chunk == 0:
            pair, own, other = joined(read(known, k * count, count), lines_of(got, count))
            write(weights_out[0], 2 * k * count, own + other)
        else:
            pair = []
            own, other = read(known, 2 * k * count, count), read(known, (2 * k + 1) * count, count)
        width = got.shape[1]
        values = kept[k, :, pl.ds(chunk * width, width)] * columns_of(own)
        put(out, values + got[pl.ds(0, quarter), :].astype(jnp.float32) * columns_of(other), pair)


def whole_kernel(chunk, bit, quarter, mine, theirs, *rest):
    count = quarter // LANES
    up = lax.axis_index("dp") >> bit & 1 == 1
    if chunk == 0:
        out, weights_out = rest
        own, other = lines_of(mine, count), lines_of(theirs, count)
        lower = [jnp.where(up, b, a) for a, b in zip(own, other)]
        upper = [jnp.where(up, a, b) for a, b in zip(own, other)]
        whole, low, high = joined(lower, upper)
        write(weights_out, 0, low + high)
    else:
        known, out = rest
        whole = []
        low, high = read(known, 0, count), read(known, count, count)
    own, other = (ref[pl.ds(0, quarter), :].astype(jnp.float32) for ref in (mine, theirs))
    values = jnp.where(up, other, own) * columns_of(low) + jnp.where(up, own, other) * columns_of(high)
    put(out, values, whole)


def place_first_kernel(orders, log_k, lower_sent, upper_sent, lower_kept, upper_kept, row, out, col_out, row_out, sent):
    blocks = (lower_sent, upper_sent, lower_kept, upper_kept)
    quarter = blocks[0].shape[0] - EXTRA
    count = quarter // LANES
    copies = []
    for k, start in enumerate(quarter_places(orders, quarter)):
        rows = pl.ds(pl.multiple_of(start, LANES), quarter)
        source = blocks[k].at[pl.ds(0, quarter)]
        copies.append(pltpu.make_async_copy(source, out.at[rows, pl.ds(0, blocks[k].shape[1])], sent.at[k]))
        copies[-1].start()
    row_out[...] = row[...]
    for block, start in zip(blocks, quarter_places(orders, count)):
        write(col_out, start, [-log_k - line for line in lines_of(block, count)])
    for copy in copies:
        copy.wait()


def last_terms(scores, row):
    lifted = scores + row[None, :]
    top = jnp.max(lifted, axis=1)
    terms = jnp.exp(lifted - top[:, None])
    mass = jnp.sum(terms, axis=1)
    return terms.astype(jnp.bfloat16), mass, top + jnp.log(mass)


def last_sum(scores, row_now, embeddings, log_k, orders):
    columns, rows_here = scores.shape
    depth = embeddings.shape[1]
    quarter = columns // 4
    width = depth // CHUNKS
    lines = quarter // LANES
    f32 = jnp.float32
    vmem = pl.BlockSpec(memory_space=pltpu.VMEM)

    def call(kernel, operands, outs, specs=None, flops=0, **options):
        return pl.pallas_call(
            kernel,
            out_shape=outs,
            in_specs=[vmem] * len(operands),
            out_specs=specs or [vmem] * len(outs),
            compiler_params=pltpu.CompilerParams(vmem_limit_bytes=VMEM_BYTES),
            cost_estimate=pl.CostEstimate(flops=flops, bytes_accessed=columns * depth, transcendentals=0),
            **options,
        )(*operands)

    def message(chunk):
        return jax.ShapeDtypeStruct((quarter + (EXTRA if chunk == 0 else 0), width), jnp.bfloat16)

    def table(count):
        return jax.ShapeDtypeStruct((count * lines, LANES), f32)

    flops = columns * rows_here * depth
    chunks = range(CHUNKS)
    plan, mass, part = last_terms(scores[:2 * quarter], row_now)
    operands = [plan, embeddings, mass.reshape(table(2).shape), part.reshape(table(2).shape)]
    sent = []
    for chunk in chunks:
        sent += call(functools.partial(sent_kernel, chunk), operands, [message(chunk)] * 2, flops=flops // CHUNKS)
    got = [flipped(sent[2 * chunk + k], "dp", 1 << orders[k][0]) for chunk in chunks for k in range(2)]
    row_now = lax.optimization_barrier((row_now, sent[:2]))[0]
    plan, mass, part = last_terms(scores[2 * quarter:], row_now)
    row = row_now[None, :]
    kept, = call(
        kept_kernel,
        [plan, embeddings, mass.reshape(table(2).shape)],
        [jax.ShapeDtypeStruct((2, quarter, depth), f32)],
        flops=flops,
    )
    pairs = []
    known = part.reshape(table(2).shape)
    for chunk in chunks:
        outs = [message(chunk)] * 2 + ([table(4)] if chunk == 0 else [])
        results = call(functools.partial(pair_kernel, chunk), [kept, got[2 * chunk], got[2 * chunk + 1], known], outs)
        both = results[:2]
        known = results[2] if chunk == 0 else known
        pairs += both
    known = [None, None]
    out = None
    for chunk in chunks:
        dones = []
        for k, order in enumerate(orders):
            mine = pairs[2 * chunk + k]
            theirs = flipped(mine, "dp", 1 << order[1])
            kernel = functools.partial(whole_kernel, chunk, order[1], quarter)
            if chunk == 0:
                done, known[k] = call(kernel, [mine, theirs], [message(chunk), table(2)])
            else:
                done, = call(kernel, [mine, theirs, known[k]], [message(chunk)])
            dones.append(done)
        blocks = [flipped(done, "dp", 1 << order[0]) for done, order in zip(dones, orders)] + dones
        if chunk == 0:
            whole = [table(4), jax.ShapeDtypeStruct(row.shape, f32)]
            out, col_out, row_out = call(
                functools.partial(place_first_kernel, orders, log_k),
                blocks + [row],
                [jax.ShapeDtypeStruct((columns, depth), jnp.bfloat16)] + whole,
                specs=[pl.BlockSpec(memory_space=pl.ANY)] + [pl.BlockSpec(x.shape, lambda: (0, 0)) for x in whole],
                scratch_shapes=[pltpu.SemaphoreType.DMA((4,))],
            )
        else:
            out = placed(chunk, orders, blocks, (columns, depth), [out])
    return out, row_out.reshape(row_now.shape), col_out.reshape(columns)


def beside_kernel(x, embeddings, out):
    out[...] = x[...]


def beside(x, embeddings):
    lines = (x.shape[0] // LANES, LANES)
    vmem = pl.BlockSpec(memory_space=pltpu.VMEM)
    return pl.pallas_call(
        beside_kernel,
        out_shape=jax.ShapeDtypeStruct(lines, x.dtype),
        in_specs=[vmem, pl.BlockSpec(memory_space=pl.ANY)],
        out_specs=vmem,
        compiler_params=pltpu.CompilerParams(vmem_limit_bytes=VMEM_BYTES),
    )(x.reshape(lines), embeddings).reshape(x.shape)


def on_device(embeddings, centroids, col_start):
    rows_here = embeddings.shape[0]
    cent_here = centroids.shape[0]
    n_total = rows_here * lax.axis_size("dp")
    k_total = cent_here * lax.axis_size("cent")

    bits = bits_of("dp")
    orders = (bits, [bits[1], bits[0]] + bits[2:])
    place = jnp.full((1,), lax.axis_index("dp"), jnp.int32)
    ups = [place >> bit & 1 for bit in bits]
    ups = [up == 1 for up in ups]
    odd = jnp.full((1,), lax.axis_index("cent"), jnp.int32) & 1 == 1
    ups, odd, embeddings, centroids = lax.optimization_barrier((ups, odd, embeddings, centroids))

    def chosen(bit, yes, no):
        return jnp.where(ups[bit].reshape((1,) * yes.ndim), yes, no)

    def sent_and_kept(value):
        quarters = jnp.split(value, 4)
        lows, highs = quarters[0::2], quarters[1::2]
        sent = [chosen(order[0], low, high) for order, low, high in zip(orders, lows, highs)]
        kept = [chosen(order[0], high, low) for order, low, high in zip(orders, lows, highs)]
        return jnp.concatenate(sent + kept)

    def aligned(value, mask):
        quarters = jnp.split(value, 4)
        for k, order in enumerate(orders):
            if mask >> order[0] & 1:
                quarters[k], quarters[2 + k] = quarters[2 + k], quarters[k]
        return jnp.concatenate(quarters)

    scores = lax.dot_general(
        sent_and_kept(centroids), embeddings, (((1,), (1,)), ((), ())), preferred_element_type=jnp.float32
    ) * (1.0 / math.sqrt(embeddings.shape[1]))
    col_now = sent_and_kept(col_start)
    for step_index in range(ITERS):
        shifted = scores + col_now[:, None]
        top = jnp.max(shifted, axis=0)
        part = top + jnp.log(jnp.sum(jnp.exp(shifted - top[None, :]), axis=0))
        last = step_index == ITERS - 1
        part = lse_over_cent(part, odd, lambda x: beside(x, embeddings) if last else x)
        row_now = -math.log(n_total) - part
        if last and len(bits) == 2:
            return last_sum(scores, row_now, embeddings, math.log(k_total), orders)
        plan, mass, part = last_terms(scores, row_now)
        if not last:
            col_now = -math.log(k_total) - lse_over_dp(part, aligned)
    new_centroids, row_out, whole = last_sum_by_vectors(plan, part, mass, row_now, embeddings, chosen, orders, aligned)
    return new_centroids, row_out, -math.log(k_total) - whole


def solution(mesh):
    specs = (P("dp", None), P("cent", None), P("cent"))
    return jax.shard_map(
        on_device,
        mesh=mesh,
        in_specs=specs,
        out_specs=(P("cent", None), P("dp"), P("cent")),
        check_vma=False,
    )
```

```python
import functools
import math

import jax
import jax.numpy as jnp
from jax import lax
from jax.experimental import pallas as pl
from jax.experimental.pallas import tpu as pltpu
from jax.sharding import PartitionSpec as P

ITERS = 3
CHUNKS = 2
LANES = 128
EXTRA = 16
VMEM_BYTES = 24 * 2**20


def bits_of(axis):
    size = lax.axis_size(axis)
    assert size & (size - 1) == 0
    return list(range(size.bit_length() - 1))


def flipped(x, axis, mask):
    size = lax.axis_size(axis)
    return lax.ppermute(x, axis, [(k, k ^ mask) for k in range(size)])


def lse(first, second):
    top = jnp.maximum(first, second)
    return top + jnp.log(jnp.exp(first - top) + jnp.exp(second - top))


def lse_over_dp(x, aligned, joined_by):
    bits = bits_of("dp")

    def partner(value, mask):
        return aligned(flipped(value, "dp", mask), mask)

    for masks in ([1 << bit for bit in bits[k:k + 2]] for k in range(0, len(bits), 2)):
        if len(masks) == 2:
            far = partner(x, masks[0] | masks[1])
            near = [partner(x, mask) for mask in reversed(masks)]
            x = lse(joined_by(lax.optimization_barrier(lse(x, far))), lse(*near))
        else:
            x = lse(x, partner(x, masks[0]))
    return x


def lse_over_cent(x, odd):
    size = lax.axis_size("cent")
    near, middle, *rest = [1 << bit for bit in bits_of("cent")[1:]]

    def split(value, even_mask, odd_mask):
        return lax.ppermute(value, "cent", [(k, k ^ (odd_mask if k % 2 else even_mask)) for k in range(size)])

    x = lse(x, flipped(x, "cent", 1))
    second = split(x, near, middle)
    first = split(x, near, near | middle)
    x = jnp.where(odd, lse(second, first), lse(x, first))
    for mask in [1] + rest:
        x = lse(x, flipped(x, "cent", mask))
    return x


def column(values):
    lane = lax.broadcasted_iota(jnp.int32, (LANES, LANES), 1)
    diagonal = lane == lax.broadcasted_iota(jnp.int32, (LANES, LANES), 0)
    return jnp.sum(jnp.where(diagonal, values, 0.0), axis=1, keepdims=True)


def quarter_places(orders, quarter):
    ups = [lax.axis_index("dp") >> order[0] & 1 for order in orders]
    sent = [(2 * k + 1 - up) * quarter for k, up in enumerate(ups)]
    return sent + [(2 * k + up) * quarter for k, up in enumerate(ups)]


def place_kernel(chunk, orders, *refs):
    blocks, (out, sent) = refs[:4], refs[-2:]
    quarter, width = blocks[0].shape
    copies = []
    for k, start in enumerate(quarter_places(orders, quarter)):
        rows = pl.ds(pl.multiple_of(start, LANES), quarter)
        copies.append(pltpu.make_async_copy(blocks[k], out.at[rows, pl.ds(chunk * width, width)], sent.at[k]))
        copies[-1].start()
    for copy in copies:
        copy.wait()


def placed(chunk, orders, blocks, shape, so_far):
    vmem = pl.BlockSpec(memory_space=pltpu.VMEM)
    anywhere = pl.BlockSpec(memory_space=pl.ANY)
    return pl.pallas_call(
        functools.partial(place_kernel, chunk, orders),
        out_shape=jax.ShapeDtypeStruct(shape, blocks[0].dtype),
        in_specs=[vmem] * 4 + [anywhere] * len(so_far),
        out_specs=anywhere,
        scratch_shapes=[pltpu.SemaphoreType.DMA((4,))],
        input_output_aliases={4: 0} if so_far else {},
        compiler_params=pltpu.CompilerParams(vmem_limit_bytes=VMEM_BYTES),
    )(*blocks, *so_far)


def means_kernel(is_kept, plan, embeddings, mass, *rest):
    half = plan.shape[0] // 2
    quarter = half // 2
    sums = jnp.dot(plan[pl.ds(is_kept * half, half), :], embeddings[...], preferred_element_type=jnp.float32)
    if is_kept:
        weights, row, out, row_out = rest
        row_out[...] = row[...]
    else:
        out = None
    for block in range(half // LANES):
        factor = 1.0 / column(mass[pl.ds(is_kept * (half // LANES) + block, 1), :])
        if is_kept:
            factor = factor * column(weights[pl.ds(block, 1), :])
        rows = pl.ds(block * LANES % quarter, LANES)
        values = sums[block * LANES:(block + 1) * LANES] * factor
        half_index = block * LANES // quarter
        if is_kept:
            out[half_index, rows, :] = values
        else:
            width = rest[0].shape[1]
            for chunk in range(CHUNKS):
                target = rest[2 * chunk + half_index]
                target[rows, :] = values[:, chunk * width:(chunk + 1) * width].astype(target.dtype)


def means_of(is_kept, plan, embeddings, mass, *rest):
    count, rows_here = plan.shape
    depth = embeddings.shape[1]
    vmem = pl.BlockSpec(memory_space=pltpu.VMEM)
    if is_kept:
        out_shape = (
            jax.ShapeDtypeStruct((2, count // 4, depth), jnp.float32),
            jax.ShapeDtypeStruct((1, rows_here), jnp.float32),
        )
        out_specs = (vmem, pl.BlockSpec((1, rows_here), lambda: (0, 0)))
    else:
        out_shape = [jax.ShapeDtypeStruct((count // 4, depth // CHUNKS), jnp.bfloat16)] * (2 * CHUNKS)
        out_specs = [vmem] * (2 * CHUNKS)
    return pl.pallas_call(
        functools.partial(means_kernel, is_kept),
        out_shape=out_shape,
        in_specs=[vmem] * (3 + len(rest)),
        out_specs=out_specs,
        compiler_params=pltpu.CompilerParams(vmem_limit_bytes=VMEM_BYTES),
        cost_estimate=pl.CostEstimate(
            flops=count * rows_here * depth, bytes_accessed=2 * rows_here * depth, transcendentals=0
        ),
    )(plan, embeddings, mass.reshape(count // LANES, LANES), *rest)


def last_sum_by_vectors(plan, part, mass, row_now, embeddings, chosen, orders, aligned):
    quarter = part.shape[0] // 4
    first, second = orders[0][:2]
    partners = {bit: aligned(flipped(part, "dp", 1 << bit), 1 << bit) for bit in (first, second)}
    sent = means_of(0, plan, embeddings, mass)
    got = [flipped(sent[2 * chunk + k], "dp", 1 << order[0]) for chunk in range(CHUNKS) for k, order in enumerate(orders)]

    def kept_of(lower, upper):
        return jnp.concatenate([lower[2 * quarter:3 * quarter], upper[3 * quarter:]])

    pairs = lax.optimization_barrier([lse(partners[first], part), lse(partners[second], part)])
    pair = kept_of(*pairs)
    weights = jnp.exp(kept_of(part, part) - pair).reshape(2 * quarter // LANES, LANES)
    kept, row_out = means_of(1, plan, embeddings, mass, weights, row_now[None, :])
    weights = jnp.exp(kept_of(partners[first], partners[second]) - pair)

    corner = flipped(partners[first], "dp", 1 << second)

    def exchanged(mine, bit, own, other):
        mine = mine.astype(jnp.bfloat16)
        theirs = flipped(mine, "dp", 1 << bit).astype(jnp.float32)
        mine = mine.astype(jnp.float32)
        lower = chosen(bit, theirs, mine) * chosen(bit, other, own)
        upper = chosen(bit, mine, theirs) * chosen(bit, own, other)
        return (lower + upper).astype(jnp.bfloat16)

    def gathered(mine, order, own, other):
        if len(order) == 1:
            return exchanged(mine, order[0], own, other)
        bit = order[0]
        low, high = jnp.split(mine, 2, axis=0)
        got = flipped(chosen(bit, low, high).astype(jnp.bfloat16), "dp", 1 << bit).astype(jnp.float32)
        own, other = (chosen(bit, high, low) for low, high in (jnp.split(x, 2, axis=0) for x in (own, other)))
        ones = jnp.ones((own.shape[0], 1), jnp.float32)
        done = gathered(chosen(bit, high, low) * own + got * other, order[1:], ones, ones)
        theirs = flipped(done, "dp", 1 << bit)
        return jnp.concatenate([chosen(bit, theirs, done), chosen(bit, done, theirs)], axis=0)

    width = kept.shape[2] // CHUNKS
    shape = (part.shape[0], kept.shape[2])
    mines = []
    for chunk in range(CHUNKS):
        columns = slice(chunk * width, (chunk + 1) * width)
        if chunk > 0:
            mines, kept, weights = lax.optimization_barrier((mines, kept, weights))
        for k in range(2):
            rows = slice(k * quarter, (k + 1) * quarter)
            mines.append(kept[k, :, columns] + got[2 * chunk + k].astype(jnp.float32) * weights[rows, None])

    pairs, partners, corner = lax.optimization_barrier((pairs, partners, corner, mines))[:3]
    corner = aligned(corner, 1 << second)
    whole = lse(pairs[0], lse(corner, partners[second]))
    for bit in orders[0][2:]:
        whole = lse(aligned(flipped(whole, "dp", 1 << bit), 1 << bit), whole)
    pair_other = kept_of(lse(partners[second], corner), lse(partners[first], corner))
    weights_own = jnp.exp(kept_of(*pairs) - kept_of(whole, whole))
    weights_other = jnp.exp(pair_other - kept_of(whole, whole))

    outs = []
    firsts = []
    for chunk in range(CHUNKS):
        dones = []
        for k, order in enumerate(orders):
            rows = slice(k * quarter, (k + 1) * quarter)
            dones.append(gathered(mines[2 * chunk + k], order[1:], weights_own[rows, None], weights_other[rows, None]))
        if chunk < CHUNKS - 1:
            dones, weights_own, weights_other = lax.optimization_barrier((dones, weights_own, weights_other))
        firsts = firsts or dones
        blocks = [flipped(done, "dp", 1 << order[0]) for done, order in zip(dones, orders)] + dones
        outs = [placed(chunk, orders, blocks, shape, outs)]
    whole = lax.optimization_barrier((whole, firsts[0]))[0]
    quarters = jnp.split(whole, 4)
    halves = []
    for k, order in enumerate(orders):
        sent, kept = quarters[k], quarters[2 + k]
        halves += [chosen(order[0], sent, kept), chosen(order[0], kept, sent)]
    return outs[0], row_out.reshape(row_now.shape), jnp.concatenate(halves)


def parts_of(lines):
    row = lax.broadcasted_iota(jnp.int32, (EXTRA, LANES), 0)
    rows = jnp.zeros((EXTRA, LANES), jnp.float32)
    for index, line in enumerate(lines):
        for part in range(3):
            rounded = line.astype(jnp.bfloat16).astype(jnp.float32)
            rows = jnp.where(row == 3 * index + part, rounded, rows)
            line = line - rounded
    return rows.astype(jnp.bfloat16)


def lines_of(message, count):
    rows = message[pl.ds(message.shape[0] - EXTRA, EXTRA), pl.ds(0, LANES)].astype(jnp.float32)
    return [(rows[k:k + 1] + rows[k + 1:k + 2]) + rows[k + 2:k + 3] for k in range(0, 3 * count, 3)]


def put(message, values, lines):
    quarter, width = values.shape
    message[pl.ds(0, quarter), :] = values.astype(message.dtype)
    if lines:
        message[pl.ds(quarter, EXTRA), pl.ds(0, LANES)] = parts_of(lines)
        message[pl.ds(quarter, EXTRA), pl.ds(LANES, width - LANES)] = jnp.zeros((EXTRA, width - LANES), message.dtype)


def columns_of(lines):
    return jnp.concatenate([column(line) for line in lines], axis=0)


def read(ref, start, count):
    return [ref[pl.ds(start + k, 1), :] for k in range(count)]


def write(ref, start, lines):
    for k, line in enumerate(lines):
        ref[pl.ds(start + k, 1), :] = line


def joined(first, second):
    whole = [lse(a, b) for a, b in zip(first, second)]
    return whole, [jnp.exp(a - b) for a, b in zip(first, whole)], [jnp.exp(a - b) for a, b in zip(second, whole)]


def sent_kernel(chunk, plan, embeddings, mass, part, *sent):
    quarter = plan.shape[0] // 2
    count = quarter // LANES
    width = embeddings.shape[1] // CHUNKS
    columns = embeddings[:, pl.ds(chunk * width, width)]
    sums = jnp.dot(plan[...], columns, preferred_element_type=jnp.float32)
    for k in range(2):
        values = sums[k * quarter:(k + 1) * quarter] / columns_of(read(mass, k * count, count))
        put(sent[k], values, read(part, k * count, count) if chunk == 0 else [])


def kept_kernel(plan, embeddings, mass, kept):
    quarter = plan.shape[0] // 2
    count = quarter // LANES
    sums = jnp.dot(plan[...], embeddings[...], preferred_element_type=jnp.float32)
    for k in range(2):
        kept[k] = sums[k * quarter:(k + 1) * quarter] / columns_of(read(mass, k * count, count))


def pair_kernel(chunk, kept, lower, upper, known, out_lower, out_upper, *weights_out):
    quarter = kept.shape[1]
    count = quarter // LANES
    for k, (got, out) in enumerate(((lower, out_lower), (upper, out_upper))):
        if chunk == 0:
            pair, own, other = joined(read(known, k * count, count), lines_of(got, count))
            write(weights_out[0], 2 * k * count, own + other)
        else:
            pair = []
            own, other = read(known, 2 * k * count, count), read(known, (2 * k + 1) * count, count)
        width = got.shape[1]
        values = kept[k, :, pl.ds(chunk * width, width)] * columns_of(own)
        put(out, values + got[pl.ds(0, quarter), :].astype(jnp.float32) * columns_of(other), pair)


def whole_kernel(chunk, bit, quarter, mine, theirs, *rest):
    count = quarter // LANES
    up = lax.axis_index("dp") >> bit & 1 == 1
    if chunk == 0:
        out, weights_out = rest
        own, other = lines_of(mine, count), lines_of(theirs, count)
        lower = [jnp.where(up, b, a) for a, b in zip(own, other)]
        upper = [jnp.where(up, a, b) for a, b in zip(own, other)]
        whole, low, high = joined(lower, upper)
        write(weights_out, 0, low + high)
    else:
        known, out = rest
        whole = []
        low, high = read(known, 0, count), read(known, count, count)
    own, other = (ref[pl.ds(0, quarter), :].astype(jnp.float32) for ref in (mine, theirs))
    values = jnp.where(up, other, own) * columns_of(low) + jnp.where(up, own, other) * columns_of(high)
    put(out, values, whole)


def place_first_kernel(orders, log_k, lower_sent, upper_sent, lower_kept, upper_kept, row, out, col_out, row_out, sent):
    blocks = (lower_sent, upper_sent, lower_kept, upper_kept)
    quarter = blocks[0].shape[0] - EXTRA
    count = quarter // LANES
    copies = []
    for k, start in enumerate(quarter_places(orders, quarter)):
        rows = pl.ds(pl.multiple_of(start, LANES), quarter)
        source = blocks[k].at[pl.ds(0, quarter)]
        copies.append(pltpu.make_async_copy(source, out.at[rows, pl.ds(0, blocks[k].shape[1])], sent.at[k]))
        copies[-1].start()
    row_out[...] = row[...]
    for block, start in zip(blocks, quarter_places(orders, count)):
        write(col_out, start, [-log_k - line for line in lines_of(block, count)])
    for copy in copies:
        copy.wait()


def last_terms(scores, row):
    lifted = scores + row[None, :]
    top = jnp.max(lifted, axis=1)
    terms = jnp.exp(lifted - top[:, None])
    mass = jnp.sum(terms, axis=1)
    return terms.astype(jnp.bfloat16), mass, top + jnp.log(mass)


def last_sum(scores, row_now, embeddings, log_k, orders):
    columns, rows_here = scores.shape
    depth = embeddings.shape[1]
    quarter = columns // 4
    width = depth // CHUNKS
    lines = quarter // LANES
    f32 = jnp.float32
    vmem = pl.BlockSpec(memory_space=pltpu.VMEM)

    def call(kernel, operands, outs, specs=None, flops=0, **options):
        return pl.pallas_call(
            kernel,
            out_shape=outs,
            in_specs=[vmem] * len(operands),
            out_specs=specs or [vmem] * len(outs),
            compiler_params=pltpu.CompilerParams(vmem_limit_bytes=VMEM_BYTES),
            cost_estimate=pl.CostEstimate(flops=flops, bytes_accessed=columns * depth, transcendentals=0),
            **options,
        )(*operands)

    def message(chunk):
        return jax.ShapeDtypeStruct((quarter + (EXTRA if chunk == 0 else 0), width), jnp.bfloat16)

    def table(count):
        return jax.ShapeDtypeStruct((count * lines, LANES), f32)

    flops = columns * rows_here * depth
    chunks = range(CHUNKS)
    plan, mass, part = last_terms(scores[:2 * quarter], row_now)
    operands = [plan, embeddings, mass.reshape(table(2).shape), part.reshape(table(2).shape)]
    sent = []
    for chunk in chunks:
        sent += call(functools.partial(sent_kernel, chunk), operands, [message(chunk)] * 2, flops=flops // CHUNKS)
    got = [flipped(sent[2 * chunk + k], "dp", 1 << orders[k][0]) for chunk in chunks for k in range(2)]
    row_now = lax.optimization_barrier((row_now, sent[:2]))[0]
    plan, mass, part = last_terms(scores[2 * quarter:], row_now)
    row = row_now[None, :]
    kept, = call(
        kept_kernel,
        [plan, embeddings, mass.reshape(table(2).shape)],
        [jax.ShapeDtypeStruct((2, quarter, depth), f32)],
        flops=flops,
    )
    pairs = []
    known = part.reshape(table(2).shape)
    for chunk in chunks:
        outs = [message(chunk)] * 2 + ([table(4)] if chunk == 0 else [])
        results = call(functools.partial(pair_kernel, chunk), [kept, got[2 * chunk], got[2 * chunk + 1], known], outs)
        both = results[:2]
        known = results[2] if chunk == 0 else known
        pairs += both
    known = [None, None]
    out = None
    for chunk in chunks:
        dones = []
        for k, order in enumerate(orders):
            mine = pairs[2 * chunk + k]
            theirs = flipped(mine, "dp", 1 << order[1])
            kernel = functools.partial(whole_kernel, chunk, order[1], quarter)
            if chunk == 0:
                done, known[k] = call(kernel, [mine, theirs], [message(chunk), table(2)])
            else:
                done, = call(kernel, [mine, theirs, known[k]], [message(chunk)])
            dones.append(done)
        blocks = [flipped(done, "dp", 1 << order[0]) for done, order in zip(dones, orders)] + dones
        if chunk == 0:
            whole = [table(4), jax.ShapeDtypeStruct(row.shape, f32)]
            out, col_out, row_out = call(
                functools.partial(place_first_kernel, orders, log_k),
                blocks + [row],
                [jax.ShapeDtypeStruct((columns, depth), jnp.bfloat16)] + whole,
                specs=[pl.BlockSpec(memory_space=pl.ANY)] + [pl.BlockSpec(x.shape, lambda: (0, 0)) for x in whole],
                scratch_shapes=[pltpu.SemaphoreType.DMA((4,))],
            )
        else:
            out = placed(chunk, orders, blocks, (columns, depth), [out])
    return out, row_out.reshape(row_now.shape), col_out.reshape(columns)


def beside_kernel(x, embeddings, out):
    out[...] = x[...]


def beside(x, embeddings):
    lines = (x.shape[0] // LANES, LANES)
    vmem = pl.BlockSpec(memory_space=pltpu.VMEM)
    return pl.pallas_call(
        beside_kernel,
        out_shape=jax.ShapeDtypeStruct(lines, x.dtype),
        in_specs=[vmem, pl.BlockSpec(memory_space=pl.ANY)],
        out_specs=vmem,
        compiler_params=pltpu.CompilerParams(vmem_limit_bytes=VMEM_BYTES),
    )(x.reshape(lines), embeddings).reshape(x.shape)


def on_device(embeddings, centroids, col_start):
    rows_here = embeddings.shape[0]
    cent_here = centroids.shape[0]
    n_total = rows_here * lax.axis_size("dp")
    k_total = cent_here * lax.axis_size("cent")

    bits = bits_of("dp")
    orders = (bits, [bits[1], bits[0]] + bits[2:])
    place = jnp.full((1,), lax.axis_index("dp"), jnp.int32)
    ups = [place >> bit & 1 for bit in bits]
    ups = [up == 1 for up in ups]
    odd = jnp.full((1,), lax.axis_index("cent"), jnp.int32) & 1 == 1
    ups, odd, embeddings, centroids = lax.optimization_barrier((ups, odd, embeddings, centroids))

    def chosen(bit, yes, no):
        return jnp.where(ups[bit].reshape((1,) * yes.ndim), yes, no)

    def sent_and_kept(value):
        quarters = jnp.split(value, 4)
        lows, highs = quarters[0::2], quarters[1::2]
        sent = [chosen(order[0], low, high) for order, low, high in zip(orders, lows, highs)]
        kept = [chosen(order[0], high, low) for order, low, high in zip(orders, lows, highs)]
        return jnp.concatenate(sent + kept)

    def aligned(value, mask):
        quarters = jnp.split(value, 4)
        for k, order in enumerate(orders):
            if mask >> order[0] & 1:
                quarters[k], quarters[2 + k] = quarters[2 + k], quarters[k]
        return jnp.concatenate(quarters)

    scores = lax.dot_general(
        sent_and_kept(centroids), embeddings, (((1,), (1,)), ((), ())), preferred_element_type=jnp.float32
    ) * (1.0 / math.sqrt(embeddings.shape[1]))
    col_now = sent_and_kept(col_start)
    for step_index in range(ITERS):
        shifted = scores + col_now[:, None]
        top = jnp.max(shifted, axis=0)
        part = top + jnp.log(jnp.sum(jnp.exp(shifted - top[None, :]), axis=0))
        last = step_index == ITERS - 1
        part = lse_over_cent(part, odd)
        row_now = -math.log(n_total) - part
        if last and len(bits) == 2:
            return last_sum(scores, row_now, embeddings, math.log(k_total), orders)
        plan, mass, part = last_terms(scores, row_now)
        if not last:
            near_end = step_index == ITERS - 2
            part = lse_over_dp(part, aligned, lambda x: beside(x, embeddings) if near_end else x)
            col_now = -math.log(k_total) - part
    new_centroids, row_out, whole = last_sum_by_vectors(plan, part, mass, row_now, embeddings, chosen, orders, aligned)
    return new_centroids, row_out, -math.log(k_total) - whole


def solution(mesh):
    specs = (P("dp", None), P("cent", None), P("cent"))
    return jax.shard_map(
        on_device,
        mesh=mesh,
        in_specs=specs,
        out_specs=(P("cent", None), P("dp"), P("cent")),
        check_vma=False,
    )
```

```python
import functools
import math

import jax
import jax.numpy as jnp
from jax import lax
from jax.experimental import pallas as pl
from jax.experimental.pallas import tpu as pltpu
from jax.sharding import PartitionSpec as P

ITERS = 3
CHUNKS = 2
LANES = 128
EXTRA = 16
VMEM_BYTES = 24 * 2**20


def bits_of(axis):
    size = lax.axis_size(axis)
    assert size & (size - 1) == 0
    return list(range(size.bit_length() - 1))


def flipped(x, axis, mask):
    size = lax.axis_size(axis)
    return lax.ppermute(x, axis, [(k, k ^ mask) for k in range(size)])


def lse(first, second):
    top = jnp.maximum(first, second)
    return top + jnp.log(jnp.exp(first - top) + jnp.exp(second - top))


def lse_over_dp(x, aligned, joined_by):
    bits = bits_of("dp")

    def partner(value, mask):
        return aligned(flipped(value, "dp", mask), mask)

    for masks in ([1 << bit for bit in bits[k:k + 2]] for k in range(0, len(bits), 2)):
        if len(masks) == 2:
            far = partner(x, masks[0] | masks[1])
            near = [partner(x, mask) for mask in reversed(masks)]
            x = lse(joined_by(lax.optimization_barrier(lse(x, far))), lse(*near))
        else:
            x = lse(x, partner(x, masks[0]))
    return x


def lse_over_cent(x, odd):
    size = lax.axis_size("cent")
    near, middle, *rest = [1 << bit for bit in bits_of("cent")[1:]]

    def split(value, even_mask, odd_mask):
        return lax.ppermute(value, "cent", [(k, k ^ (odd_mask if k % 2 else even_mask)) for k in range(size)])

    x = lse(x, flipped(x, "cent", 1))
    second = split(x, near, middle)
    first = split(x, near, near | middle)
    x = jnp.where(odd, lse(second, first), lse(x, first))
    for mask in [1] + rest:
        x = lse(x, flipped(x, "cent", mask))
    return x


def column(values):
    lane = lax.broadcasted_iota(jnp.int32, (LANES, LANES), 1)
    diagonal = lane == lax.broadcasted_iota(jnp.int32, (LANES, LANES), 0)
    return jnp.sum(jnp.where(diagonal, values, 0.0), axis=1, keepdims=True)


def quarter_places(orders, quarter):
    ups = [lax.axis_index("dp") >> order[0] & 1 for order in orders]
    sent = [(2 * k + 1 - up) * quarter for k, up in enumerate(ups)]
    return sent + [(2 * k + up) * quarter for k, up in enumerate(ups)]


def place_kernel(chunk, orders, *refs):
    blocks, (out, sent) = refs[:4], refs[-2:]
    quarter, width = blocks[0].shape
    copies = []
    for k, start in enumerate(quarter_places(orders, quarter)):
        rows = pl.ds(pl.multiple_of(start, LANES), quarter)
        copies.append(pltpu.make_async_copy(blocks[k], out.at[rows, pl.ds(chunk * width, width)], sent.at[k]))
        copies[-1].start()
    for copy in copies:
        copy.wait()


def placed(chunk, orders, blocks, shape, so_far):
    vmem = pl.BlockSpec(memory_space=pltpu.VMEM)
    anywhere = pl.BlockSpec(memory_space=pl.ANY)
    return pl.pallas_call(
        functools.partial(place_kernel, chunk, orders),
        out_shape=jax.ShapeDtypeStruct(shape, blocks[0].dtype),
        in_specs=[vmem] * 4 + [anywhere] * len(so_far),
        out_specs=anywhere,
        scratch_shapes=[pltpu.SemaphoreType.DMA((4,))],
        input_output_aliases={4: 0} if so_far else {},
        compiler_params=pltpu.CompilerParams(vmem_limit_bytes=VMEM_BYTES),
    )(*blocks, *so_far)


def means_kernel(is_kept, plan, embeddings, mass, *rest):
    half = plan.shape[0] // 2
    quarter = half // 2
    sums = jnp.dot(plan[pl.ds(is_kept * half, half), :], embeddings[...], preferred_element_type=jnp.float32)
    if is_kept:
        weights, row, out, row_out = rest
        row_out[...] = row[...]
    else:
        out = None
    for block in range(half // LANES):
        factor = 1.0 / column(mass[pl.ds(is_kept * (half // LANES) + block, 1), :])
        if is_kept:
            factor = factor * column(weights[pl.ds(block, 1), :])
        rows = pl.ds(block * LANES % quarter, LANES)
        values = sums[block * LANES:(block + 1) * LANES] * factor
        half_index = block * LANES // quarter
        if is_kept:
            out[half_index, rows, :] = values
        else:
            width = rest[0].shape[1]
            for chunk in range(CHUNKS):
                target = rest[2 * chunk + half_index]
                target[rows, :] = values[:, chunk * width:(chunk + 1) * width].astype(target.dtype)


def means_of(is_kept, plan, embeddings, mass, *rest):
    count, rows_here = plan.shape
    depth = embeddings.shape[1]
    vmem = pl.BlockSpec(memory_space=pltpu.VMEM)
    if is_kept:
        out_shape = (
            jax.ShapeDtypeStruct((2, count // 4, depth), jnp.float32),
            jax.ShapeDtypeStruct((1, rows_here), jnp.float32),
        )
        out_specs = (vmem, pl.BlockSpec((1, rows_here), lambda: (0, 0)))
    else:
        out_shape = [jax.ShapeDtypeStruct((count // 4, depth // CHUNKS), jnp.bfloat16)] * (2 * CHUNKS)
        out_specs = [vmem] * (2 * CHUNKS)
    return pl.pallas_call(
        functools.partial(means_kernel, is_kept),
        out_shape=out_shape,
        in_specs=[vmem] * (3 + len(rest)),
        out_specs=out_specs,
        compiler_params=pltpu.CompilerParams(vmem_limit_bytes=VMEM_BYTES),
        cost_estimate=pl.CostEstimate(
            flops=count * rows_here * depth, bytes_accessed=2 * rows_here * depth, transcendentals=0
        ),
    )(plan, embeddings, mass.reshape(count // LANES, LANES), *rest)


def last_sum_by_vectors(plan, part, mass, row_now, embeddings, chosen, orders, aligned):
    quarter = part.shape[0] // 4
    first, second = orders[0][:2]
    partners = {bit: aligned(flipped(part, "dp", 1 << bit), 1 << bit) for bit in (first, second)}
    sent = means_of(0, plan, embeddings, mass)
    got = [flipped(sent[2 * chunk + k], "dp", 1 << order[0]) for chunk in range(CHUNKS) for k, order in enumerate(orders)]

    def kept_of(lower, upper):
        return jnp.concatenate([lower[2 * quarter:3 * quarter], upper[3 * quarter:]])

    pairs = lax.optimization_barrier([lse(partners[first], part), lse(partners[second], part)])
    pair = kept_of(*pairs)
    weights = jnp.exp(kept_of(part, part) - pair).reshape(2 * quarter // LANES, LANES)
    kept, row_out = means_of(1, plan, embeddings, mass, weights, row_now[None, :])
    weights = jnp.exp(kept_of(partners[first], partners[second]) - pair)

    corner = flipped(partners[first], "dp", 1 << second)

    def exchanged(mine, bit, own, other):
        mine = mine.astype(jnp.bfloat16)
        theirs = flipped(mine, "dp", 1 << bit).astype(jnp.float32)
        mine = mine.astype(jnp.float32)
        lower = chosen(bit, theirs, mine) * chosen(bit, other, own)
        upper = chosen(bit, mine, theirs) * chosen(bit, own, other)
        return (lower + upper).astype(jnp.bfloat16)

    def gathered(mine, order, own, other):
        if len(order) == 1:
            return exchanged(mine, order[0], own, other)
        bit = order[0]
        low, high = jnp.split(mine, 2, axis=0)
        got = flipped(chosen(bit, low, high).astype(jnp.bfloat16), "dp", 1 << bit).astype(jnp.float32)
        own, other = (chosen(bit, high, low) for low, high in (jnp.split(x, 2, axis=0) for x in (own, other)))
        ones = jnp.ones((own.shape[0], 1), jnp.float32)
        done = gathered(chosen(bit, high, low) * own + got * other, order[1:], ones, ones)
        theirs = flipped(done, "dp", 1 << bit)
        return jnp.concatenate([chosen(bit, theirs, done), chosen(bit, done, theirs)], axis=0)

    width = kept.shape[2] // CHUNKS
    shape = (part.shape[0], kept.shape[2])
    mines = []
    for chunk in range(CHUNKS):
        columns = slice(chunk * width, (chunk + 1) * width)
        if chunk > 0:
            mines, kept, weights = lax.optimization_barrier((mines, kept, weights))
        for k in range(2):
            rows = slice(k * quarter, (k + 1) * quarter)
            mines.append(kept[k, :, columns] + got[2 * chunk + k].astype(jnp.float32) * weights[rows, None])

    pairs, partners, corner = lax.optimization_barrier((pairs, partners, corner, mines))[:3]
    corner = aligned(corner, 1 << second)
    whole = lse(pairs[0], lse(corner, partners[second]))
    for bit in orders[0][2:]:
        whole = lse(aligned(flipped(whole, "dp", 1 << bit), 1 << bit), whole)
    pair_other = kept_of(lse(partners[second], corner), lse(partners[first], corner))
    weights_own = jnp.exp(kept_of(*pairs) - kept_of(whole, whole))
    weights_other = jnp.exp(pair_other - kept_of(whole, whole))

    outs = []
    firsts = []
    for chunk in range(CHUNKS):
        dones = []
        for k, order in enumerate(orders):
            rows = slice(k * quarter, (k + 1) * quarter)
            dones.append(gathered(mines[2 * chunk + k], order[1:], weights_own[rows, None], weights_other[rows, None]))
        if chunk < CHUNKS - 1:
            dones, weights_own, weights_other = lax.optimization_barrier((dones, weights_own, weights_other))
        firsts = firsts or dones
        blocks = [flipped(done, "dp", 1 << order[0]) for done, order in zip(dones, orders)] + dones
        outs = [placed(chunk, orders, blocks, shape, outs)]
    whole = lax.optimization_barrier((whole, firsts[0]))[0]
    quarters = jnp.split(whole, 4)
    halves = []
    for k, order in enumerate(orders):
        sent, kept = quarters[k], quarters[2 + k]
        halves += [chosen(order[0], sent, kept), chosen(order[0], kept, sent)]
    return outs[0], row_out.reshape(row_now.shape), jnp.concatenate(halves)


def parts_of(lines):
    row = lax.broadcasted_iota(jnp.int32, (EXTRA, LANES), 0)
    rows = jnp.zeros((EXTRA, LANES), jnp.float32)
    for index, line in enumerate(lines):
        for part in range(3):
            rounded = line.astype(jnp.bfloat16).astype(jnp.float32)
            rows = jnp.where(row == 3 * index + part, rounded, rows)
            line = line - rounded
    return rows.astype(jnp.bfloat16)


def lines_of(message, count):
    rows = message[pl.ds(message.shape[0] - EXTRA, EXTRA), pl.ds(0, LANES)].astype(jnp.float32)
    return [(rows[k:k + 1] + rows[k + 1:k + 2]) + rows[k + 2:k + 3] for k in range(0, 3 * count, 3)]


def put(message, values, lines):
    quarter, width = values.shape
    message[pl.ds(0, quarter), :] = values.astype(message.dtype)
    if lines:
        message[pl.ds(quarter, EXTRA), pl.ds(0, LANES)] = parts_of(lines)
        message[pl.ds(quarter, EXTRA), pl.ds(LANES, width - LANES)] = jnp.zeros((EXTRA, width - LANES), message.dtype)


def columns_of(lines):
    return jnp.concatenate([column(line) for line in lines], axis=0)


def read(ref, start, count):
    return [ref[pl.ds(start + k, 1), :] for k in range(count)]


def write(ref, start, lines):
    for k, line in enumerate(lines):
        ref[pl.ds(start + k, 1), :] = line


def joined(first, second):
    whole = [lse(a, b) for a, b in zip(first, second)]
    return whole, [jnp.exp(a - b) for a, b in zip(first, whole)], [jnp.exp(a - b) for a, b in zip(second, whole)]


def sent_kernel(chunk, plan, embeddings, mass, part, *sent):
    quarter = plan.shape[0] // 2
    count = quarter // LANES
    width = embeddings.shape[1] // CHUNKS
    columns = embeddings[:, pl.ds(chunk * width, width)]
    sums = jnp.dot(plan[...], columns, preferred_element_type=jnp.float32)
    for k in range(2):
        values = sums[k * quarter:(k + 1) * quarter] / columns_of(read(mass, k * count, count))
        put(sent[k], values, read(part, k * count, count) if chunk == 0 else [])


def kept_kernel(plan, embeddings, mass, kept):
    quarter = plan.shape[0] // 2
    count = quarter // LANES
    sums = jnp.dot(plan[...], embeddings[...], preferred_element_type=jnp.float32)
    for k in range(2):
        kept[k] = sums[k * quarter:(k + 1) * quarter] / columns_of(read(mass, k * count, count))


def pair_kernel(chunk, kept, lower, upper, known, out_lower, out_upper, *weights_out):
    quarter = kept.shape[1]
    count = quarter // LANES
    for k, (got, out) in enumerate(((lower, out_lower), (upper, out_upper))):
        if chunk == 0:
            pair, own, other = joined(read(known, k * count, count), lines_of(got, count))
            write(weights_out[0], 2 * k * count, own + other)
        else:
            pair = []
            own, other = read(known, 2 * k * count, count), read(known, (2 * k + 1) * count, count)
        width = got.shape[1]
        values = kept[k, :, pl.ds(chunk * width, width)] * columns_of(own)
        put(out, values + got[pl.ds(0, quarter), :].astype(jnp.float32) * columns_of(other), pair)


def whole_kernel(chunk, bit, quarter, mine, theirs, *rest):
    count = quarter // LANES
    up = lax.axis_index("dp") >> bit & 1 == 1
    if chunk == 0:
        out, weights_out = rest
        own, other = lines_of(mine, count), lines_of(theirs, count)
        lower = [jnp.where(up, b, a) for a, b in zip(own, other)]
        upper = [jnp.where(up, a, b) for a, b in zip(own, other)]
        whole, low, high = joined(lower, upper)
        write(weights_out, 0, low + high)
    else:
        known, out = rest
        whole = []
        low, high = read(known, 0, count), read(known, count, count)
    own, other = (ref[pl.ds(0, quarter), :].astype(jnp.float32) for ref in (mine, theirs))
    values = jnp.where(up, other, own) * columns_of(low) + jnp.where(up, own, other) * columns_of(high)
    put(out, values, whole)


def place_first_kernel(orders, log_k, lower_sent, upper_sent, lower_kept, upper_kept, row, out, col_out, row_out, sent):
    blocks = (lower_sent, upper_sent, lower_kept, upper_kept)
    quarter = blocks[0].shape[0] - EXTRA
    count = quarter // LANES
    copies = []
    for k, start in enumerate(quarter_places(orders, quarter)):
        rows = pl.ds(pl.multiple_of(start, LANES), quarter)
        source = blocks[k].at[pl.ds(0, quarter)]
        copies.append(pltpu.make_async_copy(source, out.at[rows, pl.ds(0, blocks[k].shape[1])], sent.at[k]))
        copies[-1].start()
    row_out[...] = row[...]
    for block, start in zip(blocks, quarter_places(orders, count)):
        write(col_out, start, [-log_k - line for line in lines_of(block, count)])
    for copy in copies:
        copy.wait()


def last_terms(scores, row):
    lifted = scores + row[None, :]
    top = jnp.max(lifted, axis=1)
    terms = jnp.exp(lifted - top[:, None])
    mass = jnp.sum(terms, axis=1)
    return terms.astype(jnp.bfloat16), mass, top + jnp.log(mass)


def last_sum(scores, row_now, embeddings, log_k, orders):
    columns, rows_here = scores.shape
    depth = embeddings.shape[1]
    quarter = columns // 4
    width = depth // CHUNKS
    lines = quarter // LANES
    f32 = jnp.float32
    vmem = pl.BlockSpec(memory_space=pltpu.VMEM)

    def call(kernel, operands, outs, specs=None, flops=0, **options):
        return pl.pallas_call(
            kernel,
            out_shape=outs,
            in_specs=[vmem] * len(operands),
            out_specs=specs or [vmem] * len(outs),
            compiler_params=pltpu.CompilerParams(vmem_limit_bytes=VMEM_BYTES),
            cost_estimate=pl.CostEstimate(flops=flops, bytes_accessed=columns * depth, transcendentals=0),
            **options,
        )(*operands)

    def message(chunk):
        return jax.ShapeDtypeStruct((quarter + (EXTRA if chunk == 0 else 0), width), jnp.bfloat16)

    def table(count):
        return jax.ShapeDtypeStruct((count * lines, LANES), f32)

    flops = columns * rows_here * depth
    chunks = range(CHUNKS)
    plan, mass, part = last_terms(scores[:2 * quarter], row_now)
    operands = [plan, embeddings, mass.reshape(table(2).shape), part.reshape(table(2).shape)]
    sent = []
    for chunk in chunks:
        sent += call(functools.partial(sent_kernel, chunk), operands, [message(chunk)] * 2, flops=flops // CHUNKS)
    got = [flipped(sent[2 * chunk + k], "dp", 1 << orders[k][0]) for chunk in chunks for k in range(2)]
    row_now = lax.optimization_barrier((row_now, sent[:2]))[0]
    plan, mass, part = last_terms(scores[2 * quarter:], row_now)
    row = row_now[None, :]
    kept, = call(
        kept_kernel,
        [plan, embeddings, mass.reshape(table(2).shape)],
        [jax.ShapeDtypeStruct((2, quarter, depth), f32)],
        flops=flops,
    )
    pairs = []
    known = part.reshape(table(2).shape)
    for chunk in chunks:
        outs = [message(chunk)] * 2 + ([table(4)] if chunk == 0 else [])
        results = call(functools.partial(pair_kernel, chunk), [kept, got[2 * chunk], got[2 * chunk + 1], known], outs)
        both = results[:2]
        known = results[2] if chunk == 0 else known
        pairs += both
    known = [None, None]
    out = None
    for chunk in chunks:
        dones = []
        for k, order in enumerate(orders):
            mine = pairs[2 * chunk + k]
            theirs = flipped(mine, "dp", 1 << order[1])
            kernel = functools.partial(whole_kernel, chunk, order[1], quarter)
            if chunk == 0:
                done, known[k] = call(kernel, [mine, theirs], [message(chunk), table(2)])
            else:
                done, = call(kernel, [mine, theirs, known[k]], [message(chunk)])
            dones.append(done)
        blocks = [flipped(done, "dp", 1 << order[0]) for done, order in zip(dones, orders)] + dones
        if chunk == 0:
            whole = [table(4), jax.ShapeDtypeStruct(row.shape, f32)]
            out, col_out, row_out = call(
                functools.partial(place_first_kernel, orders, log_k),
                blocks + [row],
                [jax.ShapeDtypeStruct((columns, depth), jnp.bfloat16)] + whole,
                specs=[pl.BlockSpec(memory_space=pl.ANY)] + [pl.BlockSpec(x.shape, lambda: (0, 0)) for x in whole],
                scratch_shapes=[pltpu.SemaphoreType.DMA((4,))],
            )
        else:
            out = placed(chunk, orders, blocks, (columns, depth), [out])
    return out, row_out.reshape(row_now.shape), col_out.reshape(columns)


def beside_kernel(x, embeddings, out):
    out[...] = x[...]


def beside(x, embeddings):
    lines = (x.shape[0] // LANES, LANES)
    vmem = pl.BlockSpec(memory_space=pltpu.VMEM)
    return pl.pallas_call(
        beside_kernel,
        out_shape=jax.ShapeDtypeStruct(lines, x.dtype),
        in_specs=[vmem, pl.BlockSpec(memory_space=pl.ANY)],
        out_specs=vmem,
        compiler_params=pltpu.CompilerParams(vmem_limit_bytes=VMEM_BYTES),
    )(x.reshape(lines), embeddings).reshape(x.shape)


def on_device(embeddings, centroids, col_start):
    rows_here = embeddings.shape[0]
    cent_here = centroids.shape[0]
    n_total = rows_here * lax.axis_size("dp")
    k_total = cent_here * lax.axis_size("cent")

    bits = bits_of("dp")
    orders = ([bits[1], bits[0]] + bits[2:], bits)
    place = jnp.full((1,), lax.axis_index("dp"), jnp.int32)
    ups = [place >> bit & 1 for bit in bits]
    ups = [up == 1 for up in ups]
    odd = jnp.full((1,), lax.axis_index("cent"), jnp.int32) & 1 == 1
    ups, odd, embeddings, centroids = lax.optimization_barrier((ups, odd, embeddings, centroids))

    def chosen(bit, yes, no):
        return jnp.where(ups[bit].reshape((1,) * yes.ndim), yes, no)

    def sent_and_kept(value):
        quarters = jnp.split(value, 4)
        lows, highs = quarters[0::2], quarters[1::2]
        sent = [chosen(order[0], low, high) for order, low, high in zip(orders, lows, highs)]
        kept = [chosen(order[0], high, low) for order, low, high in zip(orders, lows, highs)]
        return jnp.concatenate(sent + kept)

    def aligned(value, mask):
        quarters = jnp.split(value, 4)
        for k, order in enumerate(orders):
            if mask >> order[0] & 1:
                quarters[k], quarters[2 + k] = quarters[2 + k], quarters[k]
        return jnp.concatenate(quarters)

    scores = lax.dot_general(
        sent_and_kept(centroids), embeddings, (((1,), (1,)), ((), ())), preferred_element_type=jnp.float32
    ) * (1.0 / math.sqrt(embeddings.shape[1]))
    col_now = sent_and_kept(col_start)
    for step_index in range(ITERS):
        shifted = scores + col_now[:, None]
        top = jnp.max(shifted, axis=0)
        part = top + jnp.log(jnp.sum(jnp.exp(shifted - top[None, :]), axis=0))
        last = step_index == ITERS - 1
        part = lse_over_cent(part, odd)
        row_now = -math.log(n_total) - part
        if last and len(bits) == 2:
            return last_sum(scores, row_now, embeddings, math.log(k_total), orders)
        plan, mass, part = last_terms(scores, row_now)
        if not last:
            near_end = step_index == ITERS - 2
            part = lse_over_dp(part, aligned, lambda x: beside(x, embeddings) if near_end else x)
            col_now = -math.log(k_total) - part
    new_centroids, row_out, whole = last_sum_by_vectors(plan, part, mass, row_now, embeddings, chosen, orders, aligned)
    return new_centroids, row_out, -math.log(k_total) - whole


def solution(mesh):
    specs = (P("dp", None), P("cent", None), P("cent"))
    return jax.shard_map(
        on_device,
        mesh=mesh,
        in_specs=specs,
        out_specs=(P("cent", None), P("dp"), P("cent")),
        check_vma=False,
    )
```
